128 devices in a mesh: samp: 16 (over x, y), cent: 8 (over z, core).
Axes of the slice: x: 4, y: 4, z: 4, core: 2. Of those that a mesh axis runs over, the one named last changes fastest.
Arguments:
- embeddings: float32 [65536, 1024], P(('samp', 'cent')), may hold values from -40 to 40
- assignment: int32 [65536], P(('samp', 'cent')), may hold values from 0 to 8191, as said below
- owner_map: int32 [8192], replicated, may hold values from 0 to 127, as said below
Outputs:
- centroid: float32 [8192, 1024], P(('samp', 'cent'))
- representative: float32 [8192, 1024], P(('samp', 'cent'))
- keep_weight: float32 [65536], P(('samp', 'cent'))
The draws below stay inside these ranges and needn't reach their ends.
Inputs may be any that keep to these rules, and one draw needn't show every extreme that they name: `owner_map`: every device index, samp-major, owns exactly 64 clusters. `assignment`: of the 512 rows of one device, at most 16 lie in clusters owned by any one device; in every draw some device owns clusters that hold exactly 16 rows of every device.
All inputs are finite; a program needn't handle non-finite values.
Results may differ from the reference program's by a relative error of at most 0.0034.
Values may be sent and summed in bfloat16 or wider, within the bound.
No kernel may reach another device: no remote copies, remote signals or barrier semaphores. Data moves between devices by JAX's collectives and lax.ppermute only.
A program may use at most 64 MiB of HBM per device.

```python
import jax
import jax.numpy as jnp
from jax import lax

D = 1024
ROW_DEV = 512
K_DEV = 64
ROWS = 65536
K = 8192
CAP = 16


def shared_layout(key):
    device_count = ROWS // ROW_DEV
    cluster_perm = jax.random.permutation(jax.random.fold_in(key, 11), K)
    owner_values = (cluster_perm // K_DEV).astype(jnp.int32)
    inverse_perm = jnp.argsort(cluster_perm, stable=True).astype(jnp.int32)
    hottest = jax.random.randint(jax.random.fold_in(key, 12), (), 0, device_count)
    block_keys = jax.random.split(jax.random.fold_in(key, 13), device_count)

    def one_block(block_key):
        first_key, second_key, third_key, fourth_key = jax.random.split(block_key, 4)
        other_slots = jax.random.permutation(first_key, (device_count - 1) * CAP)[:ROW_DEV - CAP] // CAP
        other_slots = other_slots + (other_slots >= hottest).astype(jnp.int32)
        targets = jnp.concatenate([jnp.full((CAP,), hottest, jnp.int32), other_slots.astype(jnp.int32)])
        targets = jax.random.permutation(second_key, targets)
        local_rank = jnp.minimum(jax.random.randint(third_key, (ROW_DEV,), 0, K_DEV), jax.random.randint(fourth_key, (ROW_DEV,), 0, K_DEV))
        return inverse_perm[targets * K_DEV + local_rank]
    chosen = jax.vmap(one_block)(block_keys).reshape(ROWS).astype(jnp.int32)
    return (owner_values, chosen)


def draw_owner_map(key, part):
    return shared_layout(key)[0]


def draw_assignment(key, part):
    return shared_layout(key)[1]


def draw_embeddings(key, part):
    chosen = shared_layout(key)[1]
    table = jax.random.normal(jax.random.fold_in(key, 21), (K, D), jnp.float32)
    strength = jax.random.uniform(jax.random.fold_in(key, 22), (ROWS, 1), jnp.float32, 0.3, 3.0)
    noise = jax.random.normal(jax.random.fold_in(key, 23), (ROWS, D), jnp.float32)
    values = strength * table[chosen] + noise
    return jnp.clip(values, -40.0, 40.0)


def setup_inputs(seed: int = 0) -> dict:
    streams_of = jax.random.split(jax.random.key(seed), 4)
    embeddings = draw_embeddings(jax.random.fold_in(streams_of[3], 71), 0)
    assignment = draw_assignment(jax.random.fold_in(streams_of[3], 71), 0)
    owner_map = draw_owner_map(jax.random.fold_in(streams_of[3], 71), 0)
    return {"embeddings": embeddings, "assignment": assignment, "owner_map": owner_map}


EPSILON = 1e-06
SHARPNESS = 8.0

def reference(embeddings, assignment, owner_map):
    unit_rows = (embeddings * lax.rsqrt(lax.optimization_barrier(jnp.sum(embeddings * embeddings, axis=1, keepdims=True)) + EPSILON)).astype(jnp.bfloat16)
    unit_wide = lax.optimization_barrier(unit_rows).astype(jnp.float32)
    cluster_sums = jax.ops.segment_sum(unit_wide, assignment, num_segments=K)
    sum_squares = lax.optimization_barrier(jnp.sum(cluster_sums * cluster_sums, axis=1))
    row_order = jnp.argsort(assignment, stable=True).astype(jnp.int32)
    sorted_units = unit_rows[row_order]
    sorted_ids = assignment[row_order]
    member_counts = jax.ops.segment_sum(jnp.ones((ROWS,), jnp.int32), assignment, num_segments=K).astype(jnp.int32)
    seg_starts = jnp.concatenate([jnp.zeros((1,), jnp.int32), jnp.cumsum(member_counts).astype(jnp.int32)])
    block_size = 128

    def score_block(block_index):
        block_rows = lax.dynamic_slice_in_dim(sorted_units, block_index * block_size, block_size)
        block_ids = lax.dynamic_slice_in_dim(sorted_ids, block_index * block_size, block_size)
        lower_bound = seg_starts[block_ids[0]]
        upper_bound = seg_starts[block_ids[block_size - 1] + 1]
        first_col = (lower_bound // block_size).astype(jnp.int32)
        last_col = ((upper_bound + block_size - 1) // block_size).astype(jnp.int32)

        def column_step(column_index, totals):
            columns = lax.dynamic_slice_in_dim(sorted_units, column_index * block_size, block_size)
            column_ids = lax.dynamic_slice_in_dim(sorted_ids, column_index * block_size, block_size)
            gram = jnp.dot(block_rows, columns.T, preferred_element_type=jnp.float32)
            same_cluster = block_ids[:, None] == column_ids[None, :]
            similar = totals[0] + lax.optimization_barrier(jnp.sum(jnp.where(same_cluster, gram, 0.0), axis=1))
            density = totals[1] + lax.optimization_barrier(jnp.sum(jnp.where(same_cluster, jnp.exp(SHARPNESS * (gram - 1.0)), 0.0), axis=1))
            return (similar, density)
        empty = jnp.zeros((block_size,), jnp.float32)
        return lax.fori_loop(first_col, last_col, column_step, (empty, empty))
    similar, density = lax.map(score_block, jnp.arange(ROWS // block_size, dtype=jnp.int32))
    similar = similar.reshape(ROWS)
    density = density.reshape(ROWS)
    inverse_norm = lax.rsqrt(sum_squares + EPSILON)[sorted_ids]
    spread = 1.0 - similar * inverse_norm
    sorted_weight = jnp.exp(spread) / density
    keep_weight = jnp.zeros((ROWS,), jnp.float32).at[row_order].set(sorted_weight)
    rounded_weight = lax.optimization_barrier(sorted_weight.astype(jnp.bfloat16)).astype(jnp.float32)
    weighted_sums = jax.ops.segment_sum(rounded_weight[:, None] * sorted_units.astype(jnp.float32), sorted_ids, num_segments=K)
    centroid = cluster_sums * lax.rsqrt(sum_squares + EPSILON)[:, None]
    representative = weighted_sums * lax.rsqrt(lax.optimization_barrier(jnp.sum(weighted_sums * weighted_sums, axis=1, keepdims=True)) + EPSILON)
    cluster_order = jnp.argsort(owner_map, stable=True).astype(jnp.int32)
    return (centroid[cluster_order], representative[cluster_order], keep_weight)
```

```python
import functools

import jax
import jax.numpy as jnp
from jax import lax
from jax.experimental import pallas as pl
from jax.experimental.pallas import tpu as pltpu
from jax.sharding import PartitionSpec as P

EPSILON = 1e-06
SHARPNESS = 8.0
LANES = 128
AXES = ("samp", "cent")


def iota(shape, dim):
    return lax.broadcasted_iota(jnp.int32, shape, dim)


def dot_nt(a, b):
    return lax.dot_general(a, b, (((1,), (1,)), ((), ())), preferred_element_type=jnp.float32)


def dot_tn(a, b):
    return lax.dot_general(a, b, (((0,), (0,)), ((), ())), preferred_element_type=jnp.float32)


def as_bf(mask):
    return jnp.where(mask, 1.0, 0.0).astype(jnp.bfloat16)


def dispatch_kernel(emb_ref, a_ref, owner_ref, out_ref, slot_ref, unit_ref, rank_ref):
    step = pl.program_id(0)
    rows = emb_ref.shape[0]
    blocks = owner_ref.shape[0]

    @pl.when(step == 0)
    def _():
        x = emb_ref[...]
        scale = lax.rsqrt(jnp.sum(x * x, axis=1, keepdims=True) + EPSILON)
        unit_ref[...] = (x * scale).astype(jnp.bfloat16)

        a = a_ref[...]
        hi = a >> 7
        lo = a & 127
        hi_onehot = as_bf(iota((blocks, rows), 0) == hi)
        owner = owner_ref[...]
        owners = dot_tn(owner.astype(jnp.float32).astype(jnp.bfloat16), hi_onehot)
        lane = iota((LANES, rows), 0)
        dest = jnp.sum(jnp.where(lane == lo, owners, 0.0), axis=0, keepdims=True)
        before = jnp.where(owners == dest, 1.0, 0.0)
        inside = jnp.sum(jnp.where(lane < lo, before, 0.0), axis=0, keepdims=True)

        counts = jnp.zeros((LANES, blocks), jnp.float32)
        device = iota((LANES, LANES), 0)
        column = iota((LANES, blocks), 1)
        for b in range(blocks):
            match = jnp.where(owner[b : b + 1, :] == device, 1.0, 0.0)
            total = jnp.sum(match, axis=1, keepdims=True)
            counts = counts + jnp.where(column == b, total, 0.0)
        earlier = as_bf(iota((blocks, rows), 0) < hi)
        prior = jnp.dot(
            counts.astype(jnp.bfloat16), earlier, preferred_element_type=jnp.float32
        )
        dest_int = dest.astype(jnp.int32)
        here = lane == dest_int
        rank = inside + jnp.sum(jnp.where(here, prior, 0.0), axis=0, keepdims=True)
        rank_ref[...] = rank.astype(jnp.int32)

        upper = as_bf(iota((rows, rows), 0) < iota((rows, rows), 1))
        running = jnp.dot(as_bf(here), upper, preferred_element_type=jnp.float32)
        within = jnp.sum(jnp.where(here, running, 0.0), axis=0, keepdims=True)
        slot_ref[...] = dest_int * 16 + within.astype(jnp.int32)

    i = iota((256, rows), 0)
    wanted = step * 256 + ((i & 127) >> 3) * 16 + (i & 7) + (i >> 7) * 8
    pick = as_bf(slot_ref[...] == wanted)
    moved = jnp.dot(pick, unit_ref[...], preferred_element_type=jnp.float32)
    for half in range(2):
        for j in range(8):
            piece = moved[half * 128 : half * 128 + 128, j * LANES : (j + 1) * LANES]
            out_ref[:, half * 8 + j, :, :] = piece.reshape(16, 8, LANES).astype(jnp.bfloat16)
    rank = rank_ref[...]
    tag = iota((LANES, rows), 0)
    tags = dot_nt(pick[:128], as_bf(tag == rank)) + dot_nt(pick[128:], as_bf(tag == rank + 64))
    out_ref[:, 16, :, :] = tags.reshape(16, 8, LANES).astype(jnp.bfloat16)


def dispatch(embeddings, a_row, owner):
    rows, width = embeddings.shape
    devices = 128
    return pl.pallas_call(
        dispatch_kernel,
        grid=(8,),
        out_shape=(
            jax.ShapeDtypeStruct((devices, 17, 8, LANES), jnp.bfloat16),
            jax.ShapeDtypeStruct((1, rows), jnp.int32),
        ),
        in_specs=[
            pl.BlockSpec((rows, width), lambda i: (0, 0)),
            pl.BlockSpec((1, rows), lambda i: (0, 0)),
            pl.BlockSpec(owner.shape, lambda i: (0, 0)),
        ],
        out_specs=(
            pl.BlockSpec((16, 17, 8, LANES), lambda i: (i, 0, 0, 0)),
            pl.BlockSpec((1, rows), lambda i: (0, 0)),
        ),
        scratch_shapes=[
            pltpu.VMEM((rows, width), jnp.bfloat16),
            pltpu.VMEM((1, rows), jnp.int32),
        ],
        compiler_params=pltpu.CompilerParams(vmem_limit_bytes=40 * 1024 * 1024),
        name="dispatch",
    )(embeddings, a_row, owner)


def process_kernel(in_ref, cent_ref, rep_ref, weight_ref, x_ref, row_ref, col_ref):
    half = 1024
    slots = 2 * half
    width = 1024
    block = 256
    labels = in_ref[:, 16, :, :].reshape(half, LANES)
    lane = iota((LANES, LANES), 1)
    source = iota((LANES, LANES), 0)
    for h in range(2):
        for j in range(8):
            x_ref[h * half : (h + 1) * half, j * LANES : (j + 1) * LANES] = in_ref[
                :, h * 8 + j, :, :
            ].reshape(half, LANES)
        take = as_bf((source == lane + h * 64) & (lane < 64))
        x_ref[h * half : (h + 1) * half, width:] = (
            4.0 * jnp.dot(labels, take, preferred_element_type=jnp.float32)
        ).astype(jnp.bfloat16)

    member4 = x_ref[:, width:]
    sums = dot_tn(member4, x_ref[:, :width]) * 0.25
    inverse = lax.rsqrt(jnp.sum(sums * sums, axis=1, keepdims=True) + EPSILON)
    centroid = sums * inverse
    cent_ref[...] = centroid[:64]
    coarse = centroid.astype(jnp.bfloat16)
    fine = (centroid - coarse.astype(jnp.float32)).astype(jnp.bfloat16)

    row_ref[...] = jnp.zeros_like(row_ref)
    col_ref[...] = jnp.zeros_like(col_ref)
    count = slots // block
    for i in range(count):
        left = x_ref[i * block : (i + 1) * block, :]
        for j in range(i, count):
            gram = dot_nt(left, x_ref[j * block : (j + 1) * block, :])
            kernel = jnp.exp(SHARPNESS * gram - 17.0 * SHARPNESS)
            row_ref[i * block : (i + 1) * block, :] += kernel[:, :LANES] + kernel[:, LANES:]
            if j > i:
                col_ref[:, j * block : (j + 1) * block] += jnp.sum(
                    kernel.reshape(block // 8, 8, block), axis=0
                )

    eye = iota((LANES, LANES), 0) == iota((LANES, LANES), 1)
    totals = jnp.zeros((LANES, LANES), jnp.float32)
    weighted = jnp.zeros((LANES, width), jnp.float32)
    device = iota((LANES, 8, LANES), 2)
    place = iota((LANES, 8, LANES), 1)
    for h in range(2):
        rows = slice(h * half, (h + 1) * half)
        x = x_ref[rows, :width]
        scores = dot_nt(x, jnp.concatenate([coarse, fine], axis=0))
        member = x_ref[rows, width:].astype(jnp.float32) * 0.25
        near = jnp.sum((scores[:, :LANES] + scores[:, LANES:]) * member, axis=1, keepdims=True)
        valid = jnp.sum(member, axis=1, keepdims=True) > 0.5
        density = jnp.sum(row_ref[rows, :], axis=1, keepdims=True)
        across = []
        for k in range(half // LANES):
            start = h * half + k * LANES
            line = jnp.sum(col_ref[:, start : start + LANES], axis=0, keepdims=True)
            across.append(jnp.sum(jnp.where(eye, line, 0.0), axis=1, keepdims=True))
        density = density + jnp.concatenate(across, axis=0)
        weight = jnp.where(valid, jnp.exp(1.0 - near) / jnp.where(valid, density, 1.0), 0.0)
        rounded = weight.astype(jnp.bfloat16).astype(jnp.float32)
        weighted = weighted + dot_tn((member * rounded).astype(jnp.bfloat16), x)
        wide = jnp.broadcast_to(weight, (half, LANES)).reshape(LANES, 8, LANES)
        totals = totals + jnp.sum(jnp.where(device == place + h * 8, wide, 0.0), axis=1)
    weight_ref[...] = totals
    rep = weighted * lax.rsqrt(jnp.sum(weighted * weighted, axis=1, keepdims=True) + EPSILON)
    rep_ref[...] = rep[:64]


def process(arrived):
    devices = arrived.shape[0]
    return pl.pallas_call(
        process_kernel,
        out_shape=(
            jax.ShapeDtypeStruct((64, 1024), jnp.float32),
            jax.ShapeDtypeStruct((64, 1024), jnp.float32),
            jax.ShapeDtypeStruct((devices, LANES), jnp.float32),
        ),
        in_specs=[pl.BlockSpec(memory_space=pltpu.VMEM)],
        out_specs=(pl.BlockSpec(memory_space=pltpu.VMEM),) * 3,
        scratch_shapes=[
            pltpu.VMEM((2048, 1152), jnp.bfloat16),
            pltpu.VMEM((2048, LANES), jnp.float32),
            pltpu.VMEM((8, 2048), jnp.float32),
        ],
        compiler_params=pltpu.CompilerParams(vmem_limit_bytes=48 * 1024 * 1024),
        name="process",
    )(arrived)


def collect_kernel(returned_ref, slot_ref, keep_ref):
    slot = slot_ref[...]
    rows = slot.shape[1]
    values = returned_ref[...]
    first = values.astype(jnp.bfloat16)
    rest = values - first.astype(jnp.float32)
    second = rest.astype(jnp.bfloat16)
    third = (rest - second.astype(jnp.float32)).astype(jnp.bfloat16)
    place = iota((LANES, rows), 0)
    here = as_bf(place == (slot >> 4))
    lines = dot_tn(first, here) + dot_tn(second, here) + dot_tn(third, here)
    keep_ref[...] = jnp.sum(jnp.where(place == (slot & 15), lines, 0.0), axis=0, keepdims=True)


def collect(returned, slot):
    return pl.pallas_call(
        collect_kernel,
        out_shape=jax.ShapeDtypeStruct(slot.shape, jnp.float32),
        in_specs=[pl.BlockSpec(memory_space=pltpu.VMEM)] * 2,
        out_specs=pl.BlockSpec(memory_space=pltpu.VMEM),
        name="collect",
    )(returned, slot)


def on_device(embeddings, assignment, owner_map):
    rows = assignment.shape[0]
    outgoing, slot = dispatch(
        embeddings, assignment.reshape(1, rows), owner_map.reshape(-1, LANES)
    )
    arrived = lax.all_to_all(outgoing, AXES, split_axis=0, concat_axis=0, tiled=True)
    centroid, representative, weight = process(arrived)
    returned = lax.all_to_all(weight, AXES, split_axis=0, concat_axis=0, tiled=True)
    keep_weight = collect(returned, slot).reshape(rows)
    return (centroid, representative, keep_weight)


def solution(mesh):
    in_specs = (P(AXES, None), P(AXES), P())
    out_specs = (P(AXES, None), P(AXES, None), P(AXES))
    return jax.shard_map(
        on_device, mesh=mesh, in_specs=in_specs, out_specs=out_specs, check_vma=False
    )
```

```python
import functools

import jax
import jax.numpy as jnp
from jax import lax
from jax.experimental import pallas as pl
from jax.experimental.pallas import tpu as pltpu
from jax.sharding import PartitionSpec as P

EPSILON = 1e-06
SHARPNESS = 8.0
LANES = 128
AXES = ("samp", "cent")


def iota(shape, dim):
    return lax.broadcasted_iota(jnp.int32, shape, dim)


def dot_nt(a, b):
    return lax.dot_general(a, b, (((1,), (1,)), ((), ())), preferred_element_type=jnp.float32)


def dot_tn(a, b):
    return lax.dot_general(a, b, (((0,), (0,)), ((), ())), preferred_element_type=jnp.float32)


def as_bf(mask):
    return jnp.where(mask, 1.0, 0.0).astype(jnp.bfloat16)


def dispatch_kernel(emb_ref, a_ref, owner_ref, out_ref, slot_ref, unit_ref, rank_ref):
    step = pl.program_id(0)
    rows = emb_ref.shape[0]
    blocks = owner_ref.shape[0]

    @pl.when(step == 0)
    def _():
        x = emb_ref[...]
        scale = lax.rsqrt(jnp.sum(x * x, axis=1, keepdims=True) + EPSILON)
        unit_ref[...] = (x * scale).astype(jnp.bfloat16)

        a = a_ref[...]
        hi = a >> 7
        lo = a & 127
        hi_onehot = as_bf(iota((blocks, rows), 0) == hi)
        owner = owner_ref[...]
        owners = dot_tn(owner.astype(jnp.float32).astype(jnp.bfloat16), hi_onehot)
        lane = iota((LANES, rows), 0)
        dest = jnp.sum(jnp.where(lane == lo, owners, 0.0), axis=0, keepdims=True)
        before = jnp.where(owners == dest, 1.0, 0.0)
        inside = jnp.sum(jnp.where(lane < lo, before, 0.0), axis=0, keepdims=True)

        counts = jnp.zeros((LANES, blocks), jnp.float32)
        device = iota((LANES, LANES), 0)
        column = iota((LANES, blocks), 1)
        for b in range(blocks):
            match = jnp.where(owner[b : b + 1, :] == device, 1.0, 0.0)
            total = jnp.sum(match, axis=1, keepdims=True)
            counts = counts + jnp.where(column == b, total, 0.0)
        earlier = as_bf(iota((blocks, rows), 0) < hi)
        prior = jnp.dot(
            counts.astype(jnp.bfloat16), earlier, preferred_element_type=jnp.float32
        )
        dest_int = dest.astype(jnp.int32)
        here = lane == dest_int
        rank = inside + jnp.sum(jnp.where(here, prior, 0.0), axis=0, keepdims=True)
        rank_ref[...] = rank.astype(jnp.int32)

        upper = as_bf(iota((rows, rows), 0) < iota((rows, rows), 1))
        running = jnp.dot(as_bf(here), upper, preferred_element_type=jnp.float32)
        within = jnp.sum(jnp.where(here, running, 0.0), axis=0, keepdims=True)
        slot_ref[...] = dest_int * 16 + within.astype(jnp.int32)

    i = iota((256, rows), 0)
    wanted = step * 256 + ((i & 127) >> 3) * 16 + (i & 7) + (i >> 7) * 8
    pick = as_bf(slot_ref[...] == wanted)
    moved = jnp.dot(pick, unit_ref[...], preferred_element_type=jnp.float32)
    for half in range(2):
        for j in range(8):
            piece = moved[half * 128 : half * 128 + 128, j * LANES : (j + 1) * LANES]
            out_ref[:, half * 8 + j, :, :] = piece.reshape(16, 8, LANES).astype(jnp.bfloat16)
    rank = rank_ref[...]
    tag = iota((LANES, rows), 0)
    tags = dot_nt(pick[:128], as_bf(tag == rank)) + dot_nt(pick[128:], as_bf(tag == rank + 64))
    out_ref[:, 16, :, :] = tags.reshape(16, 8, LANES).astype(jnp.bfloat16)


def dispatch(embeddings, a_row, owner):
    rows, width = embeddings.shape
    devices = 128
    return pl.pallas_call(
        dispatch_kernel,
        grid=(8,),
        out_shape=(
            jax.ShapeDtypeStruct((devices, 17, 8, LANES), jnp.bfloat16),
            jax.ShapeDtypeStruct((1, rows), jnp.int32),
        ),
        in_specs=[
            pl.BlockSpec((rows, width), lambda i: (0, 0)),
            pl.BlockSpec((1, rows), lambda i: (0, 0)),
            pl.BlockSpec(owner.shape, lambda i: (0, 0)),
        ],
        out_specs=(
            pl.BlockSpec((16, 17, 8, LANES), lambda i: (i, 0, 0, 0)),
            pl.BlockSpec((1, rows), lambda i: (0, 0)),
        ),
        scratch_shapes=[
            pltpu.VMEM((rows, width), jnp.bfloat16),
            pltpu.VMEM((1, rows), jnp.int32),
        ],
        compiler_params=pltpu.CompilerParams(vmem_limit_bytes=40 * 1024 * 1024),
        name="dispatch",
    )(embeddings, a_row, owner)


def process_kernel(in_ref, cent_ref, rep_ref, weight_ref, x_ref, row_ref, col_ref):
    half = 1024
    slots = 2 * half
    width = 1024
    block = 256
    labels = in_ref[:, 16, :, :].reshape(half, LANES)
    lane = iota((LANES, LANES), 1)
    source = iota((LANES, LANES), 0)
    for h in range(2):
        for j in range(8):
            x_ref[h * half : (h + 1) * half, j * LANES : (j + 1) * LANES] = in_ref[
                :, h * 8 + j, :, :
            ].reshape(half, LANES)
        take = as_bf((source == lane + h * 64) & (lane < 64))
        x_ref[h * half : (h + 1) * half, width:] = (
            4.0 * jnp.dot(labels, take, preferred_element_type=jnp.float32)
        ).astype(jnp.bfloat16)

    member4 = x_ref[:, width:]
    sums = dot_tn(member4, x_ref[:, :width]) * 0.25
    inverse = lax.rsqrt(jnp.sum(sums * sums, axis=1, keepdims=True) + EPSILON)
    centroid = sums * inverse
    cent_ref[...] = centroid[:64]
    coarse = centroid.astype(jnp.bfloat16)
    fine = (centroid - coarse.astype(jnp.float32)).astype(jnp.bfloat16)

    row_ref[...] = jnp.zeros_like(row_ref)
    col_ref[...] = jnp.zeros_like(col_ref)
    count = slots // block
    for i in range(count):
        left = x_ref[i * block : (i + 1) * block, :]
        for j in range(i, count):
            gram = dot_nt(left, x_ref[j * block : (j + 1) * block, :])
            kernel = jnp.exp(SHARPNESS * gram - 17.0 * SHARPNESS)
            row_ref[i * block : (i + 1) * block, :] += kernel[:, :LANES] + kernel[:, LANES:]
            if j > i:
                col_ref[:, j * block : (j + 1) * block] += jnp.sum(
                    kernel.reshape(block // 8, 8, block), axis=0
                )

    eye = iota((LANES, LANES), 0) == iota((LANES, LANES), 1)
    totals = jnp.zeros((LANES, LANES), jnp.float32)
    weighted = jnp.zeros((LANES, width), jnp.float32)
    device = iota((LANES, 8, LANES), 2)
    place = iota((LANES, 8, LANES), 1)
    for h in range(2):
        rows = slice(h * half, (h + 1) * half)
        x = x_ref[rows, :width]
        scores = dot_nt(x, jnp.concatenate([coarse, fine], axis=0))
        member = x_ref[rows, width:].astype(jnp.float32) * 0.25
        near = jnp.sum((scores[:, :LANES] + scores[:, LANES:]) * member, axis=1, keepdims=True)
        valid = jnp.sum(member, axis=1, keepdims=True) > 0.5
        density = jnp.sum(row_ref[rows, :], axis=1, keepdims=True)
        across = []
        for k in range(half // LANES):
            start = h * half + k * LANES
            line = jnp.sum(col_ref[:, start : start + LANES], axis=0, keepdims=True)
            across.append(jnp.sum(jnp.where(eye, line, 0.0), axis=1, keepdims=True))
        density = density + jnp.concatenate(across, axis=0)
        weight = jnp.where(valid, jnp.exp(1.0 - near) / jnp.where(valid, density, 1.0), 0.0)
        rounded = weight.astype(jnp.bfloat16).astype(jnp.float32)
        weighted = weighted + dot_tn((member * rounded).astype(jnp.bfloat16), x)
        wide = jnp.broadcast_to(weight, (half, LANES)).reshape(LANES, 8, LANES)
        totals = totals + jnp.sum(jnp.where(device == place + h * 8, wide, 0.0), axis=1)
    weight_ref[...] = totals
    rep = weighted * lax.rsqrt(jnp.sum(weighted * weighted, axis=1, keepdims=True) + EPSILON)
    rep_ref[...] = rep[:64]


def process(arrived):
    devices = arrived.shape[0]
    return pl.pallas_call(
        process_kernel,
        out_shape=(
            jax.ShapeDtypeStruct((64, 1024), jnp.float32),
            jax.ShapeDtypeStruct((64, 1024), jnp.float32),
            jax.ShapeDtypeStruct((devices, LANES), jnp.float32),
        ),
        in_specs=[pl.BlockSpec(memory_space=pltpu.VMEM)],
        out_specs=(pl.BlockSpec(memory_space=pltpu.VMEM),) * 3,
        scratch_shapes=[
            pltpu.VMEM((2048, 1152), jnp.bfloat16),
            pltpu.VMEM((2048, LANES), jnp.float32),
            pltpu.VMEM((8, 2048), jnp.float32),
        ],
        compiler_params=pltpu.CompilerParams(vmem_limit_bytes=48 * 1024 * 1024),
        name="process",
    )(arrived)


def collect_kernel(returned_ref, slot_ref, keep_ref):
    slot = slot_ref[...]
    rows = slot.shape[1]
    values = returned_ref[...]
    first = values.astype(jnp.bfloat16)
    rest = values - first.astype(jnp.float32)
    second = rest.astype(jnp.bfloat16)
    third = (rest - second.astype(jnp.float32)).astype(jnp.bfloat16)
    place = iota((LANES, rows), 0)
    here = as_bf(place == (slot >> 4))
    lines = dot_tn(first, here) + dot_tn(second, here) + dot_tn(third, here)
    keep_ref[...] = jnp.sum(jnp.where(place == (slot & 15), lines, 0.0), axis=0, keepdims=True)


def collect(returned, slot):
    return pl.pallas_call(
        collect_kernel,
        out_shape=jax.ShapeDtypeStruct(slot.shape, jnp.float32),
        in_specs=[pl.BlockSpec(memory_space=pltpu.VMEM)] * 2,
        out_specs=pl.BlockSpec(memory_space=pltpu.VMEM),
        name="collect",
    )(returned, slot)

POOL = 8


def member_of(owner, rank):
    return (owner & ~7) | ((owner + rank) & 7)


def route(a, owner, rows):
    blocks = owner.shape[0]
    hi = a >> 7
    lo = a & 127
    hi_onehot = as_bf(iota((blocks, rows), 0) == hi)
    owners = dot_tn(owner.astype(jnp.float32).astype(jnp.bfloat16), hi_onehot)
    lane = iota((LANES, rows), 0)
    dest = jnp.sum(jnp.where(lane == lo, owners, 0.0), axis=0, keepdims=True)
    before = jnp.where(owners == dest, 1.0, 0.0)
    inside = jnp.sum(jnp.where(lane < lo, before, 0.0), axis=0, keepdims=True)
    counts = jnp.zeros((LANES, blocks), jnp.float32)
    device = iota((LANES, LANES), 0)
    column = iota((LANES, blocks), 1)
    for b in range(blocks):
        match = jnp.where(owner[b : b + 1, :] == device, 1.0, 0.0)
        total = jnp.sum(match, axis=1, keepdims=True)
        counts = counts + jnp.where(column == b, total, 0.0)
    earlier = as_bf(iota((blocks, rows), 0) < hi)
    prior = jnp.dot(counts.astype(jnp.bfloat16), earlier, preferred_element_type=jnp.float32)
    dest_int = dest.astype(jnp.int32)
    rank = inside + jnp.sum(jnp.where(lane == dest_int, prior, 0.0), axis=0, keepdims=True)
    return dest_int, rank.astype(jnp.int32)


def pooled_kernel(
    emb_hbm, a_hbm, owner_hbm, out_ref, place_ref,
    emb_ref, a_ref, owner_ref, unit_ref, slot_ref, tag_ref, flag_ref, sems,
):
    step = pl.program_id(0)
    rows = emb_ref.shape[0]

    @pl.when(step == 0)
    def _():
        first = pltpu.make_async_copy(a_hbm, a_ref, sems.at[0])
        second = pltpu.make_async_copy(owner_hbm, owner_ref, sems.at[1])
        third = pltpu.make_async_copy(emb_hbm, emb_ref, sems.at[2])
        first.start()
        second.start()
        third.start()
        first.wait()
        second.wait()
        owner, rank = route(a_ref[...], owner_ref[...], rows)
        target = member_of(owner, rank)
        lane = iota((LANES, rows), 0)
        here = lane == target
        upper = as_bf(iota((rows, rows), 0) < iota((rows, rows), 1))
        running = jnp.dot(as_bf(here), upper, preferred_element_type=jnp.float32)
        within = jnp.sum(jnp.where(here, running, 0.0), axis=0, keepdims=True)
        count = jnp.sum(jnp.where(here, 1.0, 0.0), axis=1, keepdims=True)
        used = jnp.minimum(count, float(POOL))
        free = POOL - used
        start = lax.axis_index("cent")
        a_dev = iota((LANES, LANES), 0)
        b_dev = iota((LANES, LANES), 1)
        ahead = ((a_dev >> 3) == (b_dev >> 3)) & (((b_dev - start) & 7) < ((a_dev - start) & 7))
        base = jnp.dot(
            as_bf(ahead),
            jnp.broadcast_to(free, (LANES, LANES)).astype(jnp.bfloat16),
            preferred_element_type=jnp.float32,
        )[:, :1]
        past = within > POOL - 0.5
        group = as_bf((iota((16, rows), 0) == (target >> 3)) & past)
        order = jnp.dot(group, upper, preferred_element_type=jnp.float32)
        order = jnp.sum(order * group.astype(jnp.float32), axis=0, keepdims=True)
        fits = (
            ((lane >> 3) == (target >> 3)) & past & (base <= order) & (order < base + free)
        )
        relay = jnp.sum(
            jnp.where(fits, lane.astype(jnp.float32) * POOL + used - base, 0.0),
            axis=0,
            keepdims=True,
        )
        placed = jnp.sum(jnp.where(fits, 1.0, 0.0), axis=0, keepdims=True) > 0.5
        within_int = within.astype(jnp.int32)
        lost = (past & jnp.logical_not(placed)) | (within_int >= 24)
        slot = jnp.where(
            past,
            jnp.where(placed, (relay + order).astype(jnp.int32), -1),
            target * POOL + within_int,
        )
        slot_ref[...] = slot
        tag = (
            (lane == ((owner & 7) * 8 + (rank >> 3)))
            | (lane == 64 + (target & 7))
            | (past & (lane == 72 + within_int - POOL))
        )
        tag_ref[...] = as_bf(tag)
        flag_ref[...] = jnp.broadcast_to(
            jnp.max(jnp.where(lost, 1.0, 0.0), axis=1, keepdims=True), (1, LANES)
        )
        lane_back = jnp.minimum(jnp.where(past, within_int + 64, within_int), 126)
        place_ref[...] = target * LANES + lane_back
        third.wait()
        x = emb_ref[...]
        scale = lax.rsqrt(jnp.sum(x * x, axis=1, keepdims=True) + EPSILON)
        unit_ref[...] = (x * scale).astype(jnp.bfloat16)

    pick = as_bf(slot_ref[...] == iota((256, rows), 0) + step * 256)
    moved = jnp.dot(pick, unit_ref[...], preferred_element_type=jnp.float32)
    for j in range(8):
        piece = moved[:, j * LANES : (j + 1) * LANES]
        out_ref[:, j, :, :] = piece.reshape(32, 8, LANES).astype(jnp.bfloat16)
    tags = dot_nt(pick, tag_ref[...])
    tags = jnp.where(iota((256, LANES), 1) == 127, flag_ref[...], tags)
    out_ref[:, 8, :, :] = tags.reshape(32, 8, LANES).astype(jnp.bfloat16)


def pooled_dispatch(embeddings, a_row, owner):
    rows, width = embeddings.shape
    return pl.pallas_call(
        pooled_kernel,
        grid=(4,),
        out_shape=(
            jax.ShapeDtypeStruct((LANES, 9, 8, LANES), jnp.bfloat16),
            jax.ShapeDtypeStruct((1, rows), jnp.int32),
        ),
        in_specs=[pl.BlockSpec(memory_space=pltpu.HBM)] * 3,
        out_specs=(
            pl.BlockSpec((32, 9, 8, LANES), lambda i: (i, 0, 0, 0)),
            pl.BlockSpec((1, rows), lambda i: (0, 0)),
        ),
        scratch_shapes=[
            pltpu.VMEM((rows, width), jnp.float32),
            pltpu.VMEM((1, rows), jnp.int32),
            pltpu.VMEM(owner.shape, jnp.int32),
            pltpu.VMEM((rows, width), jnp.bfloat16),
            pltpu.VMEM((1, rows), jnp.int32),
            pltpu.VMEM((LANES, rows), jnp.bfloat16),
            pltpu.VMEM((1, LANES), jnp.float32),
            pltpu.SemaphoreType.DMA((3,)),
        ],
        compiler_params=pltpu.CompilerParams(vmem_limit_bytes=40 * 1024 * 1024),
        name="pooled_dispatch",
    )(embeddings, a_row, owner)


def relay_kernel(in_ref, out_ref):
    slots = 1024
    me = lax.axis_index("cent")
    tags = in_ref[:, 8, :, :].reshape(slots, LANES)
    turned = dot_nt(as_bf(iota((LANES, LANES), 0) == iota((LANES, LANES), 1)), tags)
    wrong = jnp.where(iota((8, slots), 0) == me, 0.0, turned[64:72])
    pieces = [wrong[:, k * LANES : (k + 1) * LANES] for k in range(8)]
    stacked = jnp.concatenate(pieces, axis=0)
    upper = as_bf(iota((LANES, LANES), 0) < iota((LANES, LANES), 1))
    inner = jnp.dot(stacked.astype(jnp.bfloat16), upper, preferred_element_type=jnp.float32)
    carry = jnp.zeros((8, 1), jnp.float32)
    member = iota((8, LANES), 0).astype(jnp.float32) * 8.0
    lines = []
    excess = jnp.zeros((8, LANES), jnp.float32)
    for k in range(8):
        order = inner[k * 8 : (k + 1) * 8] + carry
        excess = jnp.maximum(excess, jnp.where(order > 7.5, pieces[k], 0.0))
        goal = jnp.where((pieces[k] > 0.5) & (order < 7.5), member + order + 1.0, 0.0)
        lines.append(jnp.sum(goal, axis=0, keepdims=True))
        carry = carry + jnp.sum(pieces[k], axis=1, keepdims=True)
    goal = jnp.concatenate(lines, axis=1).astype(jnp.int32) - 1
    pick = as_bf(goal == iota((64, slots), 0))
    for j in range(8):
        piece = jnp.dot(
            pick, in_ref[:, j, :, :].reshape(slots, LANES), preferred_element_type=jnp.float32
        )
        out_ref[:, j, :, :] = piece.reshape(8, 8, LANES).astype(jnp.bfloat16)
    lane = iota((slots, LANES), 1)
    source = (iota((slots, LANES), 0) >> 3).astype(jnp.float32)
    wide = tags.astype(jnp.float32)
    named = jnp.where(lane == 96, source, wide).astype(jnp.bfloat16)
    moved = jnp.dot(pick, named, preferred_element_type=jnp.float32)
    flag = jnp.maximum(jnp.max(turned[127:128], axis=1, keepdims=True), jnp.max(excess))
    moved = jnp.where(iota((64, LANES), 1) == 127, flag, moved)
    out_ref[:, 8, :, :] = moved.reshape(8, 8, LANES).astype(jnp.bfloat16)


def relay(arrived):
    return pl.pallas_call(
        relay_kernel,
        out_shape=jax.ShapeDtypeStruct((8, 9, 8, LANES), jnp.bfloat16),
        in_specs=[pl.BlockSpec(memory_space=pltpu.VMEM)],
        out_specs=pl.BlockSpec(memory_space=pltpu.VMEM),
        compiler_params=pltpu.CompilerParams(vmem_limit_bytes=40 * 1024 * 1024),
        name="relay",
    )(arrived)


def pooled_process_kernel(in_ref, fix_ref, share_ref, weight_ref, x_ref, row_ref, col_ref):
    slots = 1024
    extra = 64
    total = x_ref.shape[0]
    width = 1024
    block = LANES
    me = lax.axis_index("cent")
    for j in range(8):
        cols = slice(j * LANES, (j + 1) * LANES)
        x_ref[:slots, cols] = in_ref[:, j, :, :].reshape(slots, LANES)
        x_ref[slots : slots + extra, cols] = fix_ref[:, j, :, :].reshape(extra, LANES)
    x_ref[slots + extra :, :] = jnp.zeros((total - slots - extra, x_ref.shape[1]), jnp.bfloat16)
    tags = in_ref[:, 8, :, :].reshape(slots, LANES).astype(jnp.float32)
    lane = iota((slots, LANES), 1)
    mine = jnp.sum(jnp.where(lane == 64 + me, tags, 0.0), axis=1, keepdims=True)
    x_ref[:slots, width:] = jnp.where(lane < 64, tags * mine * 4.0, 0.0).astype(jnp.bfloat16)
    fix_tags = fix_ref[:, 8, :, :].reshape(extra, LANES).astype(jnp.float32)
    fix_lane = iota((extra, LANES), 1)
    x_ref[slots : slots + extra, width:] = jnp.where(fix_lane < 64, fix_tags * 4.0, 0.0).astype(
        jnp.bfloat16
    )

    sums = dot_tn(x_ref[:, width:], x_ref[:, :width]) * 0.25
    inverse = lax.rsqrt(jnp.sum(sums * sums, axis=1, keepdims=True) + EPSILON)
    centroid = sums * inverse
    for j in range(8):
        share_ref[:, j, :, :] = (
            centroid[:64, j * LANES : (j + 1) * LANES].reshape(8, 8, LANES).astype(jnp.bfloat16)
        )
    coarse = centroid.astype(jnp.bfloat16)
    fine = (centroid - coarse.astype(jnp.float32)).astype(jnp.bfloat16)

    row_ref[...] = jnp.zeros_like(row_ref)
    col_ref[...] = jnp.zeros_like(col_ref)
    count = total // block
    for i in range(count):
        left = x_ref[i * block : (i + 1) * block, :]
        gram = dot_nt(left, x_ref[i * block :, :])
        kernel = jnp.exp(SHARPNESS * gram - 17.0 * SHARPNESS)
        across = kernel[:, :LANES]
        for j in range(1, count - i):
            piece = kernel[:, j * LANES : (j + 1) * LANES]
            across = across + piece
            col_ref[:, (i + j) * block : (i + j + 1) * block] += jnp.sum(
                piece.reshape(block // 8, 8, block), axis=0
            )
        row_ref[i * block : (i + 1) * block, :] = across

    eye = iota((LANES, LANES), 0) == iota((LANES, LANES), 1)
    x = x_ref[:, :width]
    scores = dot_nt(x, jnp.concatenate([coarse, fine], axis=0))
    member = x_ref[:, width:].astype(jnp.float32) * 0.25
    near = jnp.sum((scores[:, :LANES] + scores[:, LANES:]) * member, axis=1, keepdims=True)
    valid = jnp.sum(member, axis=1, keepdims=True) > 0.5
    density = jnp.sum(row_ref[...], axis=1, keepdims=True)
    across = []
    for k in range(count):
        line = jnp.sum(col_ref[:, k * LANES : (k + 1) * LANES], axis=0, keepdims=True)
        across.append(jnp.sum(jnp.where(eye, line, 0.0), axis=1, keepdims=True))
    density = density + jnp.concatenate(across, axis=0)
    weight = jnp.where(valid, jnp.exp(1.0 - near) / jnp.where(valid, density, 1.0), 0.0)
    rounded = weight.astype(jnp.bfloat16).astype(jnp.float32)
    weighted = dot_tn((member * rounded).astype(jnp.bfloat16), x)
    rep = weighted * lax.rsqrt(jnp.sum(weighted * weighted, axis=1, keepdims=True) + EPSILON)
    for j in range(8):
        share_ref[:, 8 + j, :, :] = (
            rep[:64, j * LANES : (j + 1) * LANES].reshape(8, 8, LANES).astype(jnp.bfloat16)
        )

    wide = jnp.broadcast_to(weight[:slots], (slots, LANES)).reshape(LANES, 8, LANES)
    place = iota((LANES, 8, LANES), 2) == iota((LANES, 8, LANES), 1)
    table = jnp.sum(jnp.where(place, wide, 0.0), axis=1)
    source = jnp.sum(jnp.where(fix_lane == 96, fix_tags, 0.0), axis=1, keepdims=True)
    present = valid[slots : slots + extra]
    origin = as_bf((fix_lane.astype(jnp.float32) == source) & present)
    values = jnp.where(
        (fix_lane >= 72) & (fix_lane < 88), fix_tags * weight[slots : slots + extra], 0.0
    )
    for _ in range(3):
        part = values.astype(jnp.bfloat16)
        values = values - part.astype(jnp.float32)
        table = table + dot_tn(origin, part)
    flag = jnp.maximum(
        jnp.max(jnp.where(lane == 127, tags, 0.0)), jnp.max(jnp.where(fix_lane == 127, fix_tags, 0.0))
    )
    weight_ref[...] = jnp.where(iota((LANES, LANES), 1) == 127, flag, table)


def pooled_process(arrived, fixed):
    return pl.pallas_call(
        pooled_process_kernel,
        out_shape=(
            jax.ShapeDtypeStruct((8, 16, 8, LANES), jnp.bfloat16),
            jax.ShapeDtypeStruct((LANES, LANES), jnp.float32),
        ),
        in_specs=[pl.BlockSpec(memory_space=pltpu.VMEM)] * 2,
        out_specs=(pl.BlockSpec(memory_space=pltpu.VMEM),) * 2,
        scratch_shapes=[
            pltpu.VMEM((1152, 1152), jnp.bfloat16),
            pltpu.VMEM((1152, LANES), jnp.float32),
            pltpu.VMEM((8, 1152), jnp.float32),
        ],
        compiler_params=pltpu.CompilerParams(vmem_limit_bytes=40 * 1024 * 1024),
        name="pooled_process",
    )(arrived, fixed)


def finish_kernel(share_ref, returned_ref, place_ref, cent_ref, rep_ref, keep_ref, flag_ref):
    me = lax.axis_index("cent")
    k = iota((64, 64), 0)
    q = iota((64, 64), 1)
    order = as_bf(((k & 7) == (((q >> 3) - me) & 7)) & ((k >> 3) == (q & 7)))
    for j in range(8):
        cols = slice(j * LANES, (j + 1) * LANES)
        for half, ref in enumerate((cent_ref, rep_ref)):
            piece = share_ref[:, half * 8 + j, :, :].reshape(64, LANES)
            ref[:, cols] = jnp.dot(order, piece, preferred_element_type=jnp.float32)
    place = place_ref[...]
    rows = place.shape[1]
    values = returned_ref[...]
    raised = jnp.max(jnp.where(iota((LANES, LANES), 1) == 127, values, 0.0))
    flag_ref[0, 0] = (raised > 0.5).astype(jnp.int32)
    row = iota((LANES, rows), 0)
    here = as_bf(row == (place >> 7))
    lines = jnp.zeros((LANES, rows), jnp.float32)
    for _ in range(3):
        part = values.astype(jnp.bfloat16)
        values = values - part.astype(jnp.float32)
        lines = lines + dot_tn(part, here)
    keep_ref[...] = jnp.sum(jnp.where(row == (place & 127), lines, 0.0), axis=0, keepdims=True)


def finish(share, returned, place):
    vmem = pl.BlockSpec(memory_space=pltpu.VMEM)
    return pl.pallas_call(
        finish_kernel,
        out_shape=(
            jax.ShapeDtypeStruct((64, 1024), jnp.float32),
            jax.ShapeDtypeStruct((64, 1024), jnp.float32),
            jax.ShapeDtypeStruct(place.shape, jnp.float32),
            jax.ShapeDtypeStruct((1, 1), jnp.int32),
        ),
        in_specs=[vmem] * 3,
        out_specs=(vmem, vmem, vmem, pl.BlockSpec(memory_space=pltpu.SMEM)),
        name="finish",
    )(share, returned, place)


def exchange(x, axes):
    return lax.all_to_all(x, axes, split_axis=0, concat_axis=0, tiled=True)


def full_path(embeddings, a_row, owner):
    outgoing, slot = dispatch(embeddings, a_row, owner)
    centroid, representative, weight = process(exchange(outgoing, AXES))
    return (centroid, representative, collect(exchange(weight, AXES), slot))


def on_device(embeddings, assignment, owner_map):
    rows = assignment.shape[0]
    a_row = assignment.reshape(1, rows)
    owner = owner_map.reshape(-1, LANES)
    outgoing, place = pooled_dispatch(embeddings, a_row, owner)
    arrived = exchange(outgoing, AXES)
    fixed = exchange(relay(arrived), "cent")
    share, weight = pooled_process(arrived, fixed)
    returned = exchange(weight, AXES)
    shared = exchange(share, "cent")
    centroid, representative, keep, flag = finish(shared, returned, place)
    centroid, representative, keep = lax.cond(
        flag[0, 0] > 0,
        lambda: full_path(embeddings, a_row, owner),
        lambda: (centroid, representative, keep),
    )
    return (centroid, representative, keep.reshape(rows))


def solution(mesh):
    in_specs = (P(AXES, None), P(AXES), P())
    out_specs = (P(AXES, None), P(AXES, None), P(AXES))
    return jax.shard_map(
        on_device, mesh=mesh, in_specs=in_specs, out_specs=out_specs, check_vma=False
    )
```

```python
import functools

import jax
import jax.numpy as jnp
from jax import lax
from jax.experimental import pallas as pl
from jax.experimental.pallas import tpu as pltpu
from jax.sharding import PartitionSpec as P

EPSILON = 1e-06
SHARPNESS = 8.0
LANES = 128
AXES = ("samp", "cent")


def iota(shape, dim):
    return lax.broadcasted_iota(jnp.int32, shape, dim)


def dot_nt(a, b):
    return lax.dot_general(a, b, (((1,), (1,)), ((), ())), preferred_element_type=jnp.float32)


def dot_tn(a, b):
    return lax.dot_general(a, b, (((0,), (0,)), ((), ())), preferred_element_type=jnp.float32)


def as_bf(mask):
    return jnp.where(mask, 1.0, 0.0).astype(jnp.bfloat16)


def dispatch_kernel(emb_ref, a_ref, owner_ref, out_ref, slot_ref, unit_ref, rank_ref):
    step = pl.program_id(0)
    rows = emb_ref.shape[0]
    blocks = owner_ref.shape[0]

    @pl.when(step == 0)
    def _():
        x = emb_ref[...]
        scale = lax.rsqrt(jnp.sum(x * x, axis=1, keepdims=True) + EPSILON)
        unit_ref[...] = (x * scale).astype(jnp.bfloat16)

        a = a_ref[...]
        hi = a >> 7
        lo = a & 127
        hi_onehot = as_bf(iota((blocks, rows), 0) == hi)
        owner = owner_ref[...]
        owners = dot_tn(owner.astype(jnp.float32).astype(jnp.bfloat16), hi_onehot)
        lane = iota((LANES, rows), 0)
        dest = jnp.sum(jnp.where(lane == lo, owners, 0.0), axis=0, keepdims=True)
        before = jnp.where(owners == dest, 1.0, 0.0)
        inside = jnp.sum(jnp.where(lane < lo, before, 0.0), axis=0, keepdims=True)

        counts = jnp.zeros((LANES, blocks), jnp.float32)
        device = iota((LANES, LANES), 0)
        column = iota((LANES, blocks), 1)
        for b in range(blocks):
            match = jnp.where(owner[b : b + 1, :] == device, 1.0, 0.0)
            total = jnp.sum(match, axis=1, keepdims=True)
            counts = counts + jnp.where(column == b, total, 0.0)
        earlier = as_bf(iota((blocks, rows), 0) < hi)
        prior = jnp.dot(
            counts.astype(jnp.bfloat16), earlier, preferred_element_type=jnp.float32
        )
        dest_int = dest.astype(jnp.int32)
        here = lane == dest_int
        rank = inside + jnp.sum(jnp.where(here, prior, 0.0), axis=0, keepdims=True)
        rank_ref[...] = rank.astype(jnp.int32)

        upper = as_bf(iota((rows, rows), 0) < iota((rows, rows), 1))
        running = jnp.dot(as_bf(here), upper, preferred_element_type=jnp.float32)
        within = jnp.sum(jnp.where(here, running, 0.0), axis=0, keepdims=True)
        slot_ref[...] = dest_int * 16 + within.astype(jnp.int32)

    i = iota((256, rows), 0)
    wanted = step * 256 + ((i & 127) >> 3) * 16 + (i & 7) + (i >> 7) * 8
    pick = as_bf(slot_ref[...] == wanted)
    moved = jnp.dot(pick, unit_ref[...], preferred_element_type=jnp.float32)
    for half in range(2):
        for j in range(8):
            piece = moved[half * 128 : half * 128 + 128, j * LANES : (j + 1) * LANES]
            out_ref[:, half * 8 + j, :, :] = piece.reshape(16, 8, LANES).astype(jnp.bfloat16)
    rank = rank_ref[...]
    tag = iota((LANES, rows), 0)
    tags = dot_nt(pick[:128], as_bf(tag == rank)) + dot_nt(pick[128:], as_bf(tag == rank + 64))
    out_ref[:, 16, :, :] = tags.reshape(16, 8, LANES).astype(jnp.bfloat16)


def dispatch(embeddings, a_row, owner):
    rows, width = embeddings.shape
    devices = 128
    return pl.pallas_call(
        dispatch_kernel,
        grid=(8,),
        out_shape=(
            jax.ShapeDtypeStruct((devices, 17, 8, LANES), jnp.bfloat16),
            jax.ShapeDtypeStruct((1, rows), jnp.int32),
        ),
        in_specs=[
            pl.BlockSpec((rows, width), lambda i: (0, 0)),
            pl.BlockSpec((1, rows), lambda i: (0, 0)),
            pl.BlockSpec(owner.shape, lambda i: (0, 0)),
        ],
        out_specs=(
            pl.BlockSpec((16, 17, 8, LANES), lambda i: (i, 0, 0, 0)),
            pl.BlockSpec((1, rows), lambda i: (0, 0)),
        ),
        scratch_shapes=[
            pltpu.VMEM((rows, width), jnp.bfloat16),
            pltpu.VMEM((1, rows), jnp.int32),
        ],
        compiler_params=pltpu.CompilerParams(vmem_limit_bytes=40 * 1024 * 1024),
        name="dispatch",
    )(embeddings, a_row, owner)


def process_kernel(in_ref, cent_ref, rep_ref, weight_ref, x_ref, row_ref, col_ref):
    half = 1024
    slots = 2 * half
    width = 1024
    block = 256
    labels = in_ref[:, 16, :, :].reshape(half, LANES)
    lane = iota((LANES, LANES), 1)
    source = iota((LANES, LANES), 0)
    for h in range(2):
        for j in range(8):
            x_ref[h * half : (h + 1) * half, j * LANES : (j + 1) * LANES] = in_ref[
                :, h * 8 + j, :, :
            ].reshape(half, LANES)
        take = as_bf((source == lane + h * 64) & (lane < 64))
        x_ref[h * half : (h + 1) * half, width:] = (
            4.0 * jnp.dot(labels, take, preferred_element_type=jnp.float32)
        ).astype(jnp.bfloat16)

    member4 = x_ref[:, width:]
    sums = dot_tn(member4, x_ref[:, :width]) * 0.25
    inverse = lax.rsqrt(jnp.sum(sums * sums, axis=1, keepdims=True) + EPSILON)
    centroid = sums * inverse
    cent_ref[...] = centroid[:64]
    coarse = centroid.astype(jnp.bfloat16)
    fine = (centroid - coarse.astype(jnp.float32)).astype(jnp.bfloat16)

    row_ref[...] = jnp.zeros_like(row_ref)
    col_ref[...] = jnp.zeros_like(col_ref)
    count = slots // block
    for i in range(count):
        left = x_ref[i * block : (i + 1) * block, :]
        for j in range(i, count):
            gram = dot_nt(left, x_ref[j * block : (j + 1) * block, :])
            kernel = jnp.exp(SHARPNESS * gram - 17.0 * SHARPNESS)
            row_ref[i * block : (i + 1) * block, :] += kernel[:, :LANES] + kernel[:, LANES:]
            if j > i:
                col_ref[:, j * block : (j + 1) * block] += jnp.sum(
                    kernel.reshape(block // 8, 8, block), axis=0
                )

    eye = iota((LANES, LANES), 0) == iota((LANES, LANES), 1)
    totals = jnp.zeros((LANES, LANES), jnp.float32)
    weighted = jnp.zeros((LANES, width), jnp.float32)
    device = iota((LANES, 8, LANES), 2)
    place = iota((LANES, 8, LANES), 1)
    for h in range(2):
        rows = slice(h * half, (h + 1) * half)
        x = x_ref[rows, :width]
        scores = dot_nt(x, jnp.concatenate([coarse, fine], axis=0))
        member = x_ref[rows, width:].astype(jnp.float32) * 0.25
        near = jnp.sum((scores[:, :LANES] + scores[:, LANES:]) * member, axis=1, keepdims=True)
        valid = jnp.sum(member, axis=1, keepdims=True) > 0.5
        density = jnp.sum(row_ref[rows, :], axis=1, keepdims=True)
        across = []
        for k in range(half // LANES):
            start = h * half + k * LANES
            line = jnp.sum(col_ref[:, start : start + LANES], axis=0, keepdims=True)
            across.append(jnp.sum(jnp.where(eye, line, 0.0), axis=1, keepdims=True))
        density = density + jnp.concatenate(across, axis=0)
        weight = jnp.where(valid, jnp.exp(1.0 - near) / jnp.where(valid, density, 1.0), 0.0)
        rounded = weight.astype(jnp.bfloat16).astype(jnp.float32)
        weighted = weighted + dot_tn((member * rounded).astype(jnp.bfloat16), x)
        wide = jnp.broadcast_to(weight, (half, LANES)).reshape(LANES, 8, LANES)
        totals = totals + jnp.sum(jnp.where(device == place + h * 8, wide, 0.0), axis=1)
    weight_ref[...] = totals
    rep = weighted * lax.rsqrt(jnp.sum(weighted * weighted, axis=1, keepdims=True) + EPSILON)
    rep_ref[...] = rep[:64]


def process(arrived):
    devices = arrived.shape[0]
    return pl.pallas_call(
        process_kernel,
        out_shape=(
            jax.ShapeDtypeStruct((64, 1024), jnp.float32),
            jax.ShapeDtypeStruct((64, 1024), jnp.float32),
            jax.ShapeDtypeStruct((devices, LANES), jnp.float32),
        ),
        in_specs=[pl.BlockSpec(memory_space=pltpu.VMEM)],
        out_specs=(pl.BlockSpec(memory_space=pltpu.VMEM),) * 3,
        scratch_shapes=[
            pltpu.VMEM((2048, 1152), jnp.bfloat16),
            pltpu.VMEM((2048, LANES), jnp.float32),
            pltpu.VMEM((8, 2048), jnp.float32),
        ],
        compiler_params=pltpu.CompilerParams(vmem_limit_bytes=48 * 1024 * 1024),
        name="process",
    )(arrived)


def collect_kernel(returned_ref, slot_ref, keep_ref):
    slot = slot_ref[...]
    rows = slot.shape[1]
    values = returned_ref[...]
    first = values.astype(jnp.bfloat16)
    rest = values - first.astype(jnp.float32)
    second = rest.astype(jnp.bfloat16)
    third = (rest - second.astype(jnp.float32)).astype(jnp.bfloat16)
    place = iota((LANES, rows), 0)
    here = as_bf(place == (slot >> 4))
    lines = dot_tn(first, here) + dot_tn(second, here) + dot_tn(third, here)
    keep_ref[...] = jnp.sum(jnp.where(place == (slot & 15), lines, 0.0), axis=0, keepdims=True)


def collect(returned, slot):
    return pl.pallas_call(
        collect_kernel,
        out_shape=jax.ShapeDtypeStruct(slot.shape, jnp.float32),
        in_specs=[pl.BlockSpec(memory_space=pltpu.VMEM)] * 2,
        out_specs=pl.BlockSpec(memory_space=pltpu.VMEM),
        name="collect",
    )(returned, slot)

POOL = 8


def member_of(owner, rank):
    return (owner & ~7) | ((owner + rank) & 7)


def route(a, owner, rows):
    blocks = owner.shape[0]
    hi = a >> 7
    lo = a & 127
    hi_onehot = as_bf(iota((blocks, rows), 0) == hi)
    owners = dot_tn(owner.astype(jnp.float32).astype(jnp.bfloat16), hi_onehot)
    lane = iota((LANES, rows), 0)
    dest = jnp.sum(jnp.where(lane == lo, owners, 0.0), axis=0, keepdims=True)
    before = jnp.where(owners == dest, 1.0, 0.0)
    inside = jnp.sum(jnp.where(lane < lo, before, 0.0), axis=0, keepdims=True)
    counts = jnp.zeros((LANES, blocks), jnp.float32)
    device = iota((LANES, LANES), 0)
    column = iota((LANES, blocks), 1)
    for b in range(blocks):
        match = jnp.where(owner[b : b + 1, :] == device, 1.0, 0.0)
        total = jnp.sum(match, axis=1, keepdims=True)
        counts = counts + jnp.where(column == b, total, 0.0)
    earlier = as_bf(iota((blocks, rows), 0) < hi)
    prior = jnp.dot(counts.astype(jnp.bfloat16), earlier, preferred_element_type=jnp.float32)
    dest_int = dest.astype(jnp.int32)
    rank = inside + jnp.sum(jnp.where(lane == dest_int, prior, 0.0), axis=0, keepdims=True)
    return dest_int, rank.astype(jnp.int32)


def pooled_kernel(
    emb_hbm, a_hbm, owner_hbm, out_ref, place_ref,
    emb_ref, a_ref, owner_ref, unit_ref, slot_ref, tag_ref, flag_ref, sems,
):
    step = pl.program_id(0)
    rows = emb_ref.shape[0]

    @pl.when(step == 0)
    def _():
        first = pltpu.make_async_copy(a_hbm, a_ref, sems.at[0])
        second = pltpu.make_async_copy(owner_hbm, owner_ref, sems.at[1])
        third = pltpu.make_async_copy(emb_hbm, emb_ref, sems.at[2])
        first.start()
        second.start()
        third.start()
        first.wait()
        second.wait()
        owner, rank = route(a_ref[...], owner_ref[...], rows)
        target = member_of(owner, rank)
        lane = iota((LANES, rows), 0)
        here = lane == target
        upper = as_bf(iota((rows, rows), 0) < iota((rows, rows), 1))
        running = jnp.dot(as_bf(here), upper, preferred_element_type=jnp.float32)
        within = jnp.sum(jnp.where(here, running, 0.0), axis=0, keepdims=True)
        count = jnp.sum(jnp.where(here, 1.0, 0.0), axis=1, keepdims=True)
        start = lax.axis_index("cent")
        a_dev = iota((LANES, LANES), 0)
        b_dev = iota((LANES, LANES), 1)
        together = (a_dev >> 3) == (b_dev >> 3)
        ahead = together & (((b_dev - start) & 7) < ((a_dev - start) & 7))
        open_slot = (count <= b_dev.astype(jnp.float32)) & (b_dev < POOL)
        level = jnp.dot(as_bf(together), as_bf(open_slot), preferred_element_type=jnp.float32)
        above = jnp.dot(
            level.astype(jnp.bfloat16), as_bf(a_dev > b_dev), preferred_element_type=jnp.float32
        )
        turn = above + jnp.dot(as_bf(ahead), as_bf(open_slot), preferred_element_type=jnp.float32)
        turn = jnp.where(open_slot, turn + (a_dev >> 3).astype(jnp.float32) * 1024.0, -1.0)
        past = within > POOL - 0.5
        group = as_bf((iota((16, rows), 0) == (target >> 3)) & past)
        order = jnp.dot(group, upper, preferred_element_type=jnp.float32)
        order = jnp.sum(order * group.astype(jnp.float32), axis=0, keepdims=True)
        wanted = jnp.where(past, order + (target >> 3).astype(jnp.float32) * 1024.0, -2.0)
        found = jnp.zeros((LANES, rows), jnp.float32)
        label = lane.astype(jnp.float32) * POOL + 1.0
        for i in range(POOL):
            found = found + jnp.where(turn[:, i : i + 1] == wanted, label + i, 0.0)
        relay_slot = jnp.sum(found, axis=0, keepdims=True)
        placed = relay_slot > 0.5
        within_int = within.astype(jnp.int32)
        lost = (past & jnp.logical_not(placed)) | (within_int >= 24)
        slot = jnp.where(past, relay_slot.astype(jnp.int32) - 1, target * POOL + within_int)
        slot_ref[...] = slot
        tag = (
            (lane == ((owner & 7) * 8 + (rank >> 3)))
            | (lane == 64 + (target & 7))
            | (past & (lane == 72 + within_int - POOL))
        )
        tag_ref[...] = as_bf(tag)
        flag_ref[...] = jnp.broadcast_to(
            jnp.max(jnp.where(lost, 1.0, 0.0), axis=1, keepdims=True), (1, LANES)
        )
        lane_back = jnp.minimum(jnp.where(past, within_int + 64, within_int), 126)
        place_ref[...] = target * LANES + lane_back
        third.wait()
        x = emb_ref[...]
        scale = lax.rsqrt(jnp.sum(x * x, axis=1, keepdims=True) + EPSILON)
        unit_ref[...] = (x * scale).astype(jnp.bfloat16)

    pick = as_bf(slot_ref[...] == iota((256, rows), 0) + step * 256)
    moved = jnp.dot(pick, unit_ref[...], preferred_element_type=jnp.float32)
    for j in range(8):
        piece = moved[:, j * LANES : (j + 1) * LANES]
        out_ref[:, j, :, :] = piece.reshape(32, 8, LANES).astype(jnp.bfloat16)
    tags = dot_nt(pick, tag_ref[...])
    tags = jnp.where(iota((256, LANES), 1) == 127, flag_ref[...], tags)
    out_ref[:, 8, :, :] = tags.reshape(32, 8, LANES).astype(jnp.bfloat16)


def pooled_dispatch(embeddings, a_row, owner):
    rows, width = embeddings.shape
    return pl.pallas_call(
        pooled_kernel,
        grid=(4,),
        out_shape=(
            jax.ShapeDtypeStruct((LANES, 9, 8, LANES), jnp.bfloat16),
            jax.ShapeDtypeStruct((1, rows), jnp.int32),
        ),
        in_specs=[pl.BlockSpec(memory_space=pltpu.HBM)] * 3,
        out_specs=(
            pl.BlockSpec((32, 9, 8, LANES), lambda i: (i, 0, 0, 0)),
            pl.BlockSpec((1, rows), lambda i: (0, 0)),
        ),
        scratch_shapes=[
            pltpu.VMEM((rows, width), jnp.float32),
            pltpu.VMEM((1, rows), jnp.int32),
            pltpu.VMEM(owner.shape, jnp.int32),
            pltpu.VMEM((rows, width), jnp.bfloat16),
            pltpu.VMEM((1, rows), jnp.int32),
            pltpu.VMEM((LANES, rows), jnp.bfloat16),
            pltpu.VMEM((1, LANES), jnp.float32),
            pltpu.SemaphoreType.DMA((3,)),
        ],
        compiler_params=pltpu.CompilerParams(vmem_limit_bytes=40 * 1024 * 1024),
        name="pooled_dispatch",
    )(embeddings, a_row, owner)


def relay_kernel(in_ref, out_ref):
    slots = 1024
    me = lax.axis_index("cent")
    tags = in_ref[:, 8, :, :].reshape(slots, LANES)
    turned = dot_nt(as_bf(iota((LANES, LANES), 0) == iota((LANES, LANES), 1)), tags)
    wrong = jnp.where(iota((8, slots), 0) == me, 0.0, turned[64:72])
    pieces = [wrong[:, k * LANES : (k + 1) * LANES] for k in range(8)]
    stacked = jnp.concatenate(pieces, axis=0)
    upper = as_bf(iota((LANES, LANES), 0) < iota((LANES, LANES), 1))
    inner = jnp.dot(stacked.astype(jnp.bfloat16), upper, preferred_element_type=jnp.float32)
    carry = jnp.zeros((8, 1), jnp.float32)
    member = iota((8, LANES), 0).astype(jnp.float32) * 8.0
    lines = []
    excess = jnp.zeros((8, LANES), jnp.float32)
    for k in range(8):
        order = inner[k * 8 : (k + 1) * 8] + carry
        excess = jnp.maximum(excess, jnp.where(order > 15.5, pieces[k], 0.0))
        goal = member + order + jnp.where(order > 7.5, 57.0, 1.0)
        goal = jnp.where((pieces[k] > 0.5) & (order < 15.5), goal, 0.0)
        lines.append(jnp.sum(goal, axis=0, keepdims=True))
        carry = carry + jnp.sum(pieces[k], axis=1, keepdims=True)
    goal = jnp.concatenate(lines, axis=1).astype(jnp.int32) - 1
    pick = as_bf(goal == iota((LANES, slots), 0))
    lane = iota((slots, LANES), 1)
    source = (iota((slots, LANES), 0) >> 3).astype(jnp.float32)
    named = jnp.where(lane == 96, source, tags.astype(jnp.float32)).astype(jnp.bfloat16)
    moved = jnp.dot(pick, named, preferred_element_type=jnp.float32)
    flag = jnp.maximum(jnp.max(turned[127:128], axis=1, keepdims=True), jnp.max(excess))
    moved = jnp.where(iota((LANES, LANES), 1) == 127, flag, moved)
    for half in range(2):
        out_ref[:, 16 + half, :, :] = (
            moved[half * 64 : half * 64 + 64].reshape(8, 8, LANES).astype(jnp.bfloat16)
        )
    for j in range(8):
        piece = jnp.dot(
            pick, in_ref[:, j, :, :].reshape(slots, LANES), preferred_element_type=jnp.float32
        )
        for half in range(2):
            out_ref[:, half * 8 + j, :, :] = (
                piece[half * 64 : half * 64 + 64].reshape(8, 8, LANES).astype(jnp.bfloat16)
            )


def relay(arrived):
    return pl.pallas_call(
        relay_kernel,
        out_shape=jax.ShapeDtypeStruct((8, 18, 8, LANES), jnp.bfloat16),
        in_specs=[pl.BlockSpec(memory_space=pltpu.VMEM)],
        out_specs=pl.BlockSpec(memory_space=pltpu.VMEM),
        compiler_params=pltpu.CompilerParams(vmem_limit_bytes=40 * 1024 * 1024),
        name="relay",
    )(arrived)


SLOTS = 1024
EXTRA = 128
WIDTH = 1024


def direct_kernel(in_ref, x_ref, sums_ref, dense_ref, col_ref):
    me = lax.axis_index("cent")
    block = LANES
    for j in range(8):
        x_ref[:, j * LANES : (j + 1) * LANES] = in_ref[:, j, :, :].reshape(SLOTS, LANES)
    tags = in_ref[:, 8, :, :].reshape(SLOTS, LANES).astype(jnp.float32)
    lane = iota((SLOTS, LANES), 1)
    mine = jnp.sum(jnp.where(lane == 64 + me, tags, 0.0), axis=1, keepdims=True)
    x_ref[:, WIDTH:] = jnp.where(lane < 64, tags * mine * 4.0, 0.0).astype(jnp.bfloat16)
    sums_ref[...] = dot_tn(x_ref[:, WIDTH:], x_ref[:, :WIDTH]) * 0.25

    col_ref[...] = jnp.zeros_like(col_ref)
    count = SLOTS // block
    for i in range(count):
        gram = dot_nt(x_ref[i * block : (i + 1) * block, :], x_ref[i * block :, :])
        kernel = jnp.exp(SHARPNESS * gram - 17.0 * SHARPNESS)
        across = kernel[:, :LANES]
        for j in range(1, count - i):
            piece = kernel[:, j * LANES : (j + 1) * LANES]
            across = across + piece
            col_ref[:, (i + j) * block : (i + j + 1) * block] += jnp.sum(
                piece.reshape(block // 8, 8, block), axis=0
            )
        dense_ref[i * block : (i + 1) * block, :] = across
    eye = iota((LANES, LANES), 0) == iota((LANES, LANES), 1)
    for k in range(count):
        line = jnp.sum(col_ref[:, k * LANES : (k + 1) * LANES], axis=0, keepdims=True)
        dense_ref[k * block : (k + 1) * block, :] += jnp.where(eye, line, 0.0)


def direct(arrived):
    vmem = pl.BlockSpec(memory_space=pltpu.VMEM)
    return pl.pallas_call(
        direct_kernel,
        out_shape=(
            jax.ShapeDtypeStruct((SLOTS, WIDTH + LANES), jnp.bfloat16),
            jax.ShapeDtypeStruct((LANES, WIDTH), jnp.float32),
            jax.ShapeDtypeStruct((SLOTS, LANES), jnp.float32),
        ),
        in_specs=[vmem],
        out_specs=(vmem,) * 3,
        scratch_shapes=[pltpu.VMEM((8, SLOTS), jnp.float32)],
        compiler_params=pltpu.CompilerParams(vmem_limit_bytes=40 * 1024 * 1024),
        cost_estimate=pl.CostEstimate(
            flops=2 * 640 * 1024 * 1152, bytes_accessed=6 * 1024 * 1024, transcendentals=640 * 1024
        ),
        name="direct",
    )(arrived)


def combine_kernel(in_tag_ref, fix_ref, x_ref, sums_ref, dense_ref, *refs):
    share_refs = refs[:8]
    weight_ref, y_ref, share_ref = refs[8:]
    me = lax.axis_index("cent")
    half_extra = EXTRA // 2
    for h in range(2):
        rows = slice(h * half_extra, (h + 1) * half_extra)
        for j in range(8):
            y_ref[rows, j * LANES : (j + 1) * LANES] = fix_ref[:, h * 8 + j, :, :].reshape(
                half_extra, LANES
            )
    fix_tags = jnp.concatenate(
        [fix_ref[:, 16 + h, :, :].reshape(half_extra, LANES) for h in range(2)], axis=0
    ).astype(jnp.float32)
    fix_lane = iota((EXTRA, LANES), 1)
    y_ref[:, WIDTH:] = jnp.where(fix_lane < 64, fix_tags * 4.0, 0.0).astype(jnp.bfloat16)

    sums = sums_ref[...] + dot_tn(y_ref[:, WIDTH:], y_ref[:, :WIDTH]) * 0.25
    inverse = lax.rsqrt(jnp.sum(sums * sums, axis=1, keepdims=True) + EPSILON)
    centroid = sums * inverse
    coarse = centroid.astype(jnp.bfloat16)
    fine = (centroid - coarse.astype(jnp.float32)).astype(jnp.bfloat16)
    both = jnp.concatenate([coarse, fine], axis=0)

    def share(values, first):
        for j in range(8):
            piece = values[:64, j * LANES : (j + 1) * LANES].reshape(8, 8, LANES)
            for c in range(8):
                share_ref[c ^ me, first + j, :, :] = piece[c].astype(jnp.bfloat16)

    share(centroid, 0)
    cross = jnp.exp(SHARPNESS * dot_nt(x_ref[...], y_ref[...]) - 17.0 * SHARPNESS)
    own = jnp.exp(SHARPNESS * dot_nt(y_ref[...], y_ref[...]) - 17.0 * SHARPNESS)
    eye = iota((LANES, LANES), 0) == iota((LANES, LANES), 1)
    line = jnp.sum(cross, axis=0, keepdims=True)

    def weigh(rows_ref, dense):
        rows = rows_ref[:, :WIDTH]
        scores = dot_nt(rows, both)
        member = rows_ref[:, WIDTH:].astype(jnp.float32) * 0.25
        near = jnp.sum((scores[:, :LANES] + scores[:, LANES:]) * member, axis=1, keepdims=True)
        valid = jnp.sum(member, axis=1, keepdims=True) > 0.5
        density = jnp.sum(dense, axis=1, keepdims=True)
        weight = jnp.where(valid, jnp.exp(1.0 - near) / jnp.where(valid, density, 1.0), 0.0)
        rounded = weight.astype(jnp.bfloat16).astype(jnp.float32)
        return weight, valid, dot_tn((member * rounded).astype(jnp.bfloat16), rows)

    weight, _, weighted = weigh(x_ref, dense_ref[...] + cross)
    fix_weight, present, fix_weighted = weigh(y_ref, own + jnp.where(eye, line, 0.0))
    weighted = weighted + fix_weighted
    rep = weighted * lax.rsqrt(jnp.sum(weighted * weighted, axis=1, keepdims=True) + EPSILON)
    share(rep, 8)
    for i in range(8):
        share_refs[i][...] = share_ref[i]

    wide = jnp.broadcast_to(weight, (SLOTS, LANES)).reshape(LANES, 8, LANES)
    place = iota((LANES, 8, LANES), 2) == iota((LANES, 8, LANES), 1)
    table = jnp.sum(jnp.where(place, wide, 0.0), axis=1)
    source = jnp.sum(jnp.where(fix_lane == 96, fix_tags, 0.0), axis=1, keepdims=True)
    origin = as_bf((fix_lane.astype(jnp.float32) == source) & present)
    values = jnp.where((fix_lane >= 72) & (fix_lane < 88), fix_tags * fix_weight, 0.0)
    for _ in range(3):
        part = values.astype(jnp.bfloat16)
        values = values - part.astype(jnp.float32)
        table = table + dot_tn(origin, part)
    tags = in_tag_ref[...].reshape(SLOTS, LANES).astype(jnp.float32)
    flag = jnp.maximum(
        jnp.max(tags, axis=0, keepdims=True), jnp.max(fix_tags, axis=0, keepdims=True)
    )
    weight_ref[...] = jnp.where(iota((LANES, LANES), 1) == 127, flag, table)


def combine(arrived, fixed, x, sums, dense):
    vmem = pl.BlockSpec(memory_space=pltpu.VMEM)
    share = jax.ShapeDtypeStruct((16, 8, LANES), jnp.bfloat16)
    return pl.pallas_call(
        combine_kernel,
        grid=(1,),
        out_shape=(share,) * 8 + (jax.ShapeDtypeStruct((LANES, LANES), jnp.float32),),
        in_specs=[pl.BlockSpec((LANES, 1, 8, LANES), lambda i: (0, 8, 0, 0))] + [vmem] * 4,
        out_specs=(vmem,) * 9,
        scratch_shapes=[
            pltpu.VMEM((EXTRA, WIDTH + LANES), jnp.bfloat16),
            pltpu.VMEM((8, 16, 8, LANES), jnp.bfloat16),
        ],
        compiler_params=pltpu.CompilerParams(vmem_limit_bytes=40 * 1024 * 1024),
        name="combine",
    )(arrived, fixed, x, sums, dense)


def finish_kernel(*refs):
    share_refs = refs[:8]
    returned_ref, place_hbm, cent_ref, rep_ref, keep_ref, flag_ref, place_ref, sem = refs[8:]
    fetch = pltpu.make_async_copy(place_hbm, place_ref, sem)
    fetch.start()
    me = lax.axis_index("cent")
    k = iota((64, 64), 0)
    q = iota((64, 64), 1)
    order = as_bf(((k & 7) == ((((q >> 3) ^ me) - me) & 7)) & ((k >> 3) == (q & 7)))
    for j in range(8):
        cols = slice(j * LANES, (j + 1) * LANES)
        for half, ref in enumerate((cent_ref, rep_ref)):
            piece = jnp.concatenate(
                [r[half * 8 + j, :, :].astype(jnp.float32) for r in share_refs], axis=0
            ).astype(jnp.bfloat16)
            ref[:, cols] = jnp.dot(order, piece, preferred_element_type=jnp.float32)
    values = returned_ref[...]
    raised = jnp.max(jnp.where(iota((LANES, LANES), 1) == 127, values, 0.0))
    flag_ref[0, 0] = (raised > 0.5).astype(jnp.int32)
    fetch.wait()
    place = place_ref[...]
    rows = place.shape[1]
    row = iota((LANES, rows), 0)
    here = as_bf(row == (place >> 7))
    lines = jnp.zeros((LANES, rows), jnp.float32)
    for _ in range(3):
        part = values.astype(jnp.bfloat16)
        values = values - part.astype(jnp.float32)
        lines = lines + dot_tn(part, here)
    keep_ref[...] = jnp.sum(jnp.where(row == (place & 127), lines, 0.0), axis=0, keepdims=True)


def finish(shared, returned, place):
    vmem = pl.BlockSpec(memory_space=pltpu.VMEM)
    return pl.pallas_call(
        finish_kernel,
        out_shape=(
            jax.ShapeDtypeStruct((64, 1024), jnp.float32),
            jax.ShapeDtypeStruct((64, 1024), jnp.float32),
            jax.ShapeDtypeStruct(place.shape, jnp.float32),
            jax.ShapeDtypeStruct((1, 1), jnp.int32),
        ),
        in_specs=[vmem] * 9 + [pl.BlockSpec(memory_space=pltpu.HBM)],
        out_specs=(vmem, vmem, vmem, pl.BlockSpec(memory_space=pltpu.SMEM)),
        scratch_shapes=[pltpu.VMEM(place.shape, jnp.int32), pltpu.SemaphoreType.DMA],
        name="finish",
    )(*shared, returned, place)


def exchange(x, axes):
    return lax.all_to_all(x, axes, split_axis=0, concat_axis=0, tiled=True)


def full_path(embeddings, a_row, owner):
    outgoing, slot = dispatch(embeddings, a_row, owner)
    centroid, representative, weight = process(exchange(outgoing, AXES))
    return (centroid, representative, collect(exchange(weight, AXES), slot))


def on_device(embeddings, assignment, owner_map):
    rows = assignment.shape[0]
    a_row = assignment.reshape(1, rows)
    owner = owner_map.reshape(-1, LANES)
    outgoing, place = pooled_dispatch(embeddings, a_row, owner)
    arrived = exchange(outgoing, AXES)
    fixed = exchange(relay(arrived), "cent")
    *share, weight = combine(arrived, fixed, *direct(arrived))
    members = lax.axis_size("cent")
    shared = [share[0]]
    for i in range(1, members):
        shared.append(lax.ppermute(share[i], "cent", [(c, c ^ i) for c in range(members)]))
    returned = exchange(weight, AXES)
    centroid, representative, keep, flag = finish(shared, returned, place)
    centroid, representative, keep = lax.cond(
        flag[0, 0] > 0,
        lambda: full_path(embeddings, a_row, owner),
        lambda: (centroid, representative, keep),
    )
    return (centroid, representative, keep.reshape(rows))


def solution(mesh):
    in_specs = (P(AXES, None), P(AXES), P())
    out_specs = (P(AXES, None), P(AXES, None), P(AXES))
    return jax.shard_map(
        on_device, mesh=mesh, in_specs=in_specs, out_specs=out_specs, check_vma=False
    )
```

```python
import functools

import jax
import jax.numpy as jnp
from jax import lax
from jax.experimental import pallas as pl
from jax.experimental.pallas import tpu as pltpu
from jax.sharding import PartitionSpec as P

EPSILON = 1e-06
SHARPNESS = 8.0
LANES = 128
AXES = ("samp", "cent")


def iota(shape, dim):
    return lax.broadcasted_iota(jnp.int32, shape, dim)


def dot_nt(a, b):
    return lax.dot_general(a, b, (((1,), (1,)), ((), ())), preferred_element_type=jnp.float32)


def dot_tn(a, b):
    return lax.dot_general(a, b, (((0,), (0,)), ((), ())), preferred_element_type=jnp.float32)


def as_bf(mask):
    return jnp.where(mask, 1.0, 0.0).astype(jnp.bfloat16)


def dispatch_kernel(emb_ref, a_ref, owner_ref, out_ref, slot_ref, unit_ref, rank_ref):
    step = pl.program_id(0)
    rows = emb_ref.shape[0]
    blocks = owner_ref.shape[0]

    @pl.when(step == 0)
    def _():
        x = emb_ref[...]
        scale = lax.rsqrt(jnp.sum(x * x, axis=1, keepdims=True) + EPSILON)
        unit_ref[...] = (x * scale).astype(jnp.bfloat16)

        a = a_ref[...]
        hi = a >> 7
        lo = a & 127
        hi_onehot = as_bf(iota((blocks, rows), 0) == hi)
        owner = owner_ref[...]
        owners = dot_tn(owner.astype(jnp.float32).astype(jnp.bfloat16), hi_onehot)
        lane = iota((LANES, rows), 0)
        dest = jnp.sum(jnp.where(lane == lo, owners, 0.0), axis=0, keepdims=True)
        before = jnp.where(owners == dest, 1.0, 0.0)
        inside = jnp.sum(jnp.where(lane < lo, before, 0.0), axis=0, keepdims=True)

        counts = jnp.zeros((LANES, blocks), jnp.float32)
        device = iota((LANES, LANES), 0)
        column = iota((LANES, blocks), 1)
        for b in range(blocks):
            match = jnp.where(owner[b : b + 1, :] == device, 1.0, 0.0)
            total = jnp.sum(match, axis=1, keepdims=True)
            counts = counts + jnp.where(column == b, total, 0.0)
        earlier = as_bf(iota((blocks, rows), 0) < hi)
        prior = jnp.dot(
            counts.astype(jnp.bfloat16), earlier, preferred_element_type=jnp.float32
        )
        dest_int = dest.astype(jnp.int32)
        here = lane == dest_int
        rank = inside + jnp.sum(jnp.where(here, prior, 0.0), axis=0, keepdims=True)
        rank_ref[...] = rank.astype(jnp.int32)

        upper = as_bf(iota((rows, rows), 0) < iota((rows, rows), 1))
        running = jnp.dot(as_bf(here), upper, preferred_element_type=jnp.float32)
        within = jnp.sum(jnp.where(here, running, 0.0), axis=0, keepdims=True)
        slot_ref[...] = dest_int * 16 + within.astype(jnp.int32)

    i = iota((256, rows), 0)
    wanted = step * 256 + ((i & 127) >> 3) * 16 + (i & 7) + (i >> 7) * 8
    pick = as_bf(slot_ref[...] == wanted)
    moved = jnp.dot(pick, unit_ref[...], preferred_element_type=jnp.float32)
    for half in range(2):
        for j in range(8):
            piece = moved[half * 128 : half * 128 + 128, j * LANES : (j + 1) * LANES]
            out_ref[:, half * 8 + j, :, :] = piece.reshape(16, 8, LANES).astype(jnp.bfloat16)
    rank = rank_ref[...]
    tag = iota((LANES, rows), 0)
    tags = dot_nt(pick[:128], as_bf(tag == rank)) + dot_nt(pick[128:], as_bf(tag == rank + 64))
    out_ref[:, 16, :, :] = tags.reshape(16, 8, LANES).astype(jnp.bfloat16)


def dispatch(embeddings, a_row, owner):
    rows, width = embeddings.shape
    devices = 128
    return pl.pallas_call(
        dispatch_kernel,
        grid=(8,),
        out_shape=(
            jax.ShapeDtypeStruct((devices, 17, 8, LANES), jnp.bfloat16),
            jax.ShapeDtypeStruct((1, rows), jnp.int32),
        ),
        in_specs=[
            pl.BlockSpec((rows, width), lambda i: (0, 0)),
            pl.BlockSpec((1, rows), lambda i: (0, 0)),
            pl.BlockSpec(owner.shape, lambda i: (0, 0)),
        ],
        out_specs=(
            pl.BlockSpec((16, 17, 8, LANES), lambda i: (i, 0, 0, 0)),
            pl.BlockSpec((1, rows), lambda i: (0, 0)),
        ),
        scratch_shapes=[
            pltpu.VMEM((rows, width), jnp.bfloat16),
            pltpu.VMEM((1, rows), jnp.int32),
        ],
        compiler_params=pltpu.CompilerParams(vmem_limit_bytes=40 * 1024 * 1024),
        name="dispatch",
    )(embeddings, a_row, owner)


def process_kernel(in_ref, cent_ref, rep_ref, weight_ref, x_ref, row_ref, col_ref):
    half = 1024
    slots = 2 * half
    width = 1024
    block = 256
    labels = in_ref[:, 16, :, :].reshape(half, LANES)
    lane = iota((LANES, LANES), 1)
    source = iota((LANES, LANES), 0)
    for h in range(2):
        for j in range(8):
            x_ref[h * half : (h + 1) * half, j * LANES : (j + 1) * LANES] = in_ref[
                :, h * 8 + j, :, :
            ].reshape(half, LANES)
        take = as_bf((source == lane + h * 64) & (lane < 64))
        x_ref[h * half : (h + 1) * half, width:] = (
            4.0 * jnp.dot(labels, take, preferred_element_type=jnp.float32)
        ).astype(jnp.bfloat16)

    member4 = x_ref[:, width:]
    sums = dot_tn(member4, x_ref[:, :width]) * 0.25
    inverse = lax.rsqrt(jnp.sum(sums * sums, axis=1, keepdims=True) + EPSILON)
    centroid = sums * inverse
    cent_ref[...] = centroid[:64]
    coarse = centroid.astype(jnp.bfloat16)
    fine = (centroid - coarse.astype(jnp.float32)).astype(jnp.bfloat16)

    row_ref[...] = jnp.zeros_like(row_ref)
    col_ref[...] = jnp.zeros_like(col_ref)
    count = slots // block
    for i in range(count):
        left = x_ref[i * block : (i + 1) * block, :]
        for j in range(i, count):
            gram = dot_nt(left, x_ref[j * block : (j + 1) * block, :])
            kernel = jnp.exp(SHARPNESS * gram - 17.0 * SHARPNESS)
            row_ref[i * block : (i + 1) * block, :] += kernel[:, :LANES] + kernel[:, LANES:]
            if j > i:
                col_ref[:, j * block : (j + 1) * block] += jnp.sum(
                    kernel.reshape(block // 8, 8, block), axis=0
                )

    eye = iota((LANES, LANES), 0) == iota((LANES, LANES), 1)
    totals = jnp.zeros((LANES, LANES), jnp.float32)
    weighted = jnp.zeros((LANES, width), jnp.float32)
    device = iota((LANES, 8, LANES), 2)
    place = iota((LANES, 8, LANES), 1)
    for h in range(2):
        rows = slice(h * half, (h + 1) * half)
        x = x_ref[rows, :width]
        scores = dot_nt(x, jnp.concatenate([coarse, fine], axis=0))
        member = x_ref[rows, width:].astype(jnp.float32) * 0.25
        near = jnp.sum((scores[:, :LANES] + scores[:, LANES:]) * member, axis=1, keepdims=True)
        valid = jnp.sum(member, axis=1, keepdims=True) > 0.5
        density = jnp.sum(row_ref[rows, :], axis=1, keepdims=True)
        across = []
        for k in range(half // LANES):
            start = h * half + k * LANES
            line = jnp.sum(col_ref[:, start : start + LANES], axis=0, keepdims=True)
            across.append(jnp.sum(jnp.where(eye, line, 0.0), axis=1, keepdims=True))
        density = density + jnp.concatenate(across, axis=0)
        weight = jnp.where(valid, jnp.exp(1.0 - near) / jnp.where(valid, density, 1.0), 0.0)
        rounded = weight.astype(jnp.bfloat16).astype(jnp.float32)
        weighted = weighted + dot_tn((member * rounded).astype(jnp.bfloat16), x)
        wide = jnp.broadcast_to(weight, (half, LANES)).reshape(LANES, 8, LANES)
        totals = totals + jnp.sum(jnp.where(device == place + h * 8, wide, 0.0), axis=1)
    weight_ref[...] = totals
    rep = weighted * lax.rsqrt(jnp.sum(weighted * weighted, axis=1, keepdims=True) + EPSILON)
    rep_ref[...] = rep[:64]


def process(arrived):
    devices = arrived.shape[0]
    return pl.pallas_call(
        process_kernel,
        out_shape=(
            jax.ShapeDtypeStruct((64, 1024), jnp.float32),
            jax.ShapeDtypeStruct((64, 1024), jnp.float32),
            jax.ShapeDtypeStruct((devices, LANES), jnp.float32),
        ),
        in_specs=[pl.BlockSpec(memory_space=pltpu.VMEM)],
        out_specs=(pl.BlockSpec(memory_space=pltpu.VMEM),) * 3,
        scratch_shapes=[
            pltpu.VMEM((2048, 1152), jnp.bfloat16),
            pltpu.VMEM((2048, LANES), jnp.float32),
            pltpu.VMEM((8, 2048), jnp.float32),
        ],
        compiler_params=pltpu.CompilerParams(vmem_limit_bytes=48 * 1024 * 1024),
        name="process",
    )(arrived)


def collect_kernel(returned_ref, slot_ref, keep_hbm, keep_ref, sem):
    slot = slot_ref[...]
    rows = slot.shape[1]
    values = returned_ref[...]
    first = values.astype(jnp.bfloat16)
    rest = values - first.astype(jnp.float32)
    second = rest.astype(jnp.bfloat16)
    third = (rest - second.astype(jnp.float32)).astype(jnp.bfloat16)
    place = iota((LANES, rows), 0)
    here = as_bf(place == (slot >> 4))
    lines = dot_tn(first, here) + dot_tn(second, here) + dot_tn(third, here)
    keep_ref[...] = jnp.sum(jnp.where(place == (slot & 15), lines, 0.0), axis=0, keepdims=True)
    store = pltpu.make_async_copy(keep_ref, keep_hbm, sem)
    store.start()
    store.wait()


def collect(returned, slot):
    return pl.pallas_call(
        collect_kernel,
        out_shape=jax.ShapeDtypeStruct(slot.shape, jnp.float32),
        in_specs=[pl.BlockSpec(memory_space=pltpu.VMEM)] * 2,
        out_specs=pl.BlockSpec(memory_space=pltpu.HBM),
        scratch_shapes=[pltpu.VMEM(slot.shape, jnp.float32), pltpu.SemaphoreType.DMA],
        name="collect",
    )(returned, slot)

POOL = 8
GRANT = 24 * 1024 * 1024


def member_of(owner, rank):
    return (owner & ~7) | ((owner + rank) & 7)


def route(a, owner, rows):
    blocks = owner.shape[0]
    hi = a >> 7
    lo = a & 127
    hi_onehot = as_bf(iota((blocks, rows), 0) == hi)
    owners = dot_tn(owner.astype(jnp.float32).astype(jnp.bfloat16), hi_onehot)
    lane = iota((LANES, rows), 0)
    dest = jnp.sum(jnp.where(lane == lo, owners, 0.0), axis=0, keepdims=True)
    before = jnp.where(owners == dest, 1.0, 0.0)
    inside = jnp.sum(jnp.where(lane < lo, before, 0.0), axis=0, keepdims=True)
    counts = jnp.zeros((LANES, blocks), jnp.float32)
    device = iota((LANES, LANES), 0)
    column = iota((LANES, blocks), 1)
    for b in range(blocks):
        match = jnp.where(owner[b : b + 1, :] == device, 1.0, 0.0)
        total = jnp.sum(match, axis=1, keepdims=True)
        counts = counts + jnp.where(column == b, total, 0.0)
    earlier = as_bf(iota((blocks, rows), 0) < hi)
    prior = jnp.dot(counts.astype(jnp.bfloat16), earlier, preferred_element_type=jnp.float32)
    dest_int = dest.astype(jnp.int32)
    rank = inside + jnp.sum(jnp.where(lane == dest_int, prior, 0.0), axis=0, keepdims=True)
    return dest_int, rank.astype(jnp.int32)


def pooled_kernel(
    emb_hbm, a_hbm, owner_hbm, out_ref, place_hbm,
    emb_ref, a_ref, owner_ref, unit_ref, slot_ref, tag_ref, flag_ref, back_ref, sems,
):
    step = pl.program_id(0)
    rows = emb_ref.shape[0]

    @pl.when(step == 0)
    def _():
        first = pltpu.make_async_copy(a_hbm, a_ref, sems.at[0])
        second = pltpu.make_async_copy(owner_hbm, owner_ref, sems.at[1])
        third = pltpu.make_async_copy(emb_hbm, emb_ref, sems.at[2])
        first.start()
        second.start()
        third.start()
        first.wait()
        second.wait()
        owner, rank = route(a_ref[...], owner_ref[...], rows)
        target = member_of(owner, rank)
        lane = iota((LANES, rows), 0)
        here = lane == target
        upper = as_bf(iota((rows, rows), 0) < iota((rows, rows), 1))
        running = jnp.dot(as_bf(here), upper, preferred_element_type=jnp.float32)
        within = jnp.sum(jnp.where(here, running, 0.0), axis=0, keepdims=True)
        count = jnp.sum(jnp.where(here, 1.0, 0.0), axis=1, keepdims=True)
        start = lax.axis_index("cent")
        a_dev = iota((LANES, LANES), 0)
        b_dev = iota((LANES, LANES), 1)
        together = (a_dev >> 3) == (b_dev >> 3)
        ahead = together & (((b_dev - start) & 7) < ((a_dev - start) & 7))
        open_slot = (count <= b_dev.astype(jnp.float32)) & (b_dev < POOL)
        level = jnp.dot(as_bf(together), as_bf(open_slot), preferred_element_type=jnp.float32)
        above = jnp.dot(
            level.astype(jnp.bfloat16), as_bf(a_dev > b_dev), preferred_element_type=jnp.float32
        )
        turn = above + jnp.dot(as_bf(ahead), as_bf(open_slot), preferred_element_type=jnp.float32)
        turn = jnp.where(open_slot, turn + (a_dev >> 3).astype(jnp.float32) * 1024.0, -1.0)
        past = within > POOL - 0.5
        group = as_bf((iota((16, rows), 0) == (target >> 3)) & past)
        order = jnp.dot(group, upper, preferred_element_type=jnp.float32)
        order = jnp.sum(order * group.astype(jnp.float32), axis=0, keepdims=True)
        wanted = jnp.where(past, order + (target >> 3).astype(jnp.float32) * 1024.0, -2.0)
        found = jnp.zeros((LANES, rows), jnp.float32)
        label = lane.astype(jnp.float32) * POOL + 1.0
        for i in range(POOL):
            found = found + jnp.where(turn[:, i : i + 1] == wanted, label + i, 0.0)
        relay_slot = jnp.sum(found, axis=0, keepdims=True)
        placed = relay_slot > 0.5
        within_int = within.astype(jnp.int32)
        lost = (past & jnp.logical_not(placed)) | (within_int >= 24)
        slot = jnp.where(past, relay_slot.astype(jnp.int32) - 1, target * POOL + within_int)
        slot_ref[...] = slot
        tag = (
            (lane == ((owner & 7) * 8 + (rank >> 3)))
            | (lane == 64 + (target & 7))
            | (past & (lane == 72 + within_int - POOL))
        )
        tag_ref[...] = as_bf(tag)
        flag_ref[...] = jnp.broadcast_to(
            jnp.max(jnp.where(lost, 1.0, 0.0), axis=1, keepdims=True), (1, LANES)
        )
        lane_back = jnp.minimum(jnp.where(past, within_int + 64, within_int), 126)
        back_ref[...] = target * LANES + lane_back
        fourth = pltpu.make_async_copy(back_ref, place_hbm, sems.at[3])
        fourth.start()
        third.wait()
        x = emb_ref[...]
        scale = lax.rsqrt(jnp.sum(x * x, axis=1, keepdims=True) + EPSILON)
        unit_ref[...] = (x * scale).astype(jnp.bfloat16)
        fourth.wait()

    pick = as_bf(slot_ref[...] == iota((256, rows), 0) + step * 256)
    moved = jnp.dot(pick, unit_ref[...], preferred_element_type=jnp.float32)
    for j in range(8):
        piece = moved[:, j * LANES : (j + 1) * LANES]
        out_ref[:, j, :, :] = piece.reshape(32, 8, LANES).astype(jnp.bfloat16)
    tags = dot_nt(pick, tag_ref[...])
    tags = jnp.where(iota((256, LANES), 1) == 127, flag_ref[...], tags)
    out_ref[:, 8, :, :] = tags.reshape(32, 8, LANES).astype(jnp.bfloat16)


def pooled_dispatch(embeddings, a_row, owner):
    rows, width = embeddings.shape
    return pl.pallas_call(
        pooled_kernel,
        grid=(4,),
        out_shape=(
            jax.ShapeDtypeStruct((LANES, 9, 8, LANES), jnp.bfloat16),
            jax.ShapeDtypeStruct((1, rows), jnp.int32),
        ),
        in_specs=[pl.BlockSpec(memory_space=pltpu.HBM)] * 3,
        out_specs=(
            pl.BlockSpec((32, 9, 8, LANES), lambda i: (i, 0, 0, 0)),
            pl.BlockSpec(memory_space=pltpu.HBM),
        ),
        scratch_shapes=[
            pltpu.VMEM((rows, width), jnp.float32),
            pltpu.VMEM((1, rows), jnp.int32),
            pltpu.VMEM(owner.shape, jnp.int32),
            pltpu.VMEM((rows, width), jnp.bfloat16),
            pltpu.VMEM((1, rows), jnp.int32),
            pltpu.VMEM((LANES, rows), jnp.bfloat16),
            pltpu.VMEM((1, LANES), jnp.float32),
            pltpu.VMEM((1, rows), jnp.int32),
            pltpu.SemaphoreType.DMA((4,)),
        ],
        compiler_params=pltpu.CompilerParams(vmem_limit_bytes=GRANT),
        name="pooled_dispatch",
    )(embeddings, a_row, owner)


def relay_kernel(in_ref, out_ref):
    slots = 1024
    me = lax.axis_index("cent")
    tags = in_ref[:, 8, :, :].reshape(slots, LANES)
    turned = dot_nt(as_bf(iota((LANES, LANES), 0) == iota((LANES, LANES), 1)), tags)
    wrong = jnp.where(iota((8, slots), 0) == me, 0.0, turned[64:72])
    pieces = [wrong[:, k * LANES : (k + 1) * LANES] for k in range(8)]
    stacked = jnp.concatenate(pieces, axis=0)
    upper = as_bf(iota((LANES, LANES), 0) < iota((LANES, LANES), 1))
    inner = jnp.dot(stacked.astype(jnp.bfloat16), upper, preferred_element_type=jnp.float32)
    carry = jnp.zeros((8, 1), jnp.float32)
    member = iota((8, LANES), 0).astype(jnp.float32) * 8.0
    lines = []
    excess = jnp.zeros((8, LANES), jnp.float32)
    for k in range(8):
        order = inner[k * 8 : (k + 1) * 8] + carry
        excess = jnp.maximum(excess, jnp.where(order > 15.5, pieces[k], 0.0))
        goal = member + order + jnp.where(order > 7.5, 57.0, 1.0)
        goal = jnp.where((pieces[k] > 0.5) & (order < 15.5), goal, 0.0)
        lines.append(jnp.sum(goal, axis=0, keepdims=True))
        carry = carry + jnp.sum(pieces[k], axis=1, keepdims=True)
    goal = jnp.concatenate(lines, axis=1).astype(jnp.int32) - 1
    pick = as_bf(goal == iota((LANES, slots), 0))
    lane = iota((slots, LANES), 1)
    source = (iota((slots, LANES), 0) >> 3).astype(jnp.float32)
    named = jnp.where(lane == 96, source, tags.astype(jnp.float32)).astype(jnp.bfloat16)
    moved = jnp.dot(pick, named, preferred_element_type=jnp.float32)
    flag = jnp.maximum(jnp.max(turned[127:128], axis=1, keepdims=True), jnp.max(excess))
    moved = jnp.where(iota((LANES, LANES), 1) == 127, flag, moved)
    for half in range(2):
        out_ref[:, 16 + half, :, :] = (
            moved[half * 64 : half * 64 + 64].reshape(8, 8, LANES).astype(jnp.bfloat16)
        )
    for j in range(8):
        piece = jnp.dot(
            pick, in_ref[:, j, :, :].reshape(slots, LANES), preferred_element_type=jnp.float32
        )
        for half in range(2):
            out_ref[:, half * 8 + j, :, :] = (
                piece[half * 64 : half * 64 + 64].reshape(8, 8, LANES).astype(jnp.bfloat16)
            )


def relay(arrived):
    return pl.pallas_call(
        relay_kernel,
        out_shape=jax.ShapeDtypeStruct((8, 18, 8, LANES), jnp.bfloat16),
        in_specs=[pl.BlockSpec(memory_space=pltpu.VMEM)],
        out_specs=pl.BlockSpec(memory_space=pltpu.VMEM),
        compiler_params=pltpu.CompilerParams(vmem_limit_bytes=GRANT),
        name="relay",
    )(arrived)


SLOTS = 1024
EXTRA = 128
WIDTH = 1024


def gather_rows(in_ref, x_ref):
    for j in range(8):
        x_ref[:, j * LANES : (j + 1) * LANES] = in_ref[:, j, :, :].reshape(SLOTS, LANES)


def direct_kernel(in_ref, sums_ref, note_ref, x_ref, dense_ref, col_ref):
    me = lax.axis_index("cent")
    block = LANES
    gather_rows(in_ref, x_ref)
    tags = in_ref[:, 8, :, :].reshape(SLOTS, LANES).astype(jnp.float32)
    lane = iota((SLOTS, LANES), 1)
    mine = jnp.sum(jnp.where(lane == 64 + me, tags, 0.0), axis=1, keepdims=True)
    member4 = jnp.where(lane < 64, tags * mine * 4.0, 0.0)
    x_ref[:, WIDTH:] = member4.astype(jnp.bfloat16)
    sums_ref[...] = dot_tn(x_ref[:, WIDTH:], x_ref[:, :WIDTH])[:64] * 0.25

    col_ref[...] = jnp.zeros_like(col_ref)
    count = SLOTS // block
    for i in range(count):
        gram = dot_nt(x_ref[i * block : (i + 1) * block, :], x_ref[i * block :, :])
        kernel = jnp.exp(SHARPNESS * gram - 17.0 * SHARPNESS)
        across = kernel[:, :LANES]
        for j in range(1, count - i):
            piece = kernel[:, j * LANES : (j + 1) * LANES]
            across = across + piece
            col_ref[:, (i + j) * block : (i + j + 1) * block] += jnp.sum(
                piece.reshape(block // 8, 8, block), axis=0
            )
        dense_ref[i * block : (i + 1) * block, :] = across
    eye = iota((LANES, LANES), 0) == iota((LANES, LANES), 1)
    for k in range(count):
        line = jnp.sum(col_ref[:, k * LANES : (k + 1) * LANES], axis=0, keepdims=True)
        dense_ref[k * block : (k + 1) * block, :] += jnp.where(eye, line, 0.0)
    density = jnp.sum(dense_ref[...], axis=1, keepdims=True)
    note = jnp.where(lane == 127, tags, member4)
    for i in range(64, 67):
        part = density.astype(jnp.bfloat16).astype(jnp.float32)
        density = density - part
        note = jnp.where(lane == i, part, note)
    note_ref[...] = note.astype(jnp.bfloat16)


def direct(arrived):
    vmem = pl.BlockSpec(memory_space=pltpu.VMEM)
    return pl.pallas_call(
        direct_kernel,
        out_shape=(
            jax.ShapeDtypeStruct((64, WIDTH), jnp.float32),
            jax.ShapeDtypeStruct((SLOTS, LANES), jnp.bfloat16),
        ),
        in_specs=[vmem],
        out_specs=(vmem,) * 2,
        scratch_shapes=[
            pltpu.VMEM((SLOTS, WIDTH + LANES), jnp.bfloat16),
            pltpu.VMEM((SLOTS, LANES), jnp.float32),
            pltpu.VMEM((8, SLOTS), jnp.float32),
        ],
        compiler_params=pltpu.CompilerParams(vmem_limit_bytes=GRANT),
        cost_estimate=pl.CostEstimate(
            flops=2 * 640 * 1024 * 1152, bytes_accessed=6 * 1024 * 1024, transcendentals=640 * 1024
        ),
        name="direct",
    )(arrived)


def combine_kernel(in_ref, fix_ref, sums_ref, note_ref, *refs):
    share_refs = refs[:8]
    weight_ref, x_ref, y_ref, share_ref = refs[8:]
    me = lax.axis_index("cent")
    gather_rows(in_ref, x_ref)
    note = note_ref[...].astype(jnp.float32)
    lane = iota((SLOTS, LANES), 1)
    x_ref[:, WIDTH:] = jnp.where(lane < 64, note, 0.0).astype(jnp.bfloat16)
    density = jnp.where((lane >= 64) & (lane < 67), note, 0.0)
    half_extra = EXTRA // 2
    for h in range(2):
        rows = slice(h * half_extra, (h + 1) * half_extra)
        for j in range(8):
            y_ref[rows, j * LANES : (j + 1) * LANES] = fix_ref[:, h * 8 + j, :, :].reshape(
                half_extra, LANES
            )
    fix_tags = jnp.concatenate(
        [fix_ref[:, 16 + h, :, :].reshape(half_extra, LANES) for h in range(2)], axis=0
    ).astype(jnp.float32)
    fix_lane = iota((EXTRA, LANES), 1)
    y_ref[:, WIDTH:] = jnp.where(fix_lane < 64, fix_tags * 4.0, 0.0).astype(jnp.bfloat16)

    sums = sums_ref[...] + dot_tn(y_ref[:, WIDTH:], y_ref[:, :WIDTH])[:64] * 0.25
    inverse = lax.rsqrt(jnp.sum(sums * sums, axis=1, keepdims=True) + EPSILON)
    centroid = sums * inverse
    coarse = jnp.concatenate([centroid, jnp.zeros_like(centroid)], axis=0).astype(jnp.bfloat16)

    def share(values, first):
        for j in range(8):
            piece = values[:, j * LANES : (j + 1) * LANES].reshape(8, 8, LANES)
            for c in range(8):
                share_ref[c ^ me, first + j, :, :] = piece[c].astype(jnp.bfloat16)

    share(centroid, 0)
    cross = jnp.exp(SHARPNESS * dot_nt(x_ref[...], y_ref[...]) - 17.0 * SHARPNESS)
    own = jnp.exp(SHARPNESS * dot_nt(y_ref[...], y_ref[...]) - 17.0 * SHARPNESS)
    eye = iota((LANES, LANES), 0) == iota((LANES, LANES), 1)
    line = jnp.sum(cross, axis=0, keepdims=True)

    def weigh(rows_ref, dense):
        rows = rows_ref[:, :WIDTH]
        member = rows_ref[:, WIDTH:].astype(jnp.float32) * 0.25
        near = jnp.sum(dot_nt(rows, coarse) * member, axis=1, keepdims=True)
        valid = jnp.sum(member, axis=1, keepdims=True) > 0.5
        density = jnp.sum(dense, axis=1, keepdims=True)
        weight = jnp.where(valid, jnp.exp(1.0 - near) / jnp.where(valid, density, 1.0), 0.0)
        rounded = weight.astype(jnp.bfloat16).astype(jnp.float32)
        return weight, valid, dot_tn((member * rounded).astype(jnp.bfloat16), rows)

    weight, _, weighted = weigh(x_ref, density + cross)
    fix_weight, present, fix_weighted = weigh(y_ref, own + jnp.where(eye, line, 0.0))
    weighted = (weighted + fix_weighted)[:64]
    rep = weighted * lax.rsqrt(jnp.sum(weighted * weighted, axis=1, keepdims=True) + EPSILON)
    share(rep, 8)
    for i in range(8):
        share_refs[i][...] = share_ref[i]

    wide = jnp.broadcast_to(weight, (SLOTS, LANES)).reshape(LANES, 8, LANES)
    place = iota((LANES, 8, LANES), 2) == iota((LANES, 8, LANES), 1)
    table = jnp.sum(jnp.where(place, wide, 0.0), axis=1)
    source = jnp.sum(jnp.where(fix_lane == 96, fix_tags, 0.0), axis=1, keepdims=True)
    origin = as_bf((fix_lane.astype(jnp.float32) == source) & present)
    values = jnp.where((fix_lane >= 72) & (fix_lane < 88), fix_tags * fix_weight, 0.0)
    for _ in range(3):
        part = values.astype(jnp.bfloat16)
        values = values - part.astype(jnp.float32)
        table = table + dot_tn(origin, part)
    flag = jnp.maximum(
        jnp.max(note, axis=0, keepdims=True),
        jnp.max(fix_tags, axis=0, keepdims=True),
    )
    weight_ref[...] = jnp.where(iota((LANES, LANES), 1) == 127, flag, table)


def combine(arrived, fixed, sums, note):
    vmem = pl.BlockSpec(memory_space=pltpu.VMEM)
    share = jax.ShapeDtypeStruct((16, 8, LANES), jnp.bfloat16)
    return pl.pallas_call(
        combine_kernel,
        out_shape=(share,) * 8 + (jax.ShapeDtypeStruct((LANES, LANES), jnp.float32),),
        in_specs=[vmem] * 4,
        out_specs=(vmem,) * 9,
        scratch_shapes=[
            pltpu.VMEM((SLOTS, WIDTH + LANES), jnp.bfloat16),
            pltpu.VMEM((EXTRA, WIDTH + LANES), jnp.bfloat16),
            pltpu.VMEM((8, 16, 8, LANES), jnp.bfloat16),
        ],
        compiler_params=pltpu.CompilerParams(vmem_limit_bytes=GRANT),
        name="combine",
    )(arrived, fixed, sums, note)


def finish_kernel(*refs):
    share_refs = refs[:8]
    returned_ref, place_hbm, cent_ref, rep_ref, keep_hbm, flag_ref = refs[8:14]
    place_ref, keep_ref, mixed_ref, fetch_sem, keep_sem = refs[14:]
    fetch = pltpu.make_async_copy(place_hbm, place_ref, fetch_sem)
    fetch.start()
    me = lax.axis_index("cent")
    values = returned_ref[...]
    raised = jnp.max(jnp.where(iota((LANES, LANES), 1) == 127, values, 0.0))
    flag_ref[0, 0] = (raised > 0.5).astype(jnp.int32)
    fetch.wait()
    place = place_ref[...]
    rows = place.shape[1]
    row = iota((LANES, rows), 0)
    here = as_bf(row == (place >> 7))
    lines = jnp.zeros((LANES, rows), jnp.float32)
    for _ in range(3):
        part = values.astype(jnp.bfloat16)
        values = values - part.astype(jnp.float32)
        lines = lines + dot_tn(part, here)
    keep_ref[...] = jnp.sum(jnp.where(row == (place & 127), lines, 0.0), axis=0, keepdims=True)
    store = pltpu.make_async_copy(keep_ref, keep_hbm, keep_sem)
    store.start()
    for i in range(8):
        residue = ((me ^ i) - me) & 7
        for j in range(16):
            tile = share_refs[i][j, :, :].astype(jnp.float32)
            mixed_ref[pl.ds(j * 64 + residue, 8, stride=8), :] = tile
    for j in range(8):
        cols = slice(j * LANES, (j + 1) * LANES)
        cent_ref[:, cols] = mixed_ref[j * 64 : j * 64 + 64, :]
        rep_ref[:, cols] = mixed_ref[512 + j * 64 : 512 + j * 64 + 64, :]
    store.wait()


def finish(shared, returned, place):
    vmem = pl.BlockSpec(memory_space=pltpu.VMEM)
    return pl.pallas_call(
        finish_kernel,
        out_shape=(
            jax.ShapeDtypeStruct((64, 1024), jnp.float32),
            jax.ShapeDtypeStruct((64, 1024), jnp.float32),
            jax.ShapeDtypeStruct(place.shape, jnp.float32),
            jax.ShapeDtypeStruct((1, 1), jnp.int32),
        ),
        in_specs=[vmem] * 9 + [pl.BlockSpec(memory_space=pltpu.HBM)],
        out_specs=(
            vmem,
            vmem,
            pl.BlockSpec(memory_space=pltpu.HBM),
            pl.BlockSpec(memory_space=pltpu.SMEM),
        ),
        scratch_shapes=[
            pltpu.VMEM(place.shape, jnp.int32),
            pltpu.VMEM(place.shape, jnp.float32),
            pltpu.VMEM((1024, LANES), jnp.float32),
            pltpu.SemaphoreType.DMA,
            pltpu.SemaphoreType.DMA,
        ],
        compiler_params=pltpu.CompilerParams(vmem_limit_bytes=GRANT),
        name="finish",
    )(*shared, returned, place)


def exchange(x, axes):
    return lax.all_to_all(x, axes, split_axis=0, concat_axis=0, tiled=True)


def full_path(embeddings, a_row, owner):
    outgoing, slot = dispatch(embeddings, a_row, owner)
    centroid, representative, weight = process(exchange(outgoing, AXES))
    return (centroid, representative, collect(exchange(weight, AXES), slot))


def on_device(embeddings, assignment, owner_map):
    rows = assignment.shape[0]
    a_row = assignment.reshape(1, rows)
    owner = owner_map.reshape(-1, LANES)
    outgoing, place = pooled_dispatch(embeddings, a_row, owner)
    arrived = exchange(outgoing, AXES)
    fixed = exchange(relay(arrived), "cent")
    *share, weight = combine(arrived, fixed, *direct(arrived))
    members = lax.axis_size("cent")
    shared = [share[0]]
    for i in range(1, members):
        shared.append(lax.ppermute(share[i], "cent", [(c, c ^ i) for c in range(members)]))
    returned = exchange(weight, AXES)
    centroid, representative, keep, flag = finish(shared, returned, place)
    centroid, representative, keep = lax.switch(
        flag[0, 0],
        (lambda: (centroid, representative, keep), lambda: full_path(embeddings, a_row, owner)),
    )
    return (centroid, representative, keep.reshape(rows))


def solution(mesh):
    in_specs = (P(AXES, None), P(AXES), P())
    out_specs = (P(AXES, None), P(AXES, None), P(AXES))
    return jax.shard_map(
        on_device, mesh=mesh, in_specs=in_specs, out_specs=out_specs, check_vma=False
    )
```

```python
import functools

import jax
import jax.numpy as jnp
from jax import lax
from jax.experimental import pallas as pl
from jax.experimental.pallas import tpu as pltpu
from jax.sharding import PartitionSpec as P

EPSILON = 1e-06
SHARPNESS = 8.0
LANES = 128
AXES = ("samp", "cent")


def iota(shape, dim):
    return lax.broadcasted_iota(jnp.int32, shape, dim)


def dot_nt(a, b):
    return lax.dot_general(a, b, (((1,), (1,)), ((), ())), preferred_element_type=jnp.float32)


def dot_tn(a, b):
    return lax.dot_general(a, b, (((0,), (0,)), ((), ())), preferred_element_type=jnp.float32)


def as_bf(mask):
    return jnp.where(mask, 1.0, 0.0).astype(jnp.bfloat16)


def dispatch_kernel(emb_ref, a_ref, owner_ref, out_ref, slot_ref, unit_ref, rank_ref):
    step = pl.program_id(0)
    rows = emb_ref.shape[0]
    blocks = owner_ref.shape[0]

    @pl.when(step == 0)
    def _():
        x = emb_ref[...]
        scale = lax.rsqrt(jnp.sum(x * x, axis=1, keepdims=True) + EPSILON)
        unit_ref[...] = (x * scale).astype(jnp.bfloat16)

        a = a_ref[...]
        hi = a >> 7
        lo = a & 127
        hi_onehot = as_bf(iota((blocks, rows), 0) == hi)
        owner = owner_ref[...]
        owners = dot_tn(owner.astype(jnp.float32).astype(jnp.bfloat16), hi_onehot)
        lane = iota((LANES, rows), 0)
        dest = jnp.sum(jnp.where(lane == lo, owners, 0.0), axis=0, keepdims=True)
        before = jnp.where(owners == dest, 1.0, 0.0)
        inside = jnp.sum(jnp.where(lane < lo, before, 0.0), axis=0, keepdims=True)

        counts = jnp.zeros((LANES, blocks), jnp.float32)
        device = iota((LANES, LANES), 0)
        column = iota((LANES, blocks), 1)
        for b in range(blocks):
            match = jnp.where(owner[b : b + 1, :] == device, 1.0, 0.0)
            total = jnp.sum(match, axis=1, keepdims=True)
            counts = counts + jnp.where(column == b, total, 0.0)
        earlier = as_bf(iota((blocks, rows), 0) < hi)
        prior = jnp.dot(
            counts.astype(jnp.bfloat16), earlier, preferred_element_type=jnp.float32
        )
        dest_int = dest.astype(jnp.int32)
        here = lane == dest_int
        rank = inside + jnp.sum(jnp.where(here, prior, 0.0), axis=0, keepdims=True)
        rank_ref[...] = rank.astype(jnp.int32)

        upper = as_bf(iota((rows, rows), 0) < iota((rows, rows), 1))
        running = jnp.dot(as_bf(here), upper, preferred_element_type=jnp.float32)
        within = jnp.sum(jnp.where(here, running, 0.0), axis=0, keepdims=True)
        slot_ref[...] = dest_int * 16 + within.astype(jnp.int32)

    i = iota((256, rows), 0)
    wanted = step * 256 + ((i & 127) >> 3) * 16 + (i & 7) + (i >> 7) * 8
    pick = as_bf(slot_ref[...] == wanted)
    moved = jnp.dot(pick, unit_ref[...], preferred_element_type=jnp.float32)
    for half in range(2):
        for j in range(8):
            piece = moved[half * 128 : half * 128 + 128, j * LANES : (j + 1) * LANES]
            out_ref[:, half * 8 + j, :, :] = piece.reshape(16, 8, LANES).astype(jnp.bfloat16)
    rank = rank_ref[...]
    tag = iota((LANES, rows), 0)
    tags = dot_nt(pick[:128], as_bf(tag == rank)) + dot_nt(pick[128:], as_bf(tag == rank + 64))
    out_ref[:, 16, :, :] = tags.reshape(16, 8, LANES).astype(jnp.bfloat16)


def dispatch(embeddings, a_row, owner):
    rows, width = embeddings.shape
    devices = 128
    return pl.pallas_call(
        dispatch_kernel,
        grid=(8,),
        out_shape=(
            jax.ShapeDtypeStruct((devices, 17, 8, LANES), jnp.bfloat16),
            jax.ShapeDtypeStruct((1, rows), jnp.int32),
        ),
        in_specs=[
            pl.BlockSpec((rows, width), lambda i: (0, 0)),
            pl.BlockSpec((1, rows), lambda i: (0, 0)),
            pl.BlockSpec(owner.shape, lambda i: (0, 0)),
        ],
        out_specs=(
            pl.BlockSpec((16, 17, 8, LANES), lambda i: (i, 0, 0, 0)),
            pl.BlockSpec((1, rows), lambda i: (0, 0)),
        ),
        scratch_shapes=[
            pltpu.VMEM((rows, width), jnp.bfloat16),
            pltpu.VMEM((1, rows), jnp.int32),
        ],
        compiler_params=pltpu.CompilerParams(vmem_limit_bytes=40 * 1024 * 1024),
        name="dispatch",
    )(embeddings, a_row, owner)


def process_kernel(in_ref, cent_ref, rep_ref, weight_ref, x_ref, row_ref, col_ref):
    half = 1024
    slots = 2 * half
    width = 1024
    block = 256
    labels = in_ref[:, 16, :, :].reshape(half, LANES)
    lane = iota((LANES, LANES), 1)
    source = iota((LANES, LANES), 0)
    for h in range(2):
        for j in range(8):
            x_ref[h * half : (h + 1) * half, j * LANES : (j + 1) * LANES] = in_ref[
                :, h * 8 + j, :, :
            ].reshape(half, LANES)
        take = as_bf((source == lane + h * 64) & (lane < 64))
        x_ref[h * half : (h + 1) * half, width:] = (
            4.0 * jnp.dot(labels, take, preferred_element_type=jnp.float32)
        ).astype(jnp.bfloat16)

    member4 = x_ref[:, width:]
    sums = dot_tn(member4, x_ref[:, :width]) * 0.25
    inverse = lax.rsqrt(jnp.sum(sums * sums, axis=1, keepdims=True) + EPSILON)
    centroid = sums * inverse
    cent_ref[...] = centroid[:64]
    coarse = centroid.astype(jnp.bfloat16)
    fine = (centroid - coarse.astype(jnp.float32)).astype(jnp.bfloat16)

    row_ref[...] = jnp.zeros_like(row_ref)
    col_ref[...] = jnp.zeros_like(col_ref)
    count = slots // block
    for i in range(count):
        left = x_ref[i * block : (i + 1) * block, :]
        for j in range(i, count):
            gram = dot_nt(left, x_ref[j * block : (j + 1) * block, :])
            kernel = jnp.exp(SHARPNESS * gram - 17.0 * SHARPNESS)
            row_ref[i * block : (i + 1) * block, :] += kernel[:, :LANES] + kernel[:, LANES:]
            if j > i:
                col_ref[:, j * block : (j + 1) * block] += jnp.sum(
                    kernel.reshape(block // 8, 8, block), axis=0
                )

    eye = iota((LANES, LANES), 0) == iota((LANES, LANES), 1)
    totals = jnp.zeros((LANES, LANES), jnp.float32)
    weighted = jnp.zeros((LANES, width), jnp.float32)
    device = iota((LANES, 8, LANES), 2)
    place = iota((LANES, 8, LANES), 1)
    for h in range(2):
        rows = slice(h * half, (h + 1) * half)
        x = x_ref[rows, :width]
        scores = dot_nt(x, jnp.concatenate([coarse, fine], axis=0))
        member = x_ref[rows, width:].astype(jnp.float32) * 0.25
        near = jnp.sum((scores[:, :LANES] + scores[:, LANES:]) * member, axis=1, keepdims=True)
        valid = jnp.sum(member, axis=1, keepdims=True) > 0.5
        density = jnp.sum(row_ref[rows, :], axis=1, keepdims=True)
        across = []
        for k in range(half // LANES):
            start = h * half + k * LANES
            line = jnp.sum(col_ref[:, start : start + LANES], axis=0, keepdims=True)
            across.append(jnp.sum(jnp.where(eye, line, 0.0), axis=1, keepdims=True))
        density = density + jnp.concatenate(across, axis=0)
        weight = jnp.where(valid, jnp.exp(1.0 - near) / jnp.where(valid, density, 1.0), 0.0)
        rounded = weight.astype(jnp.bfloat16).astype(jnp.float32)
        weighted = weighted + dot_tn((member * rounded).astype(jnp.bfloat16), x)
        wide = jnp.broadcast_to(weight, (half, LANES)).reshape(LANES, 8, LANES)
        totals = totals + jnp.sum(jnp.where(device == place + h * 8, wide, 0.0), axis=1)
    weight_ref[...] = totals
    rep = weighted * lax.rsqrt(jnp.sum(weighted * weighted, axis=1, keepdims=True) + EPSILON)
    rep_ref[...] = rep[:64]


def process(arrived):
    devices = arrived.shape[0]
    return pl.pallas_call(
        process_kernel,
        out_shape=(
            jax.ShapeDtypeStruct((64, 1024), jnp.float32),
            jax.ShapeDtypeStruct((64, 1024), jnp.float32),
            jax.ShapeDtypeStruct((devices, LANES), jnp.float32),
        ),
        in_specs=[pl.BlockSpec(memory_space=pltpu.VMEM)],
        out_specs=(pl.BlockSpec(memory_space=pltpu.VMEM),) * 3,
        scratch_shapes=[
            pltpu.VMEM((2048, 1152), jnp.bfloat16),
            pltpu.VMEM((2048, LANES), jnp.float32),
            pltpu.VMEM((8, 2048), jnp.float32),
        ],
        compiler_params=pltpu.CompilerParams(vmem_limit_bytes=48 * 1024 * 1024),
        name="process",
    )(arrived)


def collect_kernel(returned_ref, slot_ref, keep_hbm, keep_ref, sem):
    slot = slot_ref[...]
    rows = slot.shape[1]
    values = returned_ref[...]
    first = values.astype(jnp.bfloat16)
    rest = values - first.astype(jnp.float32)
    second = rest.astype(jnp.bfloat16)
    third = (rest - second.astype(jnp.float32)).astype(jnp.bfloat16)
    place = iota((LANES, rows), 0)
    here = as_bf(place == (slot >> 4))
    lines = dot_tn(first, here) + dot_tn(second, here) + dot_tn(third, here)
    keep_ref[...] = jnp.sum(jnp.where(place == (slot & 15), lines, 0.0), axis=0, keepdims=True)
    store = pltpu.make_async_copy(keep_ref, keep_hbm, sem)
    store.start()
    store.wait()


def collect(returned, slot):
    return pl.pallas_call(
        collect_kernel,
        out_shape=jax.ShapeDtypeStruct(slot.shape, jnp.float32),
        in_specs=[pl.BlockSpec(memory_space=pltpu.VMEM)] * 2,
        out_specs=pl.BlockSpec(memory_space=pltpu.HBM),
        scratch_shapes=[pltpu.VMEM(slot.shape, jnp.float32), pltpu.SemaphoreType.DMA],
        name="collect",
    )(returned, slot)

POOL = 8
GRANT = 24 * 1024 * 1024


def member_of(owner, rank):
    return (owner & ~7) | ((owner + rank) & 7)


def route(a, owner, rows):
    blocks = owner.shape[0]
    hi = a >> 7
    lo = a & 127
    hi_onehot = as_bf(iota((blocks, rows), 0) == hi)
    owners = dot_tn(owner.astype(jnp.float32).astype(jnp.bfloat16), hi_onehot)
    lane = iota((LANES, rows), 0)
    dest = jnp.sum(jnp.where(lane == lo, owners, 0.0), axis=0, keepdims=True)
    before = jnp.where(owners == dest, 1.0, 0.0)
    inside = jnp.sum(jnp.where(lane < lo, before, 0.0), axis=0, keepdims=True)
    turned = jnp.transpose(owner.astype(jnp.float32))
    twice = jnp.concatenate([turned, turned - 64.0], axis=1).astype(jnp.bfloat16)
    one = jnp.ones((), jnp.bfloat16)
    nil = jnp.zeros((), jnp.bfloat16)
    lines = []
    for d in range(64):
        match = jnp.where(twice == jnp.full((), d, jnp.bfloat16), one, nil)
        parts = [match[i * 16 : (i + 1) * 16] for i in range(8)]
        while len(parts) > 1:
            parts = [parts[i] + parts[i + 1] for i in range(0, len(parts), 2)]
        lines.append(jnp.sum(parts[0].astype(jnp.float32), axis=0, keepdims=True))
    pairs = jnp.concatenate(lines, axis=0)
    counts = jnp.concatenate([pairs[:, :64], pairs[:, 64:]], axis=0)
    earlier = as_bf(iota((blocks, rows), 0) < hi)
    prior = jnp.dot(counts.astype(jnp.bfloat16), earlier, preferred_element_type=jnp.float32)
    dest_int = dest.astype(jnp.int32)
    rank = inside + jnp.sum(jnp.where(lane == dest_int, prior, 0.0), axis=0, keepdims=True)
    return dest_int, rank.astype(jnp.int32)


def pooled_kernel(
    emb_hbm, a_hbm, owner_hbm, out_ref, place_hbm,
    emb_ref, a_ref, owner_ref, unit_ref, slot_ref, tag_ref, flag_ref, back_ref, sems,
):
    rows = emb_ref.shape[0]

    first = pltpu.make_async_copy(a_hbm, a_ref, sems.at[0])
    second = pltpu.make_async_copy(owner_hbm, owner_ref, sems.at[1])
    third = pltpu.make_async_copy(emb_hbm, emb_ref, sems.at[2])
    first.start()
    second.start()
    third.start()
    first.wait()
    second.wait()
    third.wait()
    x = emb_ref[...]
    scale = lax.rsqrt(jnp.sum(x * x, axis=1, keepdims=True) + EPSILON)
    unit_ref[...] = (x * scale).astype(jnp.bfloat16)
    owner, rank = route(a_ref[...], owner_ref[...], rows)
    target = member_of(owner, rank)
    lane = iota((LANES, rows), 0)
    here = lane == target
    upper = as_bf(iota((rows, rows), 0) < iota((rows, rows), 1))
    running = jnp.dot(as_bf(here), upper, preferred_element_type=jnp.float32)
    within = jnp.sum(jnp.where(here, running, 0.0), axis=0, keepdims=True)
    count = jnp.sum(jnp.where(here, 1.0, 0.0), axis=1, keepdims=True)
    start = lax.axis_index("cent")
    a_dev = iota((LANES, LANES), 0)
    b_dev = iota((LANES, LANES), 1)
    together = (a_dev >> 3) == (b_dev >> 3)
    ahead = together & (((b_dev - start) & 7) < ((a_dev - start) & 7))
    open_slot = (count <= b_dev.astype(jnp.float32)) & (b_dev < POOL)
    level = jnp.dot(as_bf(together), as_bf(open_slot), preferred_element_type=jnp.float32)
    above = jnp.dot(
        level.astype(jnp.bfloat16), as_bf(a_dev > b_dev), preferred_element_type=jnp.float32
    )
    turn = above + jnp.dot(as_bf(ahead), as_bf(open_slot), preferred_element_type=jnp.float32)
    turn = jnp.where(open_slot, turn + (a_dev >> 3).astype(jnp.float32) * 1024.0, -1.0)
    past = within > POOL - 0.5
    group = as_bf((iota((16, rows), 0) == (target >> 3)) & past)
    order = jnp.dot(group, upper, preferred_element_type=jnp.float32)
    order = jnp.sum(order * group.astype(jnp.float32), axis=0, keepdims=True)
    wanted = jnp.where(past, order + (target >> 3).astype(jnp.float32) * 1024.0, -2.0)
    found = jnp.zeros((LANES, rows), jnp.float32)
    label = lane.astype(jnp.float32) * POOL + 1.0
    for i in range(POOL):
        found = found + jnp.where(turn[:, i : i + 1] == wanted, label + i, 0.0)
    relay_slot = jnp.sum(found, axis=0, keepdims=True)
    placed = relay_slot > 0.5
    within_int = within.astype(jnp.int32)
    lost = (past & jnp.logical_not(placed)) | (within_int >= 24)
    slot = jnp.where(past, relay_slot.astype(jnp.int32) - 1, target * POOL + within_int)
    slot_ref[...] = slot
    tag = (
        (lane == ((owner & 7) * 8 + (rank >> 3)))
        | (lane == 64 + (target & 7))
        | (past & (lane == 72 + within_int - POOL))
    )
    tag_ref[...] = as_bf(tag)
    flag_ref[...] = jnp.broadcast_to(
        jnp.max(jnp.where(lost, 1.0, 0.0), axis=1, keepdims=True), (1, LANES)
    )
    lane_back = jnp.minimum(jnp.where(past, within_int + 64, within_int), 126)
    back_ref[...] = target * LANES + lane_back
    fourth = pltpu.make_async_copy(back_ref, place_hbm, sems.at[3])
    fourth.start()
    chunk = 512
    for k in range(1024 // chunk):
        pick = as_bf(slot_ref[...] == iota((chunk, rows), 0) + k * chunk)
        outs = pl.ds(k * chunk // 8, chunk // 8)
        tags = dot_nt(pick, tag_ref[...])
        tags = jnp.where(iota((chunk, LANES), 1) == 127, flag_ref[...], tags)
        out_ref[outs, 8, :, :] = tags.reshape(chunk // 8, 8, LANES).astype(jnp.bfloat16)
        for j in range(4):
            moved = jnp.dot(
                pick, unit_ref[:, j * 256 : (j + 1) * 256], preferred_element_type=jnp.float32
            )
            for h in range(2):
                piece = moved[:, h * LANES : (h + 1) * LANES]
                out_ref[outs, 2 * j + h, :, :] = piece.reshape(chunk // 8, 8, LANES).astype(
                    jnp.bfloat16
                )
    fourth.wait()


def pooled_dispatch(embeddings, a_row, owner):
    rows, width = embeddings.shape
    return pl.pallas_call(
        pooled_kernel,
        out_shape=(
            jax.ShapeDtypeStruct((LANES, 9, 8, LANES), jnp.bfloat16),
            jax.ShapeDtypeStruct((1, rows), jnp.int32),
        ),
        in_specs=[pl.BlockSpec(memory_space=pltpu.HBM)] * 3,
        out_specs=(
            pl.BlockSpec(memory_space=pltpu.VMEM),
            pl.BlockSpec(memory_space=pltpu.HBM),
        ),
        scratch_shapes=[
            pltpu.VMEM((rows, width), jnp.float32),
            pltpu.VMEM((1, rows), jnp.int32),
            pltpu.VMEM(owner.shape, jnp.int32),
            pltpu.VMEM((rows, width), jnp.bfloat16),
            pltpu.VMEM((1, rows), jnp.int32),
            pltpu.VMEM((LANES, rows), jnp.bfloat16),
            pltpu.VMEM((1, LANES), jnp.float32),
            pltpu.VMEM((1, rows), jnp.int32),
            pltpu.SemaphoreType.DMA((4,)),
        ],
        compiler_params=pltpu.CompilerParams(vmem_limit_bytes=GRANT),
        name="pooled_dispatch",
    )(embeddings, a_row, owner)


def relay_kernel(in_ref, out_ref):
    slots = 1024
    me = lax.axis_index("cent")
    tags = in_ref[:, 8, :, :].reshape(slots, LANES)
    turned = dot_nt(as_bf(iota((LANES, LANES), 0) == iota((LANES, LANES), 1)), tags)
    wrong = jnp.where(iota((8, slots), 0) == me, 0.0, turned[64:72])
    pieces = [wrong[:, k * LANES : (k + 1) * LANES] for k in range(8)]
    stacked = jnp.concatenate(pieces, axis=0)
    upper = as_bf(iota((LANES, LANES), 0) < iota((LANES, LANES), 1))
    inner = jnp.dot(stacked.astype(jnp.bfloat16), upper, preferred_element_type=jnp.float32)
    carry = jnp.zeros((8, 1), jnp.float32)
    member = iota((8, LANES), 0).astype(jnp.float32) * 8.0
    lines = []
    excess = jnp.zeros((8, LANES), jnp.float32)
    for k in range(8):
        order = inner[k * 8 : (k + 1) * 8] + carry
        excess = jnp.maximum(excess, jnp.where(order > 15.5, pieces[k], 0.0))
        goal = member + order + jnp.where(order > 7.5, 57.0, 1.0)
        goal = jnp.where((pieces[k] > 0.5) & (order < 15.5), goal, 0.0)
        lines.append(jnp.sum(goal, axis=0, keepdims=True))
        carry = carry + jnp.sum(pieces[k], axis=1, keepdims=True)
    goal = jnp.concatenate(lines, axis=1).astype(jnp.int32) - 1
    pick = as_bf(goal == iota((LANES, slots), 0))
    lane = iota((slots, LANES), 1)
    source = (iota((slots, LANES), 0) >> 3).astype(jnp.float32)
    named = jnp.where(lane == 96, source, tags.astype(jnp.float32)).astype(jnp.bfloat16)
    moved = jnp.dot(pick, named, preferred_element_type=jnp.float32)
    flag = jnp.maximum(jnp.max(turned[127:128], axis=1, keepdims=True), jnp.max(excess))
    moved = jnp.where(iota((LANES, LANES), 1) == 127, flag, moved)
    for half in range(2):
        out_ref[:, 16 + half, :, :] = (
            moved[half * 64 : half * 64 + 64].reshape(8, 8, LANES).astype(jnp.bfloat16)
        )
    for j in range(0, 8, 2):
        pair = [in_ref[:, j + k, :, :].reshape(slots, LANES) for k in range(2)]
        piece = jnp.dot(pick, jnp.concatenate(pair, axis=1), preferred_element_type=jnp.float32)
        for half in range(2):
            for k in range(2):
                part = piece[half * 64 : half * 64 + 64, k * LANES : (k + 1) * LANES]
                out_ref[:, half * 8 + j + k, :, :] = part.reshape(8, 8, LANES).astype(jnp.bfloat16)


def relay(arrived):
    return pl.pallas_call(
        relay_kernel,
        out_shape=jax.ShapeDtypeStruct((8, 18, 8, LANES), jnp.bfloat16),
        in_specs=[pl.BlockSpec(memory_space=pltpu.VMEM)],
        out_specs=pl.BlockSpec(memory_space=pltpu.VMEM),
        compiler_params=pltpu.CompilerParams(vmem_limit_bytes=GRANT),
        name="relay",
    )(arrived)


SLOTS = 1024
EXTRA = 128
WIDTH = 1024


def gather_rows(in_ref, x_ref):
    for j in range(8):
        x_ref[:, j * LANES : (j + 1) * LANES] = in_ref[:, j, :, :].reshape(SLOTS, LANES)


def direct_kernel(in_ref, sums_ref, note_ref, x_ref, dense_ref, col_ref):
    me = lax.axis_index("cent")
    block = LANES
    gather_rows(in_ref, x_ref)
    tags = in_ref[:, 8, :, :].reshape(SLOTS, LANES).astype(jnp.float32)
    lane = iota((SLOTS, LANES), 1)
    mine = jnp.sum(jnp.where(lane == 64 + me, tags, 0.0), axis=1, keepdims=True)
    member4 = jnp.where(lane < 64, tags * mine * 4.0, 0.0)
    x_ref[:, WIDTH:] = member4.astype(jnp.bfloat16)
    sums_ref[...] = dot_tn(x_ref[:, WIDTH:], x_ref[:, :WIDTH])[:64] * 0.25

    col_ref[...] = jnp.zeros_like(col_ref)
    count = SLOTS // block
    for i in range(count):
        gram = dot_nt(x_ref[i * block : (i + 1) * block, :], x_ref[i * block :, :])
        kernel = jnp.exp(SHARPNESS * gram - 17.0 * SHARPNESS)
        across = kernel[:, :LANES]
        for j in range(1, count - i):
            piece = kernel[:, j * LANES : (j + 1) * LANES]
            across = across + piece
            col_ref[:, (i + j) * block : (i + j + 1) * block] += jnp.sum(
                piece.reshape(block // 8, 8, block), axis=0
            )
        dense_ref[i * block : (i + 1) * block, :] = across
    eye = iota((LANES, LANES), 0) == iota((LANES, LANES), 1)
    for k in range(count):
        line = jnp.sum(col_ref[:, k * LANES : (k + 1) * LANES], axis=0, keepdims=True)
        dense_ref[k * block : (k + 1) * block, :] += jnp.where(eye, line, 0.0)
    density = jnp.sum(dense_ref[...], axis=1, keepdims=True)
    note = jnp.where(lane == 127, tags, member4)
    for i in range(64, 67):
        part = density.astype(jnp.bfloat16).astype(jnp.float32)
        density = density - part
        note = jnp.where(lane == i, part, note)
    note_ref[...] = note.astype(jnp.bfloat16)


def direct(arrived):
    vmem = pl.BlockSpec(memory_space=pltpu.VMEM)
    return pl.pallas_call(
        direct_kernel,
        out_shape=(
            jax.ShapeDtypeStruct((64, WIDTH), jnp.float32),
            jax.ShapeDtypeStruct((SLOTS, LANES), jnp.bfloat16),
        ),
        in_specs=[vmem],
        out_specs=(vmem,) * 2,
        scratch_shapes=[
            pltpu.VMEM((SLOTS, WIDTH + LANES), jnp.bfloat16),
            pltpu.VMEM((SLOTS, LANES), jnp.float32),
            pltpu.VMEM((8, SLOTS), jnp.float32),
        ],
        compiler_params=pltpu.CompilerParams(vmem_limit_bytes=GRANT),
        cost_estimate=pl.CostEstimate(
            flops=2 * 640 * 1024 * 1152, bytes_accessed=6 * 1024 * 1024, transcendentals=640 * 1024
        ),
        name="direct",
    )(arrived)


def combine_kernel(in_ref, fix_ref, sums_ref, note_ref, *refs):
    share_refs = refs[:8]
    weight_ref, x_ref, y_ref, share_ref = refs[8:]
    me = lax.axis_index("cent")
    gather_rows(in_ref, x_ref)
    note = note_ref[...].astype(jnp.float32)
    lane = iota((SLOTS, LANES), 1)
    x_ref[:, WIDTH:] = jnp.where(lane < 64, note, 0.0).astype(jnp.bfloat16)
    density = jnp.where((lane >= 64) & (lane < 67), note, 0.0)
    half_extra = EXTRA // 2
    for h in range(2):
        rows = slice(h * half_extra, (h + 1) * half_extra)
        for j in range(8):
            y_ref[rows, j * LANES : (j + 1) * LANES] = fix_ref[:, h * 8 + j, :, :].reshape(
                half_extra, LANES
            )
    fix_tags = jnp.concatenate(
        [fix_ref[:, 16 + h, :, :].reshape(half_extra, LANES) for h in range(2)], axis=0
    ).astype(jnp.float32)
    fix_lane = iota((EXTRA, LANES), 1)
    y_ref[:, WIDTH:] = jnp.where(fix_lane < 64, fix_tags * 4.0, 0.0).astype(jnp.bfloat16)

    sums = sums_ref[...] + dot_tn(y_ref[:, WIDTH:], y_ref[:, :WIDTH])[:64] * 0.25
    inverse = lax.rsqrt(jnp.sum(sums * sums, axis=1, keepdims=True) + EPSILON)
    centroid = sums * inverse
    coarse = jnp.concatenate([centroid, jnp.zeros_like(centroid)], axis=0).astype(jnp.bfloat16)

    def share(values, first):
        for j in range(8):
            piece = values[:, j * LANES : (j + 1) * LANES].reshape(8, 8, LANES)
            for c in range(8):
                share_ref[c ^ me, first + j, :, :] = piece[c].astype(jnp.bfloat16)

    share(centroid, 0)
    cross = jnp.exp(SHARPNESS * dot_nt(x_ref[...], y_ref[...]) - 17.0 * SHARPNESS)
    own = jnp.exp(SHARPNESS * dot_nt(y_ref[...], y_ref[...]) - 17.0 * SHARPNESS)
    eye = iota((LANES, LANES), 0) == iota((LANES, LANES), 1)
    line = jnp.sum(cross, axis=0, keepdims=True)

    def weigh(rows_ref, dense):
        rows = rows_ref[:, :WIDTH]
        member = rows_ref[:, WIDTH:].astype(jnp.float32) * 0.25
        near = jnp.sum(dot_nt(rows, coarse) * member, axis=1, keepdims=True)
        valid = jnp.sum(member, axis=1, keepdims=True) > 0.5
        density = jnp.sum(dense, axis=1, keepdims=True)
        weight = jnp.where(valid, jnp.exp(1.0 - near) / jnp.where(valid, density, 1.0), 0.0)
        rounded = weight.astype(jnp.bfloat16).astype(jnp.float32)
        return weight, valid, dot_tn((member * rounded).astype(jnp.bfloat16), rows)

    weight, _, weighted = weigh(x_ref, density + cross)
    fix_weight, present, fix_weighted = weigh(y_ref, own + jnp.where(eye, line, 0.0))
    weighted = (weighted + fix_weighted)[:64]
    rep = weighted * lax.rsqrt(jnp.sum(weighted * weighted, axis=1, keepdims=True) + EPSILON)
    share(rep, 8)
    for i in range(8):
        share_refs[i][...] = share_ref[i]

    wide = jnp.broadcast_to(weight, (SLOTS, LANES)).reshape(LANES, 8, LANES)
    place = iota((LANES, 8, LANES), 2) == iota((LANES, 8, LANES), 1)
    table = jnp.sum(jnp.where(place, wide, 0.0), axis=1)
    source = jnp.sum(jnp.where(fix_lane == 96, fix_tags, 0.0), axis=1, keepdims=True)
    origin = as_bf((fix_lane.astype(jnp.float32) == source) & present)
    values = jnp.where((fix_lane >= 72) & (fix_lane < 88), fix_tags * fix_weight, 0.0)
    for _ in range(3):
        part = values.astype(jnp.bfloat16)
        values = values - part.astype(jnp.float32)
        table = table + dot_tn(origin, part)
    flag = jnp.maximum(
        jnp.max(note, axis=0, keepdims=True),
        jnp.max(fix_tags, axis=0, keepdims=True),
    )
    weight_ref[...] = jnp.where(iota((LANES, LANES), 1) == 127, flag, table)


def combine(arrived, fixed, sums, note):
    vmem = pl.BlockSpec(memory_space=pltpu.VMEM)
    share = jax.ShapeDtypeStruct((16, 8, LANES), jnp.bfloat16)
    return pl.pallas_call(
        combine_kernel,
        out_shape=(share,) * 8 + (jax.ShapeDtypeStruct((LANES, LANES), jnp.float32),),
        in_specs=[vmem] * 4,
        out_specs=(vmem,) * 9,
        scratch_shapes=[
            pltpu.VMEM((SLOTS, WIDTH + LANES), jnp.bfloat16),
            pltpu.VMEM((EXTRA, WIDTH + LANES), jnp.bfloat16),
            pltpu.VMEM((8, 16, 8, LANES), jnp.bfloat16),
        ],
        compiler_params=pltpu.CompilerParams(vmem_limit_bytes=GRANT),
        name="combine",
    )(arrived, fixed, sums, note)


def finish_kernel(*refs):
    share_refs = refs[:8]
    returned_ref, place_hbm, cent_ref, rep_ref, keep_hbm, flag_ref = refs[8:14]
    place_ref, keep_ref, mixed_ref, fetch_sem, keep_sem = refs[14:]
    fetch = pltpu.make_async_copy(place_hbm, place_ref, fetch_sem)
    fetch.start()
    me = lax.axis_index("cent")
    values = returned_ref[...]
    raised = jnp.max(jnp.where(iota((LANES, LANES), 1) == 127, values, 0.0))
    flag_ref[0, 0] = (raised > 0.5).astype(jnp.int32)
    fetch.wait()
    place = place_ref[...]
    rows = place.shape[1]
    row = iota((LANES, rows), 0)
    here = as_bf(row == (place >> 7))
    lines = jnp.zeros((LANES, rows), jnp.float32)
    for _ in range(3):
        part = values.astype(jnp.bfloat16)
        values = values - part.astype(jnp.float32)
        lines = lines + dot_tn(part, here)
    keep_ref[...] = jnp.sum(jnp.where(row == (place & 127), lines, 0.0), axis=0, keepdims=True)
    store = pltpu.make_async_copy(keep_ref, keep_hbm, keep_sem)
    store.start()
    for i in range(8):
        residue = ((me ^ i) - me) & 7
        for j in range(16):
            tile = share_refs[i][j, :, :].astype(jnp.float32)
            mixed_ref[pl.ds(j * 64 + residue, 8, stride=8), :] = tile
    for j in range(8):
        cols = slice(j * LANES, (j + 1) * LANES)
        cent_ref[:, cols] = mixed_ref[j * 64 : j * 64 + 64, :]
        rep_ref[:, cols] = mixed_ref[512 + j * 64 : 512 + j * 64 + 64, :]
    store.wait()


def finish(shared, returned, place):
    vmem = pl.BlockSpec(memory_space=pltpu.VMEM)
    return pl.pallas_call(
        finish_kernel,
        out_shape=(
            jax.ShapeDtypeStruct((64, 1024), jnp.float32),
            jax.ShapeDtypeStruct((64, 1024), jnp.float32),
            jax.ShapeDtypeStruct(place.shape, jnp.float32),
            jax.ShapeDtypeStruct((1, 1), jnp.int32),
        ),
        in_specs=[vmem] * 9 + [pl.BlockSpec(memory_space=pltpu.HBM)],
        out_specs=(
            vmem,
            vmem,
            pl.BlockSpec(memory_space=pltpu.HBM),
            pl.BlockSpec(memory_space=pltpu.SMEM),
        ),
        scratch_shapes=[
            pltpu.VMEM(place.shape, jnp.int32),
            pltpu.VMEM(place.shape, jnp.float32),
            pltpu.VMEM((1024, LANES), jnp.float32),
            pltpu.SemaphoreType.DMA,
            pltpu.SemaphoreType.DMA,
        ],
        compiler_params=pltpu.CompilerParams(vmem_limit_bytes=GRANT),
        name="finish",
    )(*shared, returned, place)


def exchange(x, axes):
    return lax.all_to_all(x, axes, split_axis=0, concat_axis=0, tiled=True)


def full_path(embeddings, a_row, owner):
    outgoing, slot = dispatch(embeddings, a_row, owner)
    centroid, representative, weight = process(exchange(outgoing, AXES))
    return (centroid, representative, collect(exchange(weight, AXES), slot))


def on_device(embeddings, assignment, owner_map):
    rows = assignment.shape[0]
    a_row = assignment.reshape(1, rows)
    owner = owner_map.reshape(-1, LANES)
    outgoing, place = pooled_dispatch(embeddings, a_row, owner)
    arrived = exchange(outgoing, AXES)
    fixed = exchange(relay(arrived), "cent")
    *share, weight = combine(arrived, fixed, *direct(arrived))
    members = lax.axis_size("cent")
    shared = [share[0]]
    for i in range(1, members):
        shared.append(lax.ppermute(share[i], "cent", [(c, c ^ i) for c in range(members)]))
    returned = exchange(weight, AXES)
    centroid, representative, keep, flag = finish(shared, returned, place)
    centroid, representative, keep = lax.switch(
        flag[0, 0],
        (lambda: (centroid, representative, keep), lambda: full_path(embeddings, a_row, owner)),
    )
    return (centroid, representative, keep.reshape(rows))


def solution(mesh):
    in_specs = (P(AXES, None), P(AXES), P())
    out_specs = (P(AXES, None), P(AXES, None), P(AXES))
    return jax.shard_map(
        on_device, mesh=mesh, in_specs=in_specs, out_specs=out_specs, check_vma=False
    )
```

```python
import functools

import jax
import jax.numpy as jnp
from jax import lax
from jax.experimental import pallas as pl
from jax.experimental.pallas import tpu as pltpu
from jax.sharding import PartitionSpec as P

EPSILON = 1e-06
SHARPNESS = 8.0
LANES = 128
AXES = ("samp", "cent")


def iota(shape, dim):
    return lax.broadcasted_iota(jnp.int32, shape, dim)


def dot_nt(a, b):
    return lax.dot_general(a, b, (((1,), (1,)), ((), ())), preferred_element_type=jnp.float32)


def dot_tn(a, b):
    return lax.dot_general(a, b, (((0,), (0,)), ((), ())), preferred_element_type=jnp.float32)


def as_bf(mask):
    return jnp.where(mask, 1.0, 0.0).astype(jnp.bfloat16)


def dispatch_kernel(emb_ref, a_ref, owner_ref, out_ref, slot_ref, unit_ref, rank_ref):
    step = pl.program_id(0)
    rows = emb_ref.shape[0]
    blocks = owner_ref.shape[0]

    @pl.when(step == 0)
    def _():
        x = emb_ref[...]
        scale = lax.rsqrt(jnp.sum(x * x, axis=1, keepdims=True) + EPSILON)
        unit_ref[...] = (x * scale).astype(jnp.bfloat16)

        a = a_ref[...]
        hi = a >> 7
        lo = a & 127
        hi_onehot = as_bf(iota((blocks, rows), 0) == hi)
        owner = owner_ref[...]
        owners = dot_tn(owner.astype(jnp.float32).astype(jnp.bfloat16), hi_onehot)
        lane = iota((LANES, rows), 0)
        dest = jnp.sum(jnp.where(lane == lo, owners, 0.0), axis=0, keepdims=True)
        before = jnp.where(owners == dest, 1.0, 0.0)
        inside = jnp.sum(jnp.where(lane < lo, before, 0.0), axis=0, keepdims=True)

        counts = jnp.zeros((LANES, blocks), jnp.float32)
        device = iota((LANES, LANES), 0)
        column = iota((LANES, blocks), 1)
        for b in range(blocks):
            match = jnp.where(owner[b : b + 1, :] == device, 1.0, 0.0)
            total = jnp.sum(match, axis=1, keepdims=True)
            counts = counts + jnp.where(column == b, total, 0.0)
        earlier = as_bf(iota((blocks, rows), 0) < hi)
        prior = jnp.dot(
            counts.astype(jnp.bfloat16), earlier, preferred_element_type=jnp.float32
        )
        dest_int = dest.astype(jnp.int32)
        here = lane == dest_int
        rank = inside + jnp.sum(jnp.where(here, prior, 0.0), axis=0, keepdims=True)
        rank_ref[...] = rank.astype(jnp.int32)

        upper = as_bf(iota((rows, rows), 0) < iota((rows, rows), 1))
        running = jnp.dot(as_bf(here), upper, preferred_element_type=jnp.float32)
        within = jnp.sum(jnp.where(here, running, 0.0), axis=0, keepdims=True)
        slot_ref[...] = dest_int * 16 + within.astype(jnp.int32)

    i = iota((256, rows), 0)
    wanted = step * 256 + ((i & 127) >> 3) * 16 + (i & 7) + (i >> 7) * 8
    pick = as_bf(slot_ref[...] == wanted)
    moved = jnp.dot(pick, unit_ref[...], preferred_element_type=jnp.float32)
    for half in range(2):
        for j in range(8):
            piece = moved[half * 128 : half * 128 + 128, j * LANES : (j + 1) * LANES]
            out_ref[:, half * 8 + j, :, :] = piece.reshape(16, 8, LANES).astype(jnp.bfloat16)
    rank = rank_ref[...]
    tag = iota((LANES, rows), 0)
    tags = dot_nt(pick[:128], as_bf(tag == rank)) + dot_nt(pick[128:], as_bf(tag == rank + 64))
    out_ref[:, 16, :, :] = tags.reshape(16, 8, LANES).astype(jnp.bfloat16)


def dispatch(embeddings, a_row, owner):
    rows, width = embeddings.shape
    devices = 128
    return pl.pallas_call(
        dispatch_kernel,
        grid=(8,),
        out_shape=(
            jax.ShapeDtypeStruct((devices, 17, 8, LANES), jnp.bfloat16),
            jax.ShapeDtypeStruct((1, rows), jnp.int32),
        ),
        in_specs=[
            pl.BlockSpec((rows, width), lambda i: (0, 0)),
            pl.BlockSpec((1, rows), lambda i: (0, 0)),
            pl.BlockSpec(owner.shape, lambda i: (0, 0)),
        ],
        out_specs=(
            pl.BlockSpec((16, 17, 8, LANES), lambda i: (i, 0, 0, 0)),
            pl.BlockSpec((1, rows), lambda i: (0, 0)),
        ),
        scratch_shapes=[
            pltpu.VMEM((rows, width), jnp.bfloat16),
            pltpu.VMEM((1, rows), jnp.int32),
        ],
        compiler_params=pltpu.CompilerParams(vmem_limit_bytes=40 * 1024 * 1024),
        name="dispatch",
    )(embeddings, a_row, owner)


def process_kernel(in_ref, cent_ref, rep_ref, weight_ref, x_ref, row_ref, col_ref):
    half = 1024
    slots = 2 * half
    width = 1024
    block = 256
    labels = in_ref[:, 16, :, :].reshape(half, LANES)
    lane = iota((LANES, LANES), 1)
    source = iota((LANES, LANES), 0)
    for h in range(2):
        for j in range(8):
            x_ref[h * half : (h + 1) * half, j * LANES : (j + 1) * LANES] = in_ref[
                :, h * 8 + j, :, :
            ].reshape(half, LANES)
        take = as_bf((source == lane + h * 64) & (lane < 64))
        x_ref[h * half : (h + 1) * half, width:] = (
            4.0 * jnp.dot(labels, take, preferred_element_type=jnp.float32)
        ).astype(jnp.bfloat16)

    member4 = x_ref[:, width:]
    sums = dot_tn(member4, x_ref[:, :width]) * 0.25
    inverse = lax.rsqrt(jnp.sum(sums * sums, axis=1, keepdims=True) + EPSILON)
    centroid = sums * inverse
    cent_ref[...] = centroid[:64]
    coarse = centroid.astype(jnp.bfloat16)
    fine = (centroid - coarse.astype(jnp.float32)).astype(jnp.bfloat16)

    row_ref[...] = jnp.zeros_like(row_ref)
    col_ref[...] = jnp.zeros_like(col_ref)
    count = slots // block
    for i in range(count):
        left = x_ref[i * block : (i + 1) * block, :]
        for j in range(i, count):
            gram = dot_nt(left, x_ref[j * block : (j + 1) * block, :])
            kernel = jnp.exp(SHARPNESS * gram - 17.0 * SHARPNESS)
            row_ref[i * block : (i + 1) * block, :] += kernel[:, :LANES] + kernel[:, LANES:]
            if j > i:
                col_ref[:, j * block : (j + 1) * block] += jnp.sum(
                    kernel.reshape(block // 8, 8, block), axis=0
                )

    eye = iota((LANES, LANES), 0) == iota((LANES, LANES), 1)
    totals = jnp.zeros((LANES, LANES), jnp.float32)
    weighted = jnp.zeros((LANES, width), jnp.float32)
    device = iota((LANES, 8, LANES), 2)
    place = iota((LANES, 8, LANES), 1)
    for h in range(2):
        rows = slice(h * half, (h + 1) * half)
        x = x_ref[rows, :width]
        scores = dot_nt(x, jnp.concatenate([coarse, fine], axis=0))
        member = x_ref[rows, width:].astype(jnp.float32) * 0.25
        near = jnp.sum((scores[:, :LANES] + scores[:, LANES:]) * member, axis=1, keepdims=True)
        valid = jnp.sum(member, axis=1, keepdims=True) > 0.5
        density = jnp.sum(row_ref[rows, :], axis=1, keepdims=True)
        across = []
        for k in range(half // LANES):
            start = h * half + k * LANES
            line = jnp.sum(col_ref[:, start : start + LANES], axis=0, keepdims=True)
            across.append(jnp.sum(jnp.where(eye, line, 0.0), axis=1, keepdims=True))
        density = density + jnp.concatenate(across, axis=0)
        weight = jnp.where(valid, jnp.exp(1.0 - near) / jnp.where(valid, density, 1.0), 0.0)
        rounded = weight.astype(jnp.bfloat16).astype(jnp.float32)
        weighted = weighted + dot_tn((member * rounded).astype(jnp.bfloat16), x)
        wide = jnp.broadcast_to(weight, (half, LANES)).reshape(LANES, 8, LANES)
        totals = totals + jnp.sum(jnp.where(device == place + h * 8, wide, 0.0), axis=1)
    weight_ref[...] = totals
    rep = weighted * lax.rsqrt(jnp.sum(weighted * weighted, axis=1, keepdims=True) + EPSILON)
    rep_ref[...] = rep[:64]


def process(arrived):
    devices = arrived.shape[0]
    return pl.pallas_call(
        process_kernel,
        out_shape=(
            jax.ShapeDtypeStruct((64, 1024), jnp.float32),
            jax.ShapeDtypeStruct((64, 1024), jnp.float32),
            jax.ShapeDtypeStruct((devices, LANES), jnp.float32),
        ),
        in_specs=[pl.BlockSpec(memory_space=pltpu.VMEM)],
        out_specs=(pl.BlockSpec(memory_space=pltpu.VMEM),) * 3,
        scratch_shapes=[
            pltpu.VMEM((2048, 1152), jnp.bfloat16),
            pltpu.VMEM((2048, LANES), jnp.float32),
            pltpu.VMEM((8, 2048), jnp.float32),
        ],
        compiler_params=pltpu.CompilerParams(vmem_limit_bytes=48 * 1024 * 1024),
        name="process",
    )(arrived)


def collect_kernel(returned_ref, slot_ref, keep_hbm, keep_ref, sem):
    slot = slot_ref[...]
    rows = slot.shape[1]
    values = returned_ref[...]
    first = values.astype(jnp.bfloat16)
    rest = values - first.astype(jnp.float32)
    second = rest.astype(jnp.bfloat16)
    third = (rest - second.astype(jnp.float32)).astype(jnp.bfloat16)
    place = iota((LANES, rows), 0)
    here = as_bf(place == (slot >> 4))
    lines = dot_tn(first, here) + dot_tn(second, here) + dot_tn(third, here)
    keep_ref[...] = jnp.sum(jnp.where(place == (slot & 15), lines, 0.0), axis=0, keepdims=True)
    store = pltpu.make_async_copy(keep_ref, keep_hbm, sem)
    store.start()
    store.wait()


def collect(returned, slot):
    return pl.pallas_call(
        collect_kernel,
        out_shape=jax.ShapeDtypeStruct(slot.shape, jnp.float32),
        in_specs=[pl.BlockSpec(memory_space=pltpu.VMEM)] * 2,
        out_specs=pl.BlockSpec(memory_space=pltpu.HBM),
        scratch_shapes=[pltpu.VMEM(slot.shape, jnp.float32), pltpu.SemaphoreType.DMA],
        name="collect",
    )(returned, slot)

POOL = 8
GRANT = 24 * 1024 * 1024


def member_of(owner, rank):
    return (owner & ~7) | ((owner + rank) & 7)


def route(a, owner, rows):
    blocks = owner.shape[0]
    hi = a >> 7
    lo = a & 127
    hi_onehot = as_bf(iota((blocks, rows), 0) == hi)
    owners = dot_tn(owner.astype(jnp.float32).astype(jnp.bfloat16), hi_onehot)
    lane = iota((LANES, rows), 0)
    dest = jnp.sum(jnp.where(lane == lo, owners, 0.0), axis=0, keepdims=True)
    before = jnp.where(owners == dest, 1.0, 0.0)
    inside = jnp.sum(jnp.where(lane < lo, before, 0.0), axis=0, keepdims=True)
    turned = jnp.transpose(owner.astype(jnp.float32))
    twice = jnp.concatenate([turned, turned - 64.0], axis=1).astype(jnp.bfloat16)
    one = jnp.ones((), jnp.bfloat16)
    nil = jnp.zeros((), jnp.bfloat16)
    lines = []
    for d in range(64):
        match = jnp.where(twice == jnp.full((), d, jnp.bfloat16), one, nil)
        parts = [match[i * 16 : (i + 1) * 16] for i in range(8)]
        while len(parts) > 1:
            parts = [parts[i] + parts[i + 1] for i in range(0, len(parts), 2)]
        lines.append(jnp.sum(parts[0].astype(jnp.float32), axis=0, keepdims=True))
    pairs = jnp.concatenate(lines, axis=0)
    counts = jnp.concatenate([pairs[:, :64], pairs[:, 64:]], axis=0)
    earlier = as_bf(iota((blocks, rows), 0) < hi)
    prior = jnp.dot(counts.astype(jnp.bfloat16), earlier, preferred_element_type=jnp.float32)
    dest_int = dest.astype(jnp.int32)
    rank = inside + jnp.sum(jnp.where(lane == dest_int, prior, 0.0), axis=0, keepdims=True)
    return dest_int, rank.astype(jnp.int32)


def pooled_kernel(
    emb_hbm, a_hbm, owner_hbm, out_ref, place_hbm,
    emb_ref, a_ref, owner_ref, unit_ref, slot_ref, tag_ref, flag_ref, back_ref, sems,
):
    rows = emb_ref.shape[0]

    first = pltpu.make_async_copy(a_hbm, a_ref, sems.at[0])
    second = pltpu.make_async_copy(owner_hbm, owner_ref, sems.at[1])
    part = rows // 8
    thirds = [
        pltpu.make_async_copy(
            emb_hbm.at[pl.ds(i * part, part)], emb_ref.at[pl.ds(i * part, part)], sems.at[4 + i]
        )
        for i in range(8)
    ]
    first.start()
    second.start()
    for copy in thirds:
        copy.start()
    first.wait()
    second.wait()
    owner, rank = route(a_ref[...], owner_ref[...], rows)
    for copy in thirds:
        copy.wait()
    x = emb_ref[...]
    scale = lax.rsqrt(jnp.sum(x * x, axis=1, keepdims=True) + EPSILON)
    unit_ref[...] = (x * scale).astype(jnp.bfloat16)
    target = member_of(owner, rank)
    lane = iota((LANES, rows), 0)
    here = lane == target
    upper = as_bf(iota((rows, rows), 0) < iota((rows, rows), 1))
    running = jnp.dot(as_bf(here), upper, preferred_element_type=jnp.float32)
    within = jnp.sum(jnp.where(here, running, 0.0), axis=0, keepdims=True)
    count = jnp.sum(jnp.where(here, 1.0, 0.0), axis=1, keepdims=True)
    start = lax.axis_index("cent")
    a_dev = iota((LANES, LANES), 0)
    b_dev = iota((LANES, LANES), 1)
    together = (a_dev >> 3) == (b_dev >> 3)
    ahead = together & (((b_dev - start) & 7) < ((a_dev - start) & 7))
    open_slot = (count <= b_dev.astype(jnp.float32)) & (b_dev < POOL)
    level = jnp.dot(as_bf(together), as_bf(open_slot), preferred_element_type=jnp.float32)
    above = jnp.dot(
        level.astype(jnp.bfloat16), as_bf(a_dev > b_dev), preferred_element_type=jnp.float32
    )
    turn = above + jnp.dot(as_bf(ahead), as_bf(open_slot), preferred_element_type=jnp.float32)
    turn = jnp.where(open_slot, turn + (a_dev >> 3).astype(jnp.float32) * 1024.0, -1.0)
    past = within > POOL - 0.5
    group = as_bf((iota((16, rows), 0) == (target >> 3)) & past)
    order = jnp.dot(group, upper, preferred_element_type=jnp.float32)
    order = jnp.sum(order * group.astype(jnp.float32), axis=0, keepdims=True)
    wanted = jnp.where(past, order + (target >> 3).astype(jnp.float32) * 1024.0, -2.0)
    found = jnp.zeros((LANES, rows), jnp.float32)
    label = lane.astype(jnp.float32) * POOL + 1.0
    for i in range(POOL):
        found = found + jnp.where(turn[:, i : i + 1] == wanted, label + i, 0.0)
    relay_slot = jnp.sum(found, axis=0, keepdims=True)
    placed = relay_slot > 0.5
    within_int = within.astype(jnp.int32)
    lost = (past & jnp.logical_not(placed)) | (within_int >= 24)
    slot = jnp.where(past, relay_slot.astype(jnp.int32) - 1, target * POOL + within_int)
    slot_ref[...] = slot
    tag = (
        (lane == ((owner & 7) * 8 + (rank >> 3)))
        | (lane == 64 + (target & 7))
        | (past & (lane == 72 + within_int - POOL))
    )
    tag_ref[...] = as_bf(tag)
    flag_ref[...] = jnp.broadcast_to(
        jnp.max(jnp.where(lost, 1.0, 0.0), axis=1, keepdims=True), (1, LANES)
    )
    lane_back = jnp.minimum(jnp.where(past, within_int + 64, within_int), 126)
    back_ref[...] = target * LANES + lane_back
    fourth = pltpu.make_async_copy(back_ref, place_hbm, sems.at[3])
    fourth.start()
    chunk = 512
    for k in range(1024 // chunk):
        pick = as_bf(slot_ref[...] == iota((chunk, rows), 0) + k * chunk)
        outs = pl.ds(k * chunk // 8, chunk // 8)
        tags = dot_nt(pick, tag_ref[...])
        tags = jnp.where(iota((chunk, LANES), 1) == 127, flag_ref[...], tags)
        out_ref[outs, 8, :, :] = tags.reshape(chunk // 8, 8, LANES).astype(jnp.bfloat16)
        for j in range(4):
            moved = jnp.dot(
                pick, unit_ref[:, j * 256 : (j + 1) * 256], preferred_element_type=jnp.float32
            )
            for h in range(2):
                piece = moved[:, h * LANES : (h + 1) * LANES]
                out_ref[outs, 2 * j + h, :, :] = piece.reshape(chunk // 8, 8, LANES).astype(
                    jnp.bfloat16
                )
    fourth.wait()


def pooled_dispatch(embeddings, a_row, owner):
    rows, width = embeddings.shape
    return pl.pallas_call(
        pooled_kernel,
        out_shape=(
            jax.ShapeDtypeStruct((LANES, 9, 8, LANES), jnp.bfloat16),
            jax.ShapeDtypeStruct((1, rows), jnp.int32),
        ),
        in_specs=[pl.BlockSpec(memory_space=pltpu.HBM)] * 3,
        out_specs=(
            pl.BlockSpec(memory_space=pltpu.VMEM),
            pl.BlockSpec(memory_space=pltpu.HBM),
        ),
        scratch_shapes=[
            pltpu.VMEM((rows, width), jnp.float32),
            pltpu.VMEM((1, rows), jnp.int32),
            pltpu.VMEM(owner.shape, jnp.int32),
            pltpu.VMEM((rows, width), jnp.bfloat16),
            pltpu.VMEM((1, rows), jnp.int32),
            pltpu.VMEM((LANES, rows), jnp.bfloat16),
            pltpu.VMEM((1, LANES), jnp.float32),
            pltpu.VMEM((1, rows), jnp.int32),
            pltpu.SemaphoreType.DMA((12,)),
        ],
        compiler_params=pltpu.CompilerParams(vmem_limit_bytes=GRANT),
        name="pooled_dispatch",
    )(embeddings, a_row, owner)


def relay_kernel(in_ref, out_ref):
    slots = 1024
    me = lax.axis_index("cent")
    tags = in_ref[:, 8, :, :].reshape(slots, LANES)
    turned = dot_nt(as_bf(iota((LANES, LANES), 0) == iota((LANES, LANES), 1)), tags)
    wrong = jnp.where(iota((8, slots), 0) == me, 0.0, turned[64:72])
    pieces = [wrong[:, k * LANES : (k + 1) * LANES] for k in range(8)]
    stacked = jnp.concatenate(pieces, axis=0)
    upper = as_bf(iota((LANES, LANES), 0) < iota((LANES, LANES), 1))
    inner = jnp.dot(stacked.astype(jnp.bfloat16), upper, preferred_element_type=jnp.float32)
    carry = jnp.zeros((8, 1), jnp.float32)
    member = iota((8, LANES), 0).astype(jnp.float32) * 8.0
    lines = []
    excess = jnp.zeros((8, LANES), jnp.float32)
    for k in range(8):
        order = inner[k * 8 : (k + 1) * 8] + carry
        excess = jnp.maximum(excess, jnp.where(order > 15.5, pieces[k], 0.0))
        goal = member + order + jnp.where(order > 7.5, 57.0, 1.0)
        goal = jnp.where((pieces[k] > 0.5) & (order < 15.5), goal, 0.0)
        lines.append(jnp.sum(goal, axis=0, keepdims=True))
        carry = carry + jnp.sum(pieces[k], axis=1, keepdims=True)
    goal = jnp.concatenate(lines, axis=1).astype(jnp.int32) - 1
    pick = as_bf(goal == iota((LANES, slots), 0))
    lane = iota((slots, LANES), 1)
    source = (iota((slots, LANES), 0) >> 3).astype(jnp.float32)
    named = jnp.where(lane == 96, source, tags.astype(jnp.float32)).astype(jnp.bfloat16)
    moved = jnp.dot(pick, named, preferred_element_type=jnp.float32)
    flag = jnp.maximum(jnp.max(turned[127:128], axis=1, keepdims=True), jnp.max(excess))
    moved = jnp.where(iota((LANES, LANES), 1) == 127, flag, moved)
    for half in range(2):
        out_ref[:, 16 + half, :, :] = (
            moved[half * 64 : half * 64 + 64].reshape(8, 8, LANES).astype(jnp.bfloat16)
        )
    for j in range(0, 8, 2):
        pair = [in_ref[:, j + k, :, :].reshape(slots, LANES) for k in range(2)]
        piece = jnp.dot(pick, jnp.concatenate(pair, axis=1), preferred_element_type=jnp.float32)
        for half in range(2):
            for k in range(2):
                part = piece[half * 64 : half * 64 + 64, k * LANES : (k + 1) * LANES]
                out_ref[:, half * 8 + j + k, :, :] = part.reshape(8, 8, LANES).astype(jnp.bfloat16)


def relay(arrived):
    return pl.pallas_call(
        relay_kernel,
        out_shape=jax.ShapeDtypeStruct((8, 18, 8, LANES), jnp.bfloat16),
        in_specs=[pl.BlockSpec(memory_space=pltpu.VMEM)],
        out_specs=pl.BlockSpec(memory_space=pltpu.VMEM),
        compiler_params=pltpu.CompilerParams(vmem_limit_bytes=GRANT),
        name="relay",
    )(arrived)


SLOTS = 1024
EXTRA = 128
WIDTH = 1024


def gather_rows(in_ref, x_ref):
    for j in range(8):
        x_ref[:, j * LANES : (j + 1) * LANES] = in_ref[:, j, :, :].reshape(SLOTS, LANES)


def direct_kernel(in_ref, sums_ref, note_ref, x_ref, dense_ref, col_ref):
    me = lax.axis_index("cent")
    block = LANES
    gather_rows(in_ref, x_ref)
    tags = in_ref[:, 8, :, :].reshape(SLOTS, LANES).astype(jnp.float32)
    lane = iota((SLOTS, LANES), 1)
    mine = jnp.sum(jnp.where(lane == 64 + me, tags, 0.0), axis=1, keepdims=True)
    member4 = jnp.where(lane < 64, tags * mine * 4.0, 0.0)
    x_ref[:, WIDTH:] = member4.astype(jnp.bfloat16)
    sums_ref[...] = dot_tn(x_ref[:, WIDTH:], x_ref[:, :WIDTH])[:64] * 0.25

    col_ref[...] = jnp.zeros_like(col_ref)
    count = SLOTS // block
    for i in range(count):
        gram = dot_nt(x_ref[i * block : (i + 1) * block, :], x_ref[i * block :, :])
        kernel = jnp.exp(SHARPNESS * gram - 17.0 * SHARPNESS)
        across = kernel[:, :LANES]
        for j in range(1, count - i):
            piece = kernel[:, j * LANES : (j + 1) * LANES]
            across = across + piece
            col_ref[:, (i + j) * block : (i + j + 1) * block] += jnp.sum(
                piece.reshape(block // 8, 8, block), axis=0
            )
        dense_ref[i * block : (i + 1) * block, :] = across
    eye = iota((LANES, LANES), 0) == iota((LANES, LANES), 1)
    for k in range(count):
        line = jnp.sum(col_ref[:, k * LANES : (k + 1) * LANES], axis=0, keepdims=True)
        dense_ref[k * block : (k + 1) * block, :] += jnp.where(eye, line, 0.0)
    density = jnp.sum(dense_ref[...], axis=1, keepdims=True)
    note = jnp.where(lane == 127, tags, member4)
    for i in range(64, 67):
        part = density.astype(jnp.bfloat16).astype(jnp.float32)
        density = density - part
        note = jnp.where(lane == i, part, note)
    note_ref[...] = note.astype(jnp.bfloat16)


def direct(arrived):
    vmem = pl.BlockSpec(memory_space=pltpu.VMEM)
    return pl.pallas_call(
        direct_kernel,
        out_shape=(
            jax.ShapeDtypeStruct((64, WIDTH), jnp.float32),
            jax.ShapeDtypeStruct((SLOTS, LANES), jnp.bfloat16),
        ),
        in_specs=[vmem],
        out_specs=(vmem,) * 2,
        scratch_shapes=[
            pltpu.VMEM((SLOTS, WIDTH + LANES), jnp.bfloat16),
            pltpu.VMEM((SLOTS, LANES), jnp.float32),
            pltpu.VMEM((8, SLOTS), jnp.float32),
        ],
        compiler_params=pltpu.CompilerParams(vmem_limit_bytes=GRANT),
        cost_estimate=pl.CostEstimate(
            flops=2 * 640 * 1024 * 1152, bytes_accessed=6 * 1024 * 1024, transcendentals=640 * 1024
        ),
        name="direct",
    )(arrived)


def combine_kernel(in_ref, fix_ref, sums_ref, note_ref, *refs):
    share_refs = refs[:8]
    weight_ref, x_ref, y_ref, share_ref = refs[8:]
    me = lax.axis_index("cent")
    gather_rows(in_ref, x_ref)
    note = note_ref[...].astype(jnp.float32)
    lane = iota((SLOTS, LANES), 1)
    x_ref[:, WIDTH:] = jnp.where(lane < 64, note, 0.0).astype(jnp.bfloat16)
    density = jnp.where((lane >= 64) & (lane < 67), note, 0.0)
    half_extra = EXTRA // 2
    for h in range(2):
        rows = slice(h * half_extra, (h + 1) * half_extra)
        for j in range(8):
            y_ref[rows, j * LANES : (j + 1) * LANES] = fix_ref[:, h * 8 + j, :, :].reshape(
                half_extra, LANES
            )
    fix_tags = jnp.concatenate(
        [fix_ref[:, 16 + h, :, :].reshape(half_extra, LANES) for h in range(2)], axis=0
    ).astype(jnp.float32)
    fix_lane = iota((EXTRA, LANES), 1)
    y_ref[:, WIDTH:] = jnp.where(fix_lane < 64, fix_tags * 4.0, 0.0).astype(jnp.bfloat16)

    sums = sums_ref[...] + dot_tn(y_ref[:, WIDTH:], y_ref[:, :WIDTH])[:64] * 0.25
    inverse = lax.rsqrt(jnp.sum(sums * sums, axis=1, keepdims=True) + EPSILON)
    centroid = sums * inverse
    coarse = jnp.concatenate([centroid, jnp.zeros_like(centroid)], axis=0).astype(jnp.bfloat16)

    def share(values, first):
        for j in range(8):
            piece = values[:, j * LANES : (j + 1) * LANES].reshape(8, 8, LANES)
            for c in range(8):
                share_ref[c ^ me, first + j, :, :] = piece[c].astype(jnp.bfloat16)

    share(centroid, 0)
    cross = jnp.exp(SHARPNESS * dot_nt(x_ref[...], y_ref[...]) - 17.0 * SHARPNESS)
    own = jnp.exp(SHARPNESS * dot_nt(y_ref[...], y_ref[...]) - 17.0 * SHARPNESS)
    eye = iota((LANES, LANES), 0) == iota((LANES, LANES), 1)
    line = jnp.sum(cross, axis=0, keepdims=True)

    def weigh(rows_ref, dense):
        rows = rows_ref[:, :WIDTH]
        member = rows_ref[:, WIDTH:].astype(jnp.float32) * 0.25
        near = jnp.sum(dot_nt(rows, coarse) * member, axis=1, keepdims=True)
        valid = jnp.sum(member, axis=1, keepdims=True) > 0.5
        density = jnp.sum(dense, axis=1, keepdims=True)
        weight = jnp.where(valid, jnp.exp(1.0 - near) / jnp.where(valid, density, 1.0), 0.0)
        rounded = weight.astype(jnp.bfloat16).astype(jnp.float32)
        return weight, valid, dot_tn((member * rounded).astype(jnp.bfloat16), rows)

    weight, _, weighted = weigh(x_ref, density + cross)
    fix_weight, present, fix_weighted = weigh(y_ref, own + jnp.where(eye, line, 0.0))
    weighted = (weighted + fix_weighted)[:64]
    rep = weighted * lax.rsqrt(jnp.sum(weighted * weighted, axis=1, keepdims=True) + EPSILON)
    share(rep, 8)
    for i in range(8):
        share_refs[i][...] = share_ref[i]

    wide = jnp.broadcast_to(weight, (SLOTS, LANES)).reshape(LANES, 8, LANES)
    place = iota((LANES, 8, LANES), 2) == iota((LANES, 8, LANES), 1)
    table = jnp.sum(jnp.where(place, wide, 0.0), axis=1)
    source = jnp.sum(jnp.where(fix_lane == 96, fix_tags, 0.0), axis=1, keepdims=True)
    origin = as_bf((fix_lane.astype(jnp.float32) == source) & present)
    values = jnp.where((fix_lane >= 72) & (fix_lane < 88), fix_tags * fix_weight, 0.0)
    for _ in range(3):
        part = values.astype(jnp.bfloat16)
        values = values - part.astype(jnp.float32)
        table = table + dot_tn(origin, part)
    flag = jnp.maximum(
        jnp.max(note, axis=0, keepdims=True),
        jnp.max(fix_tags, axis=0, keepdims=True),
    )
    weight_ref[...] = jnp.where(iota((LANES, LANES), 1) == 127, flag, table)


def combine(arrived, fixed, sums, note):
    vmem = pl.BlockSpec(memory_space=pltpu.VMEM)
    share = jax.ShapeDtypeStruct((16, 8, LANES), jnp.bfloat16)
    return pl.pallas_call(
        combine_kernel,
        out_shape=(share,) * 8 + (jax.ShapeDtypeStruct((LANES, LANES), jnp.float32),),
        in_specs=[vmem] * 4,
        out_specs=(vmem,) * 9,
        scratch_shapes=[
            pltpu.VMEM((SLOTS, WIDTH + LANES), jnp.bfloat16),
            pltpu.VMEM((EXTRA, WIDTH + LANES), jnp.bfloat16),
            pltpu.VMEM((8, 16, 8, LANES), jnp.bfloat16),
        ],
        compiler_params=pltpu.CompilerParams(vmem_limit_bytes=GRANT),
        name="combine",
    )(arrived, fixed, sums, note)


def finish_kernel(*refs):
    share_refs = refs[:8]
    returned_ref, place_hbm, cent_ref, rep_ref, keep_hbm, flag_ref = refs[8:14]
    place_ref, keep_ref, mixed_ref, fetch_sem, keep_sem = refs[14:]
    fetch = pltpu.make_async_copy(place_hbm, place_ref, fetch_sem)
    fetch.start()
    me = lax.axis_index("cent")
    values = returned_ref[...]
    raised = jnp.max(jnp.where(iota((LANES, LANES), 1) == 127, values, 0.0))
    flag_ref[0, 0] = (raised > 0.5).astype(jnp.int32)
    fetch.wait()
    place = place_ref[...]
    rows = place.shape[1]
    row = iota((LANES, rows), 0)
    here = as_bf(row == (place >> 7))
    lines = jnp.zeros((LANES, rows), jnp.float32)
    for _ in range(3):
        part = values.astype(jnp.bfloat16)
        values = values - part.astype(jnp.float32)
        lines = lines + dot_tn(part, here)
    keep_ref[...] = jnp.sum(jnp.where(row == (place & 127), lines, 0.0), axis=0, keepdims=True)
    store = pltpu.make_async_copy(keep_ref, keep_hbm, keep_sem)
    store.start()
    for i in range(8):
        residue = ((me ^ i) - me) & 7
        for j in range(16):
            tile = share_refs[i][j, :, :].astype(jnp.float32)
            mixed_ref[pl.ds(j * 64 + residue, 8, stride=8), :] = tile
    for j in range(8):
        cols = slice(j * LANES, (j + 1) * LANES)
        cent_ref[:, cols] = mixed_ref[j * 64 : j * 64 + 64, :]
        rep_ref[:, cols] = mixed_ref[512 + j * 64 : 512 + j * 64 + 64, :]
    store.wait()


def finish(shared, returned, place):
    vmem = pl.BlockSpec(memory_space=pltpu.VMEM)
    return pl.pallas_call(
        finish_kernel,
        out_shape=(
            jax.ShapeDtypeStruct((64, 1024), jnp.float32),
            jax.ShapeDtypeStruct((64, 1024), jnp.float32),
            jax.ShapeDtypeStruct(place.shape, jnp.float32),
            jax.ShapeDtypeStruct((1, 1), jnp.int32),
        ),
        in_specs=[vmem] * 9 + [pl.BlockSpec(memory_space=pltpu.HBM)],
        out_specs=(
            vmem,
            vmem,
            pl.BlockSpec(memory_space=pltpu.HBM),
            pl.BlockSpec(memory_space=pltpu.SMEM),
        ),
        scratch_shapes=[
            pltpu.VMEM(place.shape, jnp.int32),
            pltpu.VMEM(place.shape, jnp.float32),
            pltpu.VMEM((1024, LANES), jnp.float32),
            pltpu.SemaphoreType.DMA,
            pltpu.SemaphoreType.DMA,
        ],
        compiler_params=pltpu.CompilerParams(vmem_limit_bytes=GRANT),
        name="finish",
    )(*shared, returned, place)


def exchange(x, axes):
    return lax.all_to_all(x, axes, split_axis=0, concat_axis=0, tiled=True)


def full_path(embeddings, a_row, owner):
    outgoing, slot = dispatch(embeddings, a_row, owner)
    centroid, representative, weight = process(exchange(outgoing, AXES))
    keep = collect(exchange(weight, AXES), slot)
    return (centroid, representative, keep.reshape(keep.shape[1]))


def on_device(embeddings, assignment, owner_map):
    rows = assignment.shape[0]
    a_row = assignment.reshape(1, rows)
    owner = owner_map.reshape(-1, LANES)
    outgoing, place = pooled_dispatch(embeddings, a_row, owner)
    arrived = exchange(outgoing, AXES)
    fixed = exchange(relay(arrived), "cent")
    *share, weight = combine(arrived, fixed, *direct(arrived))
    members = lax.axis_size("cent")
    shared = [share[0]]
    for i in range(1, members):
        shared.append(lax.ppermute(share[i], "cent", [(c, c ^ i) for c in range(members)]))
    returned = exchange(weight, AXES)
    centroid, representative, keep, flag = finish(shared, returned, place)
    centroid, representative, keep = lax.switch(
        flag[0, 0],
        (
            lambda: (centroid, representative, keep.reshape(rows)),
            lambda: full_path(embeddings, a_row, owner),
        ),
    )
    return (centroid, representative, keep)


def solution(mesh):
    in_specs = (P(AXES, None), P(AXES), P())
    out_specs = (P(AXES, None), P(AXES, None), P(AXES))
    return jax.shard_map(
        on_device, mesh=mesh, in_specs=in_specs, out_specs=out_specs, check_vma=False
    )
```

```python
import functools

import jax
import jax.numpy as jnp
from jax import lax
from jax.experimental import pallas as pl
from jax.experimental.pallas import tpu as pltpu
from jax.sharding import PartitionSpec as P

EPSILON = 1e-06
SHARPNESS = 8.0
LANES = 128
AXES = ("samp", "cent")


def iota(shape, dim):
    return lax.broadcasted_iota(jnp.int32, shape, dim)


def dot_nt(a, b):
    return lax.dot_general(a, b, (((1,), (1,)), ((), ())), preferred_element_type=jnp.float32)


def dot_tn(a, b):
    return lax.dot_general(a, b, (((0,), (0,)), ((), ())), preferred_element_type=jnp.float32)


def as_bf(mask):
    return jnp.where(mask, 1.0, 0.0).astype(jnp.bfloat16)


def dispatch_kernel(emb_ref, a_ref, owner_ref, out_ref, slot_ref, unit_ref, rank_ref):
    step = pl.program_id(0)
    rows = emb_ref.shape[0]
    blocks = owner_ref.shape[0]

    @pl.when(step == 0)
    def _():
        x = emb_ref[...]
        scale = lax.rsqrt(jnp.sum(x * x, axis=1, keepdims=True) + EPSILON)
        unit_ref[...] = (x * scale).astype(jnp.bfloat16)

        a = a_ref[...]
        hi = a >> 7
        lo = a & 127
        hi_onehot = as_bf(iota((blocks, rows), 0) == hi)
        owner = owner_ref[...]
        owners = dot_tn(owner.astype(jnp.float32).astype(jnp.bfloat16), hi_onehot)
        lane = iota((LANES, rows), 0)
        dest = jnp.sum(jnp.where(lane == lo, owners, 0.0), axis=0, keepdims=True)
        before = jnp.where(owners == dest, 1.0, 0.0)
        inside = jnp.sum(jnp.where(lane < lo, before, 0.0), axis=0, keepdims=True)

        counts = jnp.zeros((LANES, blocks), jnp.float32)
        device = iota((LANES, LANES), 0)
        column = iota((LANES, blocks), 1)
        for b in range(blocks):
            match = jnp.where(owner[b : b + 1, :] == device, 1.0, 0.0)
            total = jnp.sum(match, axis=1, keepdims=True)
            counts = counts + jnp.where(column == b, total, 0.0)
        earlier = as_bf(iota((blocks, rows), 0) < hi)
        prior = jnp.dot(
            counts.astype(jnp.bfloat16), earlier, preferred_element_type=jnp.float32
        )
        dest_int = dest.astype(jnp.int32)
        here = lane == dest_int
        rank = inside + jnp.sum(jnp.where(here, prior, 0.0), axis=0, keepdims=True)
        rank_ref[...] = rank.astype(jnp.int32)

        upper = as_bf(iota((rows, rows), 0) < iota((rows, rows), 1))
        running = jnp.dot(as_bf(here), upper, preferred_element_type=jnp.float32)
        within = jnp.sum(jnp.where(here, running, 0.0), axis=0, keepdims=True)
        slot_ref[...] = dest_int * 16 + within.astype(jnp.int32)

    i = iota((256, rows), 0)
    wanted = step * 256 + ((i & 127) >> 3) * 16 + (i & 7) + (i >> 7) * 8
    pick = as_bf(slot_ref[...] == wanted)
    moved = jnp.dot(pick, unit_ref[...], preferred_element_type=jnp.float32)
    for half in range(2):
        for j in range(8):
            piece = moved[half * 128 : half * 128 + 128, j * LANES : (j + 1) * LANES]
            out_ref[:, half * 8 + j, :, :] = piece.reshape(16, 8, LANES).astype(jnp.bfloat16)
    rank = rank_ref[...]
    tag = iota((LANES, rows), 0)
    tags = dot_nt(pick[:128], as_bf(tag == rank)) + dot_nt(pick[128:], as_bf(tag == rank + 64))
    out_ref[:, 16, :, :] = tags.reshape(16, 8, LANES).astype(jnp.bfloat16)


def dispatch(embeddings, a_row, owner):
    rows, width = embeddings.shape
    devices = 128
    return pl.pallas_call(
        dispatch_kernel,
        grid=(8,),
        out_shape=(
            jax.ShapeDtypeStruct((devices, 17, 8, LANES), jnp.bfloat16),
            jax.ShapeDtypeStruct((1, rows), jnp.int32),
        ),
        in_specs=[
            pl.BlockSpec((rows, width), lambda i: (0, 0)),
            pl.BlockSpec((1, rows), lambda i: (0, 0)),
            pl.BlockSpec(owner.shape, lambda i: (0, 0)),
        ],
        out_specs=(
            pl.BlockSpec((16, 17, 8, LANES), lambda i: (i, 0, 0, 0)),
            pl.BlockSpec((1, rows), lambda i: (0, 0)),
        ),
        scratch_shapes=[
            pltpu.VMEM((rows, width), jnp.bfloat16),
            pltpu.VMEM((1, rows), jnp.int32),
        ],
        compiler_params=pltpu.CompilerParams(vmem_limit_bytes=40 * 1024 * 1024),
        name="dispatch",
    )(embeddings, a_row, owner)


def process_kernel(in_ref, cent_ref, rep_ref, weight_ref, x_ref, row_ref, col_ref):
    half = 1024
    slots = 2 * half
    width = 1024
    block = 256
    labels = in_ref[:, 16, :, :].reshape(half, LANES)
    lane = iota((LANES, LANES), 1)
    source = iota((LANES, LANES), 0)
    for h in range(2):
        for j in range(8):
            x_ref[h * half : (h + 1) * half, j * LANES : (j + 1) * LANES] = in_ref[
                :, h * 8 + j, :, :
            ].reshape(half, LANES)
        take = as_bf((source == lane + h * 64) & (lane < 64))
        x_ref[h * half : (h + 1) * half, width:] = (
            4.0 * jnp.dot(labels, take, preferred_element_type=jnp.float32)
        ).astype(jnp.bfloat16)

    member4 = x_ref[:, width:]
    sums = dot_tn(member4, x_ref[:, :width]) * 0.25
    inverse = lax.rsqrt(jnp.sum(sums * sums, axis=1, keepdims=True) + EPSILON)
    centroid = sums * inverse
    cent_ref[...] = centroid[:64]
    coarse = centroid.astype(jnp.bfloat16)
    fine = (centroid - coarse.astype(jnp.float32)).astype(jnp.bfloat16)

    row_ref[...] = jnp.zeros_like(row_ref)
    col_ref[...] = jnp.zeros_like(col_ref)
    count = slots // block
    for i in range(count):
        left = x_ref[i * block : (i + 1) * block, :]
        for j in range(i, count):
            gram = dot_nt(left, x_ref[j * block : (j + 1) * block, :])
            kernel = jnp.exp(SHARPNESS * gram - 17.0 * SHARPNESS)
            row_ref[i * block : (i + 1) * block, :] += kernel[:, :LANES] + kernel[:, LANES:]
            if j > i:
                col_ref[:, j * block : (j + 1) * block] += jnp.sum(
                    kernel.reshape(block // 8, 8, block), axis=0
                )

    eye = iota((LANES, LANES), 0) == iota((LANES, LANES), 1)
    totals = jnp.zeros((LANES, LANES), jnp.float32)
    weighted = jnp.zeros((LANES, width), jnp.float32)
    device = iota((LANES, 8, LANES), 2)
    place = iota((LANES, 8, LANES), 1)
    for h in range(2):
        rows = slice(h * half, (h + 1) * half)
        x = x_ref[rows, :width]
        scores = dot_nt(x, jnp.concatenate([coarse, fine], axis=0))
        member = x_ref[rows, width:].astype(jnp.float32) * 0.25
        near = jnp.sum((scores[:, :LANES] + scores[:, LANES:]) * member, axis=1, keepdims=True)
        valid = jnp.sum(member, axis=1, keepdims=True) > 0.5
        density = jnp.sum(row_ref[rows, :], axis=1, keepdims=True)
        across = []
        for k in range(half // LANES):
            start = h * half + k * LANES
            line = jnp.sum(col_ref[:, start : start + LANES], axis=0, keepdims=True)
            across.append(jnp.sum(jnp.where(eye, line, 0.0), axis=1, keepdims=True))
        density = density + jnp.concatenate(across, axis=0)
        weight = jnp.where(valid, jnp.exp(1.0 - near) / jnp.where(valid, density, 1.0), 0.0)
        rounded = weight.astype(jnp.bfloat16).astype(jnp.float32)
        weighted = weighted + dot_tn((member * rounded).astype(jnp.bfloat16), x)
        wide = jnp.broadcast_to(weight, (half, LANES)).reshape(LANES, 8, LANES)
        totals = totals + jnp.sum(jnp.where(device == place + h * 8, wide, 0.0), axis=1)
    weight_ref[...] = totals
    rep = weighted * lax.rsqrt(jnp.sum(weighted * weighted, axis=1, keepdims=True) + EPSILON)
    rep_ref[...] = rep[:64]


def process(arrived):
    devices = arrived.shape[0]
    return pl.pallas_call(
        process_kernel,
        out_shape=(
            jax.ShapeDtypeStruct((64, 1024), jnp.float32),
            jax.ShapeDtypeStruct((64, 1024), jnp.float32),
            jax.ShapeDtypeStruct((devices, LANES), jnp.float32),
        ),
        in_specs=[pl.BlockSpec(memory_space=pltpu.VMEM)],
        out_specs=(pl.BlockSpec(memory_space=pltpu.VMEM),) * 3,
        scratch_shapes=[
            pltpu.VMEM((2048, 1152), jnp.bfloat16),
            pltpu.VMEM((2048, LANES), jnp.float32),
            pltpu.VMEM((8, 2048), jnp.float32),
        ],
        compiler_params=pltpu.CompilerParams(vmem_limit_bytes=48 * 1024 * 1024),
        name="process",
    )(arrived)


def collect_kernel(returned_ref, slot_ref, keep_hbm, keep_ref, sem):
    slot = slot_ref[...]
    rows = slot.shape[1]
    values = returned_ref[...]
    first = values.astype(jnp.bfloat16)
    rest = values - first.astype(jnp.float32)
    second = rest.astype(jnp.bfloat16)
    third = (rest - second.astype(jnp.float32)).astype(jnp.bfloat16)
    place = iota((LANES, rows), 0)
    here = as_bf(place == (slot >> 4))
    lines = dot_tn(first, here) + dot_tn(second, here) + dot_tn(third, here)
    keep_ref[...] = jnp.sum(jnp.where(place == (slot & 15), lines, 0.0), axis=0, keepdims=True)
    store = pltpu.make_async_copy(keep_ref, keep_hbm, sem)
    store.start()
    store.wait()


def collect(returned, slot):
    return pl.pallas_call(
        collect_kernel,
        out_shape=jax.ShapeDtypeStruct(slot.shape, jnp.float32),
        in_specs=[pl.BlockSpec(memory_space=pltpu.VMEM)] * 2,
        out_specs=pl.BlockSpec(memory_space=pltpu.HBM),
        scratch_shapes=[pltpu.VMEM(slot.shape, jnp.float32), pltpu.SemaphoreType.DMA],
        name="collect",
    )(returned, slot)

POOL = 8
GRANT = 24 * 1024 * 1024


def member_of(owner, rank):
    return (owner & ~7) | ((owner + rank) & 7)


def route(a, owner, rows):
    blocks = owner.shape[0]
    hi = a >> 7
    lo = a & 127
    hi_onehot = as_bf(iota((blocks, rows), 0) == hi)
    owners = dot_tn(owner.astype(jnp.float32).astype(jnp.bfloat16), hi_onehot)
    lane = iota((LANES, rows), 0)
    dest = jnp.sum(jnp.where(lane == lo, owners, 0.0), axis=0, keepdims=True)
    before = jnp.where(owners == dest, 1.0, 0.0)
    inside = jnp.sum(jnp.where(lane < lo, before, 0.0), axis=0, keepdims=True)
    turned = jnp.transpose(owner.astype(jnp.float32))
    twice = jnp.concatenate([turned, turned - 64.0], axis=1).astype(jnp.bfloat16)
    one = jnp.ones((), jnp.bfloat16)
    nil = jnp.zeros((), jnp.bfloat16)
    lines = []
    for d in range(64):
        match = jnp.where(twice == jnp.full((), d, jnp.bfloat16), one, nil)
        parts = [match[i * 16 : (i + 1) * 16] for i in range(8)]
        while len(parts) > 1:
            parts = [parts[i] + parts[i + 1] for i in range(0, len(parts), 2)]
        lines.append(jnp.sum(parts[0].astype(jnp.float32), axis=0, keepdims=True))
    pairs = jnp.concatenate(lines, axis=0)
    counts = jnp.concatenate([pairs[:, :64], pairs[:, 64:]], axis=0)
    earlier = as_bf(iota((blocks, rows), 0) < hi)
    prior = jnp.dot(counts.astype(jnp.bfloat16), earlier, preferred_element_type=jnp.float32)
    dest_int = dest.astype(jnp.int32)
    rank = inside + jnp.sum(jnp.where(lane == dest_int, prior, 0.0), axis=0, keepdims=True)
    return dest_int, rank.astype(jnp.int32)


def pooled_kernel(
    emb_hbm, a_hbm, owner_hbm, out_ref, place_hbm,
    emb_ref, a_ref, owner_ref, unit_ref, slot_ref, tag_ref, flag_ref, back_ref, sems,
):
    rows = emb_ref.shape[0]

    first = pltpu.make_async_copy(a_hbm, a_ref, sems.at[0])
    second = pltpu.make_async_copy(owner_hbm, owner_ref, sems.at[1])
    part = rows // 8
    thirds = [
        pltpu.make_async_copy(
            emb_hbm.at[pl.ds(i * part, part)], emb_ref.at[pl.ds(i * part, part)], sems.at[4 + i]
        )
        for i in range(8)
    ]
    first.start()
    second.start()
    for copy in thirds:
        copy.start()
    first.wait()
    second.wait()
    owner, rank = route(a_ref[...], owner_ref[...], rows)
    for copy in thirds:
        copy.wait()
    x = emb_ref[...]
    scale = lax.rsqrt(jnp.sum(x * x, axis=1, keepdims=True) + EPSILON)
    unit_ref[...] = (x * scale).astype(jnp.bfloat16)
    target = member_of(owner, rank)
    lane = iota((LANES, rows), 0)
    here = lane == target
    upper = as_bf(iota((rows, rows), 0) < iota((rows, rows), 1))
    running = jnp.dot(as_bf(here), upper, preferred_element_type=jnp.float32)
    within = jnp.sum(jnp.where(here, running, 0.0), axis=0, keepdims=True)
    count = jnp.sum(jnp.where(here, 1.0, 0.0), axis=1, keepdims=True)
    start = lax.axis_index("cent")
    a_dev = iota((LANES, LANES), 0)
    b_dev = iota((LANES, LANES), 1)
    together = (a_dev >> 3) == (b_dev >> 3)
    ahead = together & (((b_dev - start) & 7) < ((a_dev - start) & 7))
    open_slot = (count <= b_dev.astype(jnp.float32)) & (b_dev < POOL)
    level = jnp.dot(as_bf(together), as_bf(open_slot), preferred_element_type=jnp.float32)
    above = jnp.dot(
        level.astype(jnp.bfloat16), as_bf(a_dev > b_dev), preferred_element_type=jnp.float32
    )
    turn = above + jnp.dot(as_bf(ahead), as_bf(open_slot), preferred_element_type=jnp.float32)
    turn = jnp.where(open_slot, turn + (a_dev >> 3).astype(jnp.float32) * 1024.0, -1.0)
    past = within > POOL - 0.5
    group = as_bf((iota((16, rows), 0) == (target >> 3)) & past)
    order = jnp.dot(group, upper, preferred_element_type=jnp.float32)
    order = jnp.sum(order * group.astype(jnp.float32), axis=0, keepdims=True)
    wanted = jnp.where(past, order + (target >> 3).astype(jnp.float32) * 1024.0, -2.0)
    found = jnp.zeros((LANES, rows), jnp.float32)
    label = lane.astype(jnp.float32) * POOL + 1.0
    for i in range(POOL):
        found = found + jnp.where(turn[:, i : i + 1] == wanted, label + i, 0.0)
    relay_slot = jnp.sum(found, axis=0, keepdims=True)
    placed = relay_slot > 0.5
    within_int = within.astype(jnp.int32)
    lost = (past & jnp.logical_not(placed)) | (within_int >= 24)
    slot = jnp.where(past, relay_slot.astype(jnp.int32) - 1, target * POOL + within_int)
    slot_ref[...] = slot
    tag = (
        (lane == ((owner & 7) * 8 + (rank >> 3)))
        | (lane == 64 + (target & 7))
        | (past & (lane == 72 + within_int - POOL))
    )
    tag_ref[...] = as_bf(tag)
    flag_ref[...] = jnp.broadcast_to(
        jnp.max(jnp.where(lost, 1.0, 0.0), axis=1, keepdims=True), (1, LANES)
    )
    lane_back = jnp.minimum(jnp.where(past, within_int + 64, within_int), 126)
    back_ref[...] = target * LANES + lane_back
    fourth = pltpu.make_async_copy(back_ref, place_hbm, sems.at[3])
    fourth.start()
    chunk = 512
    for k in range(1024 // chunk):
        pick = as_bf(slot_ref[...] == iota((chunk, rows), 0) + k * chunk)
        outs = pl.ds(k * chunk // 8, chunk // 8)
        tags = dot_nt(pick, tag_ref[...])
        tags = jnp.where(iota((chunk, LANES), 1) == 127, flag_ref[...], tags)
        out_ref[outs, 8, :, :] = tags.reshape(chunk // 8, 8, LANES).astype(jnp.bfloat16)
        for j in range(4):
            moved = jnp.dot(
                pick, unit_ref[:, j * 256 : (j + 1) * 256], preferred_element_type=jnp.float32
            )
            for h in range(2):
                piece = moved[:, h * LANES : (h + 1) * LANES]
                out_ref[outs, 2 * j + h, :, :] = piece.reshape(chunk // 8, 8, LANES).astype(
                    jnp.bfloat16
                )
    fourth.wait()


def pooled_dispatch(embeddings, a_row, owner):
    rows, width = embeddings.shape
    return pl.pallas_call(
        pooled_kernel,
        out_shape=(
            jax.ShapeDtypeStruct((LANES, 9, 8, LANES), jnp.bfloat16),
            jax.ShapeDtypeStruct((1, rows), jnp.int32),
        ),
        in_specs=[pl.BlockSpec(memory_space=pltpu.HBM)] * 3,
        out_specs=(
            pl.BlockSpec(memory_space=pltpu.VMEM),
            pl.BlockSpec(memory_space=pltpu.HBM),
        ),
        scratch_shapes=[
            pltpu.VMEM((rows, width), jnp.float32),
            pltpu.VMEM((1, rows), jnp.int32),
            pltpu.VMEM(owner.shape, jnp.int32),
            pltpu.VMEM((rows, width), jnp.bfloat16),
            pltpu.VMEM((1, rows), jnp.int32),
            pltpu.VMEM((LANES, rows), jnp.bfloat16),
            pltpu.VMEM((1, LANES), jnp.float32),
            pltpu.VMEM((1, rows), jnp.int32),
            pltpu.SemaphoreType.DMA((12,)),
        ],
        compiler_params=pltpu.CompilerParams(vmem_limit_bytes=GRANT),
        name="pooled_dispatch",
    )(embeddings, a_row, owner)


def relay_kernel(in_ref, out_ref):
    slots = 1024
    me = lax.axis_index("cent")
    tags = in_ref[:, 8, :, :].reshape(slots, LANES)
    turned = dot_nt(as_bf(iota((LANES, LANES), 0) == iota((LANES, LANES), 1)), tags)
    wrong = jnp.where(iota((8, slots), 0) == me, 0.0, turned[64:72])
    pieces = [wrong[:, k * LANES : (k + 1) * LANES] for k in range(8)]
    stacked = jnp.concatenate(pieces, axis=0)
    upper = as_bf(iota((LANES, LANES), 0) < iota((LANES, LANES), 1))
    inner = jnp.dot(stacked.astype(jnp.bfloat16), upper, preferred_element_type=jnp.float32)
    carry = jnp.zeros((8, 1), jnp.float32)
    member = iota((8, LANES), 0).astype(jnp.float32) * 8.0
    lines = []
    excess = jnp.zeros((8, LANES), jnp.float32)
    for k in range(8):
        order = inner[k * 8 : (k + 1) * 8] + carry
        excess = jnp.maximum(excess, jnp.where(order > 15.5, pieces[k], 0.0))
        goal = member + order + jnp.where(order > 7.5, 57.0, 1.0)
        goal = jnp.where((pieces[k] > 0.5) & (order < 15.5), goal, 0.0)
        lines.append(jnp.sum(goal, axis=0, keepdims=True))
        carry = carry + jnp.sum(pieces[k], axis=1, keepdims=True)
    goal = jnp.concatenate(lines, axis=1).astype(jnp.int32) - 1
    pick = as_bf(goal == iota((LANES, slots), 0))
    lane = iota((slots, LANES), 1)
    source = (iota((slots, LANES), 0) >> 3).astype(jnp.float32)
    named = jnp.where(lane == 96, source, tags.astype(jnp.float32)).astype(jnp.bfloat16)
    moved = jnp.dot(pick, named, preferred_element_type=jnp.float32)
    flag = jnp.maximum(jnp.max(turned[127:128], axis=1, keepdims=True), jnp.max(excess))
    moved = jnp.where(iota((LANES, LANES), 1) == 127, flag, moved)
    for half in range(2):
        out_ref[:, 16 + half, :, :] = (
            moved[half * 64 : half * 64 + 64].reshape(8, 8, LANES).astype(jnp.bfloat16)
        )
    for j in range(0, 8, 2):
        pair = [in_ref[:, j + k, :, :].reshape(slots, LANES) for k in range(2)]
        piece = jnp.dot(pick, jnp.concatenate(pair, axis=1), preferred_element_type=jnp.float32)
        for half in range(2):
            for k in range(2):
                part = piece[half * 64 : half * 64 + 64, k * LANES : (k + 1) * LANES]
                out_ref[:, half * 8 + j + k, :, :] = part.reshape(8, 8, LANES).astype(jnp.bfloat16)


def relay(arrived):
    return pl.pallas_call(
        relay_kernel,
        out_shape=jax.ShapeDtypeStruct((8, 18, 8, LANES), jnp.bfloat16),
        in_specs=[pl.BlockSpec(memory_space=pltpu.VMEM)],
        out_specs=pl.BlockSpec(memory_space=pltpu.VMEM),
        compiler_params=pltpu.CompilerParams(vmem_limit_bytes=GRANT),
        name="relay",
    )(arrived)


SLOTS = 1024
EXTRA = 128
WIDTH = 1024


def gather_rows(in_ref, x_ref):
    for j in range(8):
        x_ref[:, j * LANES : (j + 1) * LANES] = in_ref[:, j, :, :].reshape(SLOTS, LANES)


def direct_kernel(in_ref, sums_ref, note_ref, x_ref, dense_ref, col_ref):
    me = lax.axis_index("cent")
    block = LANES
    gather_rows(in_ref, x_ref)
    tags = in_ref[:, 8, :, :].reshape(SLOTS, LANES).astype(jnp.float32)
    lane = iota((SLOTS, LANES), 1)
    mine = jnp.sum(jnp.where(lane == 64 + me, tags, 0.0), axis=1, keepdims=True)
    member4 = jnp.where(lane < 64, tags * mine * 4.0, 0.0)
    x_ref[:, WIDTH:] = member4.astype(jnp.bfloat16)
    sums_ref[...] = dot_tn(x_ref[:, WIDTH:], x_ref[:, :WIDTH])[:64] * 0.25

    col_ref[...] = jnp.zeros_like(col_ref)
    count = SLOTS // block
    for i in range(count):
        gram = dot_nt(x_ref[i * block : (i + 1) * block, :], x_ref[i * block :, :])
        kernel = jnp.exp(SHARPNESS * gram - 17.0 * SHARPNESS)
        across = kernel[:, :LANES]
        for j in range(1, count - i):
            piece = kernel[:, j * LANES : (j + 1) * LANES]
            across = across + piece
            col_ref[:, (i + j) * block : (i + j + 1) * block] += jnp.sum(
                piece.reshape(block // 8, 8, block), axis=0
            )
        dense_ref[i * block : (i + 1) * block, :] = across
    eye = iota((LANES, LANES), 0) == iota((LANES, LANES), 1)
    for k in range(count):
        line = jnp.sum(col_ref[:, k * LANES : (k + 1) * LANES], axis=0, keepdims=True)
        dense_ref[k * block : (k + 1) * block, :] += jnp.where(eye, line, 0.0)
    density = jnp.sum(dense_ref[...], axis=1, keepdims=True)
    note = jnp.where(lane == 127, tags, member4)
    for i in range(64, 67):
        part = density.astype(jnp.bfloat16).astype(jnp.float32)
        density = density - part
        note = jnp.where(lane == i, part, note)
    note_ref[...] = note.astype(jnp.bfloat16)


def direct(arrived):
    vmem = pl.BlockSpec(memory_space=pltpu.VMEM)
    return pl.pallas_call(
        direct_kernel,
        out_shape=(
            jax.ShapeDtypeStruct((64, WIDTH), jnp.float32),
            jax.ShapeDtypeStruct((SLOTS, LANES), jnp.bfloat16),
        ),
        in_specs=[vmem],
        out_specs=(vmem,) * 2,
        scratch_shapes=[
            pltpu.VMEM((SLOTS, WIDTH + LANES), jnp.bfloat16),
            pltpu.VMEM((SLOTS, LANES), jnp.float32),
            pltpu.VMEM((8, SLOTS), jnp.float32),
        ],
        compiler_params=pltpu.CompilerParams(vmem_limit_bytes=GRANT),
        cost_estimate=pl.CostEstimate(
            flops=2 * 640 * 1024 * 1152, bytes_accessed=6 * 1024 * 1024, transcendentals=640 * 1024
        ),
        name="direct",
    )(arrived)


def combine_kernel(
    in_ref, fix_ref, sums_ref, note_ref, even_ref, odd_ref, weight_ref, x_ref, y_ref, share_ref
):
    me = lax.axis_index("cent")
    gather_rows(in_ref, x_ref)
    note = note_ref[...].astype(jnp.float32)
    lane = iota((SLOTS, LANES), 1)
    x_ref[:, WIDTH:] = jnp.where(lane < 64, note, 0.0).astype(jnp.bfloat16)
    density = jnp.where((lane >= 64) & (lane < 67), note, 0.0)
    half_extra = EXTRA // 2
    for h in range(2):
        rows = slice(h * half_extra, (h + 1) * half_extra)
        for j in range(8):
            y_ref[rows, j * LANES : (j + 1) * LANES] = fix_ref[:, h * 8 + j, :, :].reshape(
                half_extra, LANES
            )
    fix_tags = jnp.concatenate(
        [fix_ref[:, 16 + h, :, :].reshape(half_extra, LANES) for h in range(2)], axis=0
    ).astype(jnp.float32)
    fix_lane = iota((EXTRA, LANES), 1)
    y_ref[:, WIDTH:] = jnp.where(fix_lane < 64, fix_tags * 4.0, 0.0).astype(jnp.bfloat16)

    sums = sums_ref[...] + dot_tn(y_ref[:, WIDTH:], y_ref[:, :WIDTH])[:64] * 0.25
    inverse = lax.rsqrt(jnp.sum(sums * sums, axis=1, keepdims=True) + EPSILON)
    centroid = sums * inverse
    coarse = jnp.concatenate([centroid, jnp.zeros_like(centroid)], axis=0).astype(jnp.bfloat16)

    def share(values, first):
        for j in range(8):
            piece = values[:, j * LANES : (j + 1) * LANES].reshape(8, 8, LANES)
            for c in range(8):
                share_ref[c ^ me, first + j, :, :] = piece[c].astype(jnp.bfloat16)

    share(centroid, 0)
    cross = jnp.exp(SHARPNESS * dot_nt(x_ref[...], y_ref[...]) - 17.0 * SHARPNESS)
    own = jnp.exp(SHARPNESS * dot_nt(y_ref[...], y_ref[...]) - 17.0 * SHARPNESS)
    eye = iota((LANES, LANES), 0) == iota((LANES, LANES), 1)
    line = jnp.sum(cross, axis=0, keepdims=True)

    def weigh(rows_ref, dense):
        rows = rows_ref[:, :WIDTH]
        member = rows_ref[:, WIDTH:].astype(jnp.float32) * 0.25
        near = jnp.sum(dot_nt(rows, coarse) * member, axis=1, keepdims=True)
        valid = jnp.sum(member, axis=1, keepdims=True) > 0.5
        density = jnp.sum(dense, axis=1, keepdims=True)
        weight = jnp.where(valid, jnp.exp(1.0 - near) / jnp.where(valid, density, 1.0), 0.0)
        rounded = weight.astype(jnp.bfloat16).astype(jnp.float32)
        return weight, valid, dot_tn((member * rounded).astype(jnp.bfloat16), rows)

    weight, _, weighted = weigh(x_ref, density + cross)
    fix_weight, present, fix_weighted = weigh(y_ref, own + jnp.where(eye, line, 0.0))
    weighted = (weighted + fix_weighted)[:64]
    rep = weighted * lax.rsqrt(jnp.sum(weighted * weighted, axis=1, keepdims=True) + EPSILON)
    share(rep, 8)
    for i in range(4):
        even_ref[i] = share_ref[2 * i]
        odd_ref[i] = share_ref[2 * i + 1]

    wide = jnp.broadcast_to(weight, (SLOTS, LANES)).reshape(LANES, 8, LANES)
    place = iota((LANES, 8, LANES), 2) == iota((LANES, 8, LANES), 1)
    table = jnp.sum(jnp.where(place, wide, 0.0), axis=1)
    source = jnp.sum(jnp.where(fix_lane == 96, fix_tags, 0.0), axis=1, keepdims=True)
    origin = as_bf((fix_lane.astype(jnp.float32) == source) & present)
    values = jnp.where((fix_lane >= 72) & (fix_lane < 88), fix_tags * fix_weight, 0.0)
    for _ in range(3):
        part = values.astype(jnp.bfloat16)
        values = values - part.astype(jnp.float32)
        table = table + dot_tn(origin, part)
    flag = jnp.maximum(
        jnp.max(note, axis=0, keepdims=True),
        jnp.max(fix_tags, axis=0, keepdims=True),
    )
    weight_ref[...] = jnp.where(iota((LANES, LANES), 1) == 127, flag, table)


def combine(arrived, fixed, sums, note):
    vmem = pl.BlockSpec(memory_space=pltpu.VMEM)
    share = jax.ShapeDtypeStruct((4, 16, 8, LANES), jnp.bfloat16)
    return pl.pallas_call(
        combine_kernel,
        out_shape=(share,) * 2 + (jax.ShapeDtypeStruct((LANES, LANES), jnp.float32),),
        in_specs=[vmem] * 4,
        out_specs=(vmem,) * 3,
        scratch_shapes=[
            pltpu.VMEM((SLOTS, WIDTH + LANES), jnp.bfloat16),
            pltpu.VMEM((EXTRA, WIDTH + LANES), jnp.bfloat16),
            pltpu.VMEM((8, 16, 8, LANES), jnp.bfloat16),
        ],
        compiler_params=pltpu.CompilerParams(vmem_limit_bytes=GRANT),
        name="combine",
    )(arrived, fixed, sums, note)


def merge_kernel(even_ref, mate_ref, *out_refs):
    for i in range(3):
        out_refs[i][0] = even_ref[i + 1]
        out_refs[i][1] = mate_ref[i + 1]


def merge(even, mate):
    vmem = pl.BlockSpec(memory_space=pltpu.VMEM)
    return pl.pallas_call(
        merge_kernel,
        out_shape=(jax.ShapeDtypeStruct((2,) + even.shape[1:], even.dtype),) * 3,
        in_specs=[vmem] * 2,
        out_specs=(vmem,) * 3,
        compiler_params=pltpu.CompilerParams(vmem_limit_bytes=GRANT),
        cost_estimate=pl.CostEstimate(flops=8 * 10**9, bytes_accessed=8 * 1024 * 1024, transcendentals=0),
        name="merge",
    )(even, mate)


def finish_kernel(*refs):
    even_ref, mate_ref = refs[:2]
    returned_ref, place_hbm, cent_ref, rep_ref, keep_hbm, flag_ref = refs[5:11]
    place_ref, keep_ref, mixed_ref, fetch_sem, keep_sem = refs[11:]
    shares = [even_ref.at[0], mate_ref.at[0]]
    for ref in refs[2:5]:
        shares += [ref.at[0], ref.at[1]]
    fetch = pltpu.make_async_copy(place_hbm, place_ref, fetch_sem)
    fetch.start()
    me = lax.axis_index("cent")
    values = returned_ref[...]
    raised = jnp.max(jnp.where(iota((LANES, LANES), 1) == 127, values, 0.0))
    flag_ref[0, 0] = (raised > 0.5).astype(jnp.int32)
    fetch.wait()
    place = place_ref[...]
    rows = place.shape[1]
    row = iota((LANES, rows), 0)
    here = as_bf(row == (place >> 7))
    lines = jnp.zeros((LANES, rows), jnp.float32)
    for _ in range(3):
        part = values.astype(jnp.bfloat16)
        values = values - part.astype(jnp.float32)
        lines = lines + dot_tn(part, here)
    keep_ref[...] = jnp.sum(jnp.where(row == (place & 127), lines, 0.0), axis=0, keepdims=True)
    store = pltpu.make_async_copy(keep_ref, keep_hbm, keep_sem)
    store.start()
    for i in range(8):
        residue = ((me ^ i) - me) & 7
        for j in range(16):
            tile = shares[i][j, :, :].astype(jnp.float32)
            mixed_ref[pl.ds(j * 64 + residue, 8, stride=8), :] = tile
    for j in range(8):
        cols = slice(j * LANES, (j + 1) * LANES)
        cent_ref[:, cols] = mixed_ref[j * 64 : j * 64 + 64, :]
        rep_ref[:, cols] = mixed_ref[512 + j * 64 : 512 + j * 64 + 64, :]
    store.wait()


def finish(shared, returned, place):
    vmem = pl.BlockSpec(memory_space=pltpu.VMEM)
    return pl.pallas_call(
        finish_kernel,
        out_shape=(
            jax.ShapeDtypeStruct((64, 1024), jnp.float32),
            jax.ShapeDtypeStruct((64, 1024), jnp.float32),
            jax.ShapeDtypeStruct(place.shape, jnp.float32),
            jax.ShapeDtypeStruct((1, 1), jnp.int32),
        ),
        in_specs=[vmem] * 6 + [pl.BlockSpec(memory_space=pltpu.HBM)],
        out_specs=(
            vmem,
            vmem,
            pl.BlockSpec(memory_space=pltpu.HBM),
            pl.BlockSpec(memory_space=pltpu.SMEM),
        ),
        scratch_shapes=[
            pltpu.VMEM(place.shape, jnp.int32),
            pltpu.VMEM(place.shape, jnp.float32),
            pltpu.VMEM((1024, LANES), jnp.float32),
            pltpu.SemaphoreType.DMA,
            pltpu.SemaphoreType.DMA,
        ],
        compiler_params=pltpu.CompilerParams(vmem_limit_bytes=GRANT),
        name="finish",
    )(*shared, returned, place)


def exchange(x, axes):
    return lax.all_to_all(x, axes, split_axis=0, concat_axis=0, tiled=True)


def full_path(embeddings, a_row, owner):
    outgoing, slot = dispatch(embeddings, a_row, owner)
    centroid, representative, weight = process(exchange(outgoing, AXES))
    keep = collect(exchange(weight, AXES), slot)
    return (centroid, representative, keep.reshape(keep.shape[1]))


def on_device(embeddings, assignment, owner_map):
    rows = assignment.shape[0]
    a_row = assignment.reshape(1, rows)
    owner = owner_map.reshape(-1, LANES)
    outgoing, place = pooled_dispatch(embeddings, a_row, owner)
    arrived = exchange(outgoing, AXES)
    fixed = exchange(relay(arrived), "cent")
    even, odd, weight = combine(arrived, fixed, *direct(arrived))
    members = lax.axis_size("cent")
    pairs = lambda i: [(c, c ^ i) for c in range(members)]
    mate = lax.ppermute(odd, "cent", pairs(1))
    shared = [even, mate]
    for i, block in enumerate(merge(even, mate)):
        shared.append(lax.ppermute(block, "cent", pairs(2 * i + 2)))
    returned = exchange(weight, AXES)
    centroid, representative, keep, flag = finish(shared, returned, place)
    centroid, representative, keep = lax.switch(
        flag[0, 0],
        (
            lambda: (centroid, representative, keep.reshape(rows)),
            lambda: full_path(embeddings, a_row, owner),
        ),
    )
    return (centroid, representative, keep)


def solution(mesh):
    in_specs = (P(AXES, None), P(AXES), P())
    out_specs = (P(AXES, None), P(AXES, None), P(AXES))
    return jax.shard_map(
        on_device, mesh=mesh, in_specs=in_specs, out_specs=out_specs, check_vma=False
    )
```

```python
import functools

import jax
import jax.numpy as jnp
from jax import lax
from jax.experimental import pallas as pl
from jax.experimental.pallas import tpu as pltpu
from jax.sharding import PartitionSpec as P

EPSILON = 1e-06
SHARPNESS = 8.0
LANES = 128
AXES = ("samp", "cent")


def iota(shape, dim):
    return lax.broadcasted_iota(jnp.int32, shape, dim)


def dot_nt(a, b):
    return lax.dot_general(a, b, (((1,), (1,)), ((), ())), preferred_element_type=jnp.float32)


def dot_tn(a, b):
    return lax.dot_general(a, b, (((0,), (0,)), ((), ())), preferred_element_type=jnp.float32)


def as_bf(mask):
    return jnp.where(mask, 1.0, 0.0).astype(jnp.bfloat16)


def dispatch_kernel(emb_ref, a_ref, owner_ref, out_ref, slot_ref, unit_ref, rank_ref):
    step = pl.program_id(0)
    rows = emb_ref.shape[0]
    blocks = owner_ref.shape[0]

    @pl.when(step == 0)
    def _():
        x = emb_ref[...]
        scale = lax.rsqrt(jnp.sum(x * x, axis=1, keepdims=True) + EPSILON)
        unit_ref[...] = (x * scale).astype(jnp.bfloat16)

        a = a_ref[...]
        hi = a >> 7
        lo = a & 127
        hi_onehot = as_bf(iota((blocks, rows), 0) == hi)
        owner = owner_ref[...]
        owners = dot_tn(owner.astype(jnp.float32).astype(jnp.bfloat16), hi_onehot)
        lane = iota((LANES, rows), 0)
        dest = jnp.sum(jnp.where(lane == lo, owners, 0.0), axis=0, keepdims=True)
        before = jnp.where(owners == dest, 1.0, 0.0)
        inside = jnp.sum(jnp.where(lane < lo, before, 0.0), axis=0, keepdims=True)

        counts = jnp.zeros((LANES, blocks), jnp.float32)
        device = iota((LANES, LANES), 0)
        column = iota((LANES, blocks), 1)
        for b in range(blocks):
            match = jnp.where(owner[b : b + 1, :] == device, 1.0, 0.0)
            total = jnp.sum(match, axis=1, keepdims=True)
            counts = counts + jnp.where(column == b, total, 0.0)
        earlier = as_bf(iota((blocks, rows), 0) < hi)
        prior = jnp.dot(
            counts.astype(jnp.bfloat16), earlier, preferred_element_type=jnp.float32
        )
        dest_int = dest.astype(jnp.int32)
        here = lane == dest_int
        rank = inside + jnp.sum(jnp.where(here, prior, 0.0), axis=0, keepdims=True)
        rank_ref[...] = rank.astype(jnp.int32)

        upper = as_bf(iota((rows, rows), 0) < iota((rows, rows), 1))
        running = jnp.dot(as_bf(here), upper, preferred_element_type=jnp.float32)
        within = jnp.sum(jnp.where(here, running, 0.0), axis=0, keepdims=True)
        slot_ref[...] = dest_int * 16 + within.astype(jnp.int32)

    i = iota((256, rows), 0)
    wanted = step * 256 + ((i & 127) >> 3) * 16 + (i & 7) + (i >> 7) * 8
    pick = as_bf(slot_ref[...] == wanted)
    moved = jnp.dot(pick, unit_ref[...], preferred_element_type=jnp.float32)
    for half in range(2):
        for j in range(8):
            piece = moved[half * 128 : half * 128 + 128, j * LANES : (j + 1) * LANES]
            out_ref[:, half * 8 + j, :, :] = piece.reshape(16, 8, LANES).astype(jnp.bfloat16)
    rank = rank_ref[...]
    tag = iota((LANES, rows), 0)
    tags = dot_nt(pick[:128], as_bf(tag == rank)) + dot_nt(pick[128:], as_bf(tag == rank + 64))
    out_ref[:, 16, :, :] = tags.reshape(16, 8, LANES).astype(jnp.bfloat16)


def dispatch(embeddings, a_row, owner):
    rows, width = embeddings.shape
    devices = 128
    return pl.pallas_call(
        dispatch_kernel,
        grid=(8,),
        out_shape=(
            jax.ShapeDtypeStruct((devices, 17, 8, LANES), jnp.bfloat16),
            jax.ShapeDtypeStruct((1, rows), jnp.int32),
        ),
        in_specs=[
            pl.BlockSpec((rows, width), lambda i: (0, 0)),
            pl.BlockSpec((1, rows), lambda i: (0, 0)),
            pl.BlockSpec(owner.shape, lambda i: (0, 0)),
        ],
        out_specs=(
            pl.BlockSpec((16, 17, 8, LANES), lambda i: (i, 0, 0, 0)),
            pl.BlockSpec((1, rows), lambda i: (0, 0)),
        ),
        scratch_shapes=[
            pltpu.VMEM((rows, width), jnp.bfloat16),
            pltpu.VMEM((1, rows), jnp.int32),
        ],
        compiler_params=pltpu.CompilerParams(vmem_limit_bytes=40 * 1024 * 1024),
        name="dispatch",
    )(embeddings, a_row, owner)


def process_kernel(in_ref, cent_ref, rep_ref, weight_ref, x_ref, row_ref, col_ref):
    half = 1024
    slots = 2 * half
    width = 1024
    block = 256
    labels = in_ref[:, 16, :, :].reshape(half, LANES)
    lane = iota((LANES, LANES), 1)
    source = iota((LANES, LANES), 0)
    for h in range(2):
        for j in range(8):
            x_ref[h * half : (h + 1) * half, j * LANES : (j + 1) * LANES] = in_ref[
                :, h * 8 + j, :, :
            ].reshape(half, LANES)
        take = as_bf((source == lane + h * 64) & (lane < 64))
        x_ref[h * half : (h + 1) * half, width:] = (
            4.0 * jnp.dot(labels, take, preferred_element_type=jnp.float32)
        ).astype(jnp.bfloat16)

    member4 = x_ref[:, width:]
    sums = dot_tn(member4, x_ref[:, :width]) * 0.25
    inverse = lax.rsqrt(jnp.sum(sums * sums, axis=1, keepdims=True) + EPSILON)
    centroid = sums * inverse
    cent_ref[...] = centroid[:64]
    coarse = centroid.astype(jnp.bfloat16)
    fine = (centroid - coarse.astype(jnp.float32)).astype(jnp.bfloat16)

    row_ref[...] = jnp.zeros_like(row_ref)
    col_ref[...] = jnp.zeros_like(col_ref)
    count = slots // block
    for i in range(count):
        left = x_ref[i * block : (i + 1) * block, :]
        for j in range(i, count):
            gram = dot_nt(left, x_ref[j * block : (j + 1) * block, :])
            kernel = jnp.exp(SHARPNESS * gram - 17.0 * SHARPNESS)
            row_ref[i * block : (i + 1) * block, :] += kernel[:, :LANES] + kernel[:, LANES:]
            if j > i:
                col_ref[:, j * block : (j + 1) * block] += jnp.sum(
                    kernel.reshape(block // 8, 8, block), axis=0
                )

    eye = iota((LANES, LANES), 0) == iota((LANES, LANES), 1)
    totals = jnp.zeros((LANES, LANES), jnp.float32)
    weighted = jnp.zeros((LANES, width), jnp.float32)
    device = iota((LANES, 8, LANES), 2)
    place = iota((LANES, 8, LANES), 1)
    for h in range(2):
        rows = slice(h * half, (h + 1) * half)
        x = x_ref[rows, :width]
        scores = dot_nt(x, jnp.concatenate([coarse, fine], axis=0))
        member = x_ref[rows, width:].astype(jnp.float32) * 0.25
        near = jnp.sum((scores[:, :LANES] + scores[:, LANES:]) * member, axis=1, keepdims=True)
        valid = jnp.sum(member, axis=1, keepdims=True) > 0.5
        density = jnp.sum(row_ref[rows, :], axis=1, keepdims=True)
        across = []
        for k in range(half // LANES):
            start = h * half + k * LANES
            line = jnp.sum(col_ref[:, start : start + LANES], axis=0, keepdims=True)
            across.append(jnp.sum(jnp.where(eye, line, 0.0), axis=1, keepdims=True))
        density = density + jnp.concatenate(across, axis=0)
        weight = jnp.where(valid, jnp.exp(1.0 - near) / jnp.where(valid, density, 1.0), 0.0)
        rounded = weight.astype(jnp.bfloat16).astype(jnp.float32)
        weighted = weighted + dot_tn((member * rounded).astype(jnp.bfloat16), x)
        wide = jnp.broadcast_to(weight, (half, LANES)).reshape(LANES, 8, LANES)
        totals = totals + jnp.sum(jnp.where(device == place + h * 8, wide, 0.0), axis=1)
    weight_ref[...] = totals
    rep = weighted * lax.rsqrt(jnp.sum(weighted * weighted, axis=1, keepdims=True) + EPSILON)
    rep_ref[...] = rep[:64]


def process(arrived):
    devices = arrived.shape[0]
    return pl.pallas_call(
        process_kernel,
        out_shape=(
            jax.ShapeDtypeStruct((64, 1024), jnp.float32),
            jax.ShapeDtypeStruct((64, 1024), jnp.float32),
            jax.ShapeDtypeStruct((devices, LANES), jnp.float32),
        ),
        in_specs=[pl.BlockSpec(memory_space=pltpu.VMEM)],
        out_specs=(pl.BlockSpec(memory_space=pltpu.VMEM),) * 3,
        scratch_shapes=[
            pltpu.VMEM((2048, 1152), jnp.bfloat16),
            pltpu.VMEM((2048, LANES), jnp.float32),
            pltpu.VMEM((8, 2048), jnp.float32),
        ],
        compiler_params=pltpu.CompilerParams(vmem_limit_bytes=48 * 1024 * 1024),
        name="process",
    )(arrived)


def collect_kernel(returned_ref, slot_ref, keep_hbm, keep_ref, sem):
    slot = slot_ref[...]
    rows = slot.shape[1]
    values = returned_ref[...]
    first = values.astype(jnp.bfloat16)
    rest = values - first.astype(jnp.float32)
    second = rest.astype(jnp.bfloat16)
    third = (rest - second.astype(jnp.float32)).astype(jnp.bfloat16)
    place = iota((LANES, rows), 0)
    here = as_bf(place == (slot >> 4))
    lines = dot_tn(first, here) + dot_tn(second, here) + dot_tn(third, here)
    keep_ref[...] = jnp.sum(jnp.where(place == (slot & 15), lines, 0.0), axis=0, keepdims=True)
    store = pltpu.make_async_copy(keep_ref, keep_hbm, sem)
    store.start()
    store.wait()


def collect(returned, slot):
    return pl.pallas_call(
        collect_kernel,
        out_shape=jax.ShapeDtypeStruct(slot.shape, jnp.float32),
        in_specs=[pl.BlockSpec(memory_space=pltpu.VMEM)] * 2,
        out_specs=pl.BlockSpec(memory_space=pltpu.HBM),
        scratch_shapes=[pltpu.VMEM(slot.shape, jnp.float32), pltpu.SemaphoreType.DMA],
        name="collect",
    )(returned, slot)

POOL = 8
GRANT = 24 * 1024 * 1024


def member_of(owner, rank):
    return (owner & ~7) | ((owner + rank) & 7)


def route(a, owner, rows):
    blocks = owner.shape[0]
    hi = a >> 7
    lo = a & 127
    hi_onehot = as_bf(iota((blocks, rows), 0) == hi)
    owners = dot_tn(owner.astype(jnp.float32).astype(jnp.bfloat16), hi_onehot)
    lane = iota((LANES, rows), 0)
    dest = jnp.sum(jnp.where(lane == lo, owners, 0.0), axis=0, keepdims=True)
    before = jnp.where(owners == dest, 1.0, 0.0)
    inside = jnp.sum(jnp.where(lane < lo, before, 0.0), axis=0, keepdims=True)
    turned = jnp.transpose(owner.astype(jnp.float32))
    twice = jnp.concatenate([turned, turned - 64.0], axis=1).astype(jnp.bfloat16)
    one = jnp.ones((), jnp.bfloat16)
    nil = jnp.zeros((), jnp.bfloat16)
    lines = []
    for d in range(64):
        match = jnp.where(twice == jnp.full((), d, jnp.bfloat16), one, nil)
        parts = [match[i * 16 : (i + 1) * 16] for i in range(8)]
        while len(parts) > 1:
            parts = [parts[i] + parts[i + 1] for i in range(0, len(parts), 2)]
        lines.append(jnp.sum(parts[0].astype(jnp.float32), axis=0, keepdims=True))
    pairs = jnp.concatenate(lines, axis=0)
    counts = jnp.concatenate([pairs[:, :64], pairs[:, 64:]], axis=0)
    earlier = as_bf(iota((blocks, rows), 0) < hi)
    prior = jnp.dot(counts.astype(jnp.bfloat16), earlier, preferred_element_type=jnp.float32)
    dest_int = dest.astype(jnp.int32)
    rank = inside + jnp.sum(jnp.where(lane == dest_int, prior, 0.0), axis=0, keepdims=True)
    return dest_int, rank.astype(jnp.int32)


def pooled_kernel(
    emb_hbm, a_hbm, owner_hbm, out_ref, place_hbm,
    emb_ref, a_ref, owner_ref, unit_ref, slot_ref, tag_ref, flag_ref, back_ref, sems,
):
    rows = emb_ref.shape[0]

    first = pltpu.make_async_copy(a_hbm, a_ref, sems.at[0])
    second = pltpu.make_async_copy(owner_hbm, owner_ref, sems.at[1])
    part = rows // 8
    thirds = [
        pltpu.make_async_copy(
            emb_hbm.at[pl.ds(i * part, part)], emb_ref.at[pl.ds(i * part, part)], sems.at[4 + i]
        )
        for i in range(8)
    ]
    first.start()
    second.start()
    for copy in thirds:
        copy.start()
    first.wait()
    second.wait()
    owner, rank = route(a_ref[...], owner_ref[...], rows)
    for copy in thirds:
        copy.wait()
    x = emb_ref[...]
    scale = lax.rsqrt(jnp.sum(x * x, axis=1, keepdims=True) + EPSILON)
    unit_ref[...] = (x * scale).astype(jnp.bfloat16)
    target = member_of(owner, rank)
    lane = iota((LANES, rows), 0)
    here = lane == target
    upper = as_bf(iota((rows, rows), 0) < iota((rows, rows), 1))
    running = jnp.dot(as_bf(here), upper, preferred_element_type=jnp.float32)
    within = jnp.sum(jnp.where(here, running, 0.0), axis=0, keepdims=True)
    count = jnp.sum(jnp.where(here, 1.0, 0.0), axis=1, keepdims=True)
    start = lax.axis_index("cent")
    a_dev = iota((LANES, LANES), 0)
    b_dev = iota((LANES, LANES), 1)
    together = (a_dev >> 3) == (b_dev >> 3)
    ahead = together & (((b_dev - start) & 7) < ((a_dev - start) & 7))
    open_slot = (count <= b_dev.astype(jnp.float32)) & (b_dev < POOL)
    level = jnp.dot(as_bf(together), as_bf(open_slot), preferred_element_type=jnp.float32)
    above = jnp.dot(
        level.astype(jnp.bfloat16), as_bf(a_dev > b_dev), preferred_element_type=jnp.float32
    )
    turn = above + jnp.dot(as_bf(ahead), as_bf(open_slot), preferred_element_type=jnp.float32)
    turn = jnp.where(open_slot, turn + (a_dev >> 3).astype(jnp.float32) * 1024.0, -1.0)
    past = within > POOL - 0.5
    group = as_bf((iota((16, rows), 0) == (target >> 3)) & past)
    order = jnp.dot(group, upper, preferred_element_type=jnp.float32)
    order = jnp.sum(order * group.astype(jnp.float32), axis=0, keepdims=True)
    wanted = jnp.where(past, order + (target >> 3).astype(jnp.float32) * 1024.0, -2.0)
    found = jnp.zeros((LANES, rows), jnp.float32)
    label = lane.astype(jnp.float32) * POOL + 1.0
    for i in range(POOL):
        found = found + jnp.where(turn[:, i : i + 1] == wanted, label + i, 0.0)
    relay_slot = jnp.sum(found, axis=0, keepdims=True)
    placed = relay_slot > 0.5
    within_int = within.astype(jnp.int32)
    lost = (past & jnp.logical_not(placed)) | (within_int >= 24)
    slot = jnp.where(past, relay_slot.astype(jnp.int32) - 1, target * POOL + within_int)
    slot_ref[...] = slot
    tag = (
        (lane == ((owner & 7) * 8 + (rank >> 3)))
        | (lane == 64 + (target & 7))
        | (past & (lane == 72 + within_int - POOL))
    )
    tag_ref[...] = as_bf(tag)
    flag_ref[...] = jnp.broadcast_to(
        jnp.max(jnp.where(lost, 1.0, 0.0), axis=1, keepdims=True), (1, LANES)
    )
    lane_back = jnp.minimum(jnp.where(past, within_int + 64, within_int), 126)
    back_ref[...] = target * LANES + lane_back
    fourth = pltpu.make_async_copy(back_ref, place_hbm, sems.at[3])
    fourth.start()
    chunk = 512
    for k in range(1024 // chunk):
        pick = as_bf(slot_ref[...] == iota((chunk, rows), 0) + k * chunk)
        outs = pl.ds(k * chunk // 8, chunk // 8)
        tags = dot_nt(pick, tag_ref[...])
        tags = jnp.where(iota((chunk, LANES), 1) == 127, flag_ref[...], tags)
        out_ref[outs, 8, :, :] = tags.reshape(chunk // 8, 8, LANES).astype(jnp.bfloat16)
        for j in range(4):
            moved = jnp.dot(
                pick, unit_ref[:, j * 256 : (j + 1) * 256], preferred_element_type=jnp.float32
            )
            for h in range(2):
                piece = moved[:, h * LANES : (h + 1) * LANES]
                out_ref[outs, 2 * j + h, :, :] = piece.reshape(chunk // 8, 8, LANES).astype(
                    jnp.bfloat16
                )
    fourth.wait()


def pooled_dispatch(embeddings, a_row, owner):
    rows, width = embeddings.shape
    return pl.pallas_call(
        pooled_kernel,
        out_shape=(
            jax.ShapeDtypeStruct((LANES, 9, 8, LANES), jnp.bfloat16),
            jax.ShapeDtypeStruct((1, rows), jnp.int32),
        ),
        in_specs=[pl.BlockSpec(memory_space=pltpu.HBM)] * 3,
        out_specs=(
            pl.BlockSpec(memory_space=pltpu.VMEM),
            pl.BlockSpec(memory_space=pltpu.HBM),
        ),
        scratch_shapes=[
            pltpu.VMEM((rows, width), jnp.float32),
            pltpu.VMEM((1, rows), jnp.int32),
            pltpu.VMEM(owner.shape, jnp.int32),
            pltpu.VMEM((rows, width), jnp.bfloat16),
            pltpu.VMEM((1, rows), jnp.int32),
            pltpu.VMEM((LANES, rows), jnp.bfloat16),
            pltpu.VMEM((1, LANES), jnp.float32),
            pltpu.VMEM((1, rows), jnp.int32),
            pltpu.SemaphoreType.DMA((12,)),
        ],
        compiler_params=pltpu.CompilerParams(vmem_limit_bytes=GRANT),
        name="pooled_dispatch",
    )(embeddings, a_row, owner)


def relay_kernel(in_ref, out_hbm, out_ref, sems):
    slots = 1024
    me = lax.axis_index("cent")
    tags = in_ref[:, 8, :, :].reshape(slots, LANES)
    turned = dot_nt(as_bf(iota((LANES, LANES), 0) == iota((LANES, LANES), 1)), tags)
    wrong = jnp.where(iota((8, slots), 0) == me, 0.0, turned[64:72])
    pieces = [wrong[:, k * LANES : (k + 1) * LANES] for k in range(8)]
    stacked = jnp.concatenate(pieces, axis=0)
    upper = as_bf(iota((LANES, LANES), 0) < iota((LANES, LANES), 1))
    inner = jnp.dot(stacked.astype(jnp.bfloat16), upper, preferred_element_type=jnp.float32)
    carry = jnp.zeros((8, 1), jnp.float32)
    member = iota((8, LANES), 0).astype(jnp.float32) * 8.0
    lines = []
    excess = jnp.zeros((8, LANES), jnp.float32)
    for k in range(8):
        order = inner[k * 8 : (k + 1) * 8] + carry
        excess = jnp.maximum(excess, jnp.where(order > 15.5, pieces[k], 0.0))
        goal = member + order + jnp.where(order > 7.5, 57.0, 1.0)
        goal = jnp.where((pieces[k] > 0.5) & (order < 15.5), goal, 0.0)
        lines.append(jnp.sum(goal, axis=0, keepdims=True))
        carry = carry + jnp.sum(pieces[k], axis=1, keepdims=True)
    goal = jnp.concatenate(lines, axis=1).astype(jnp.int32) - 1
    pick = as_bf(goal == iota((LANES, slots), 0))
    lane = iota((slots, LANES), 1)
    source = (iota((slots, LANES), 0) >> 3).astype(jnp.float32)
    named = jnp.where(lane == 96, source, tags.astype(jnp.float32)).astype(jnp.bfloat16)
    moved = jnp.dot(pick, named, preferred_element_type=jnp.float32)
    flag = jnp.maximum(jnp.max(turned[127:128], axis=1, keepdims=True), jnp.max(excess))
    moved = jnp.where(iota((LANES, LANES), 1) == 127, flag, moved)
    for half in range(2):
        out_ref[:, 16 + half, :, :] = (
            moved[half * 64 : half * 64 + 64].reshape(8, 8, LANES).astype(jnp.bfloat16)
        )
    copies = []

    def leave(tile):
        part = pl.ds(tile, 2)
        copies.append(
            pltpu.make_async_copy(out_ref.at[:, part], out_hbm.at[:, part], sems.at[len(copies)])
        )
        copies[-1].start()

    leave(16)
    for j in range(0, 8, 2):
        pair = [in_ref[:, j + k, :, :].reshape(slots, LANES) for k in range(2)]
        piece = jnp.dot(pick, jnp.concatenate(pair, axis=1), preferred_element_type=jnp.float32)
        for half in range(2):
            for k in range(2):
                part = piece[half * 64 : half * 64 + 64, k * LANES : (k + 1) * LANES]
                out_ref[:, half * 8 + j + k, :, :] = part.reshape(8, 8, LANES).astype(jnp.bfloat16)
            leave(half * 8 + j)
    for copy in copies:
        copy.wait()


def relay(arrived):
    return pl.pallas_call(
        relay_kernel,
        out_shape=jax.ShapeDtypeStruct((8, 18, 8, LANES), jnp.bfloat16),
        in_specs=[pl.BlockSpec(memory_space=pltpu.VMEM)],
        out_specs=pl.BlockSpec(memory_space=pltpu.HBM),
        scratch_shapes=[
            pltpu.VMEM((8, 18, 8, LANES), jnp.bfloat16),
            pltpu.SemaphoreType.DMA((9,)),
        ],
        compiler_params=pltpu.CompilerParams(vmem_limit_bytes=GRANT),
        name="relay",
    )(arrived)


SLOTS = 1024
EXTRA = 128
WIDTH = 1024


def gather_rows(in_ref, x_ref):
    for j in range(8):
        x_ref[:, j * LANES : (j + 1) * LANES] = in_ref[:, j, :, :].reshape(SLOTS, LANES)


def direct_kernel(in_ref, sums_ref, note_ref, x_ref, dense_ref, col_ref):
    me = lax.axis_index("cent")
    block = LANES
    gather_rows(in_ref, x_ref)
    tags = in_ref[:, 8, :, :].reshape(SLOTS, LANES).astype(jnp.float32)
    lane = iota((SLOTS, LANES), 1)
    mine = jnp.sum(jnp.where(lane == 64 + me, tags, 0.0), axis=1, keepdims=True)
    member4 = jnp.where(lane < 64, tags * mine * 4.0, 0.0)
    x_ref[:, WIDTH:] = member4.astype(jnp.bfloat16)
    sums_ref[...] = dot_tn(x_ref[:, WIDTH:], x_ref[:, :WIDTH])[:64] * 0.25

    col_ref[...] = jnp.zeros_like(col_ref)
    count = SLOTS // block
    for i in range(count):
        gram = dot_nt(x_ref[i * block : (i + 1) * block, :], x_ref[i * block :, :])
        kernel = jnp.exp(SHARPNESS * gram - 17.0 * SHARPNESS)
        across = kernel[:, :LANES]
        for j in range(1, count - i):
            piece = kernel[:, j * LANES : (j + 1) * LANES]
            across = across + piece
            col_ref[:, (i + j) * block : (i + j + 1) * block] += jnp.sum(
                piece.reshape(block // 8, 8, block), axis=0
            )
        dense_ref[i * block : (i + 1) * block, :] = across
    eye = iota((LANES, LANES), 0) == iota((LANES, LANES), 1)
    for k in range(count):
        line = jnp.sum(col_ref[:, k * LANES : (k + 1) * LANES], axis=0, keepdims=True)
        dense_ref[k * block : (k + 1) * block, :] += jnp.where(eye, line, 0.0)
    density = jnp.sum(dense_ref[...], axis=1, keepdims=True)
    note = jnp.where(lane == 127, tags, member4)
    for i in range(64, 67):
        part = density.astype(jnp.bfloat16).astype(jnp.float32)
        density = density - part
        note = jnp.where(lane == i, part, note)
    note_ref[...] = note.astype(jnp.bfloat16)


def direct(arrived):
    vmem = pl.BlockSpec(memory_space=pltpu.VMEM)
    return pl.pallas_call(
        direct_kernel,
        out_shape=(
            jax.ShapeDtypeStruct((64, WIDTH), jnp.float32),
            jax.ShapeDtypeStruct((SLOTS, LANES), jnp.bfloat16),
        ),
        in_specs=[vmem],
        out_specs=(vmem,) * 2,
        scratch_shapes=[
            pltpu.VMEM((SLOTS, WIDTH + LANES), jnp.bfloat16),
            pltpu.VMEM((SLOTS, LANES), jnp.float32),
            pltpu.VMEM((8, SLOTS), jnp.float32),
        ],
        compiler_params=pltpu.CompilerParams(vmem_limit_bytes=GRANT),
        cost_estimate=pl.CostEstimate(
            flops=2 * 640 * 1024 * 1152, bytes_accessed=6 * 1024 * 1024, transcendentals=640 * 1024
        ),
        name="direct",
    )(arrived)


def combine_kernel(in_ref, fix_ref, sums_ref, note_ref, *refs):
    share_refs = refs[:8]
    weight_hbm, x_ref, y_ref, share_ref, table_ref, sem = refs[8:]
    me = lax.axis_index("cent")
    gather_rows(in_ref, x_ref)
    note = note_ref[...].astype(jnp.float32)
    lane = iota((SLOTS, LANES), 1)
    x_ref[:, WIDTH:] = jnp.where(lane < 64, note, 0.0).astype(jnp.bfloat16)
    density = jnp.where((lane >= 64) & (lane < 67), note, 0.0)
    half_extra = EXTRA // 2
    for h in range(2):
        rows = slice(h * half_extra, (h + 1) * half_extra)
        for j in range(8):
            y_ref[rows, j * LANES : (j + 1) * LANES] = fix_ref[:, h * 8 + j, :, :].reshape(
                half_extra, LANES
            )
    fix_tags = jnp.concatenate(
        [fix_ref[:, 16 + h, :, :].reshape(half_extra, LANES) for h in range(2)], axis=0
    ).astype(jnp.float32)
    fix_lane = iota((EXTRA, LANES), 1)
    y_ref[:, WIDTH:] = jnp.where(fix_lane < 64, fix_tags * 4.0, 0.0).astype(jnp.bfloat16)

    sums = sums_ref[...] + dot_tn(y_ref[:, WIDTH:], y_ref[:, :WIDTH])[:64] * 0.25
    inverse = lax.rsqrt(jnp.sum(sums * sums, axis=1, keepdims=True) + EPSILON)
    centroid = sums * inverse
    coarse = jnp.concatenate([centroid, jnp.zeros_like(centroid)], axis=0).astype(jnp.bfloat16)

    def share(values, first):
        for j in range(8):
            piece = values[:, j * LANES : (j + 1) * LANES].reshape(8, 8, LANES)
            for c in range(8):
                share_ref[c ^ me, first + j, :, :] = piece[c].astype(jnp.bfloat16)

    share(centroid, 0)
    cross = jnp.exp(SHARPNESS * dot_nt(x_ref[...], y_ref[...]) - 17.0 * SHARPNESS)
    own = jnp.exp(SHARPNESS * dot_nt(y_ref[...], y_ref[...]) - 17.0 * SHARPNESS)
    eye = iota((LANES, LANES), 0) == iota((LANES, LANES), 1)
    line = jnp.sum(cross, axis=0, keepdims=True)

    def weigh(rows_ref, dense):
        rows = rows_ref[:, :WIDTH]
        member = rows_ref[:, WIDTH:].astype(jnp.float32) * 0.25
        near = jnp.sum(dot_nt(rows, coarse) * member, axis=1, keepdims=True)
        valid = jnp.sum(member, axis=1, keepdims=True) > 0.5
        density = jnp.sum(dense, axis=1, keepdims=True)
        weight = jnp.where(valid, jnp.exp(1.0 - near) / jnp.where(valid, density, 1.0), 0.0)
        rounded = weight.astype(jnp.bfloat16).astype(jnp.float32)
        return weight, valid, (member * rounded).astype(jnp.bfloat16)

    weight, _, scaled = weigh(x_ref, density + cross)
    fix_weight, present, fix_scaled = weigh(y_ref, own + jnp.where(eye, line, 0.0))

    wide = jnp.broadcast_to(weight, (SLOTS, LANES)).reshape(LANES, 8, LANES)
    place = iota((LANES, 8, LANES), 2) == iota((LANES, 8, LANES), 1)
    table = jnp.sum(jnp.where(place, wide, 0.0), axis=1)
    source = jnp.sum(jnp.where(fix_lane == 96, fix_tags, 0.0), axis=1, keepdims=True)
    origin = as_bf((fix_lane.astype(jnp.float32) == source) & present)
    values = jnp.where((fix_lane >= 72) & (fix_lane < 88), fix_tags * fix_weight, 0.0)
    for _ in range(3):
        part = values.astype(jnp.bfloat16)
        values = values - part.astype(jnp.float32)
        table = table + dot_tn(origin, part)
    flag = jnp.maximum(
        jnp.max(note, axis=0, keepdims=True),
        jnp.max(fix_tags, axis=0, keepdims=True),
    )
    table_ref[...] = jnp.where(iota((LANES, LANES), 1) == 127, flag, table)
    leave = pltpu.make_async_copy(table_ref, weight_hbm, sem)
    leave.start()

    weighted = dot_tn(scaled, x_ref[:, :WIDTH]) + dot_tn(fix_scaled, y_ref[:, :WIDTH])
    weighted = weighted[:64]
    rep = weighted * lax.rsqrt(jnp.sum(weighted * weighted, axis=1, keepdims=True) + EPSILON)
    share(rep, 8)
    for i in range(8):
        share_refs[i][...] = share_ref[i]
    leave.wait()


def combine(arrived, fixed, sums, note):
    vmem = pl.BlockSpec(memory_space=pltpu.VMEM)
    share = jax.ShapeDtypeStruct((16, 8, LANES), jnp.bfloat16)
    return pl.pallas_call(
        combine_kernel,
        out_shape=(share,) * 8 + (jax.ShapeDtypeStruct((LANES, LANES), jnp.float32),),
        in_specs=[vmem] * 4,
        out_specs=(vmem,) * 8 + (pl.BlockSpec(memory_space=pltpu.HBM),),
        scratch_shapes=[
            pltpu.VMEM((SLOTS, WIDTH + LANES), jnp.bfloat16),
            pltpu.VMEM((EXTRA, WIDTH + LANES), jnp.bfloat16),
            pltpu.VMEM((8, 16, 8, LANES), jnp.bfloat16),
            pltpu.VMEM((LANES, LANES), jnp.float32),
            pltpu.SemaphoreType.DMA,
        ],
        compiler_params=pltpu.CompilerParams(vmem_limit_bytes=GRANT),
        name="combine",
    )(arrived, fixed, sums, note)


def finish_kernel(*refs):
    share_refs = refs[:8]
    returned_ref, place_hbm, cent_ref, rep_ref, keep_hbm, flag_ref = refs[8:14]
    place_ref, keep_ref, mixed_ref, fetch_sem, keep_sem = refs[14:]
    fetch = pltpu.make_async_copy(place_hbm, place_ref, fetch_sem)
    fetch.start()
    me = lax.axis_index("cent")
    values = returned_ref[...]
    raised = jnp.max(jnp.where(iota((LANES, LANES), 1) == 127, values, 0.0))
    flag_ref[0, 0] = (raised > 0.5).astype(jnp.int32)
    fetch.wait()
    place = place_ref[...]
    rows = place.shape[1]
    row = iota((LANES, rows), 0)
    here = as_bf(row == (place >> 7))
    lines = jnp.zeros((LANES, rows), jnp.float32)
    for _ in range(3):
        part = values.astype(jnp.bfloat16)
        values = values - part.astype(jnp.float32)
        lines = lines + dot_tn(part, here)
    keep_ref[...] = jnp.sum(jnp.where(row == (place & 127), lines, 0.0), axis=0, keepdims=True)
    store = pltpu.make_async_copy(keep_ref, keep_hbm, keep_sem)
    store.start()
    for i in range(8):
        residue = ((me ^ i) - me) & 7
        for j in range(16):
            tile = share_refs[i][j, :, :].astype(jnp.float32)
            mixed_ref[pl.ds(j * 64 + residue, 8, stride=8), :] = tile
    for j in range(8):
        cols = slice(j * LANES, (j + 1) * LANES)
        cent_ref[:, cols] = mixed_ref[j * 64 : j * 64 + 64, :]
        rep_ref[:, cols] = mixed_ref[512 + j * 64 : 512 + j * 64 + 64, :]
    store.wait()


def finish(shared, returned, place):
    vmem = pl.BlockSpec(memory_space=pltpu.VMEM)
    return pl.pallas_call(
        finish_kernel,
        out_shape=(
            jax.ShapeDtypeStruct((64, 1024), jnp.float32),
            jax.ShapeDtypeStruct((64, 1024), jnp.float32),
            jax.ShapeDtypeStruct(place.shape, jnp.float32),
            jax.ShapeDtypeStruct((1, 1), jnp.int32),
        ),
        in_specs=[vmem] * 9 + [pl.BlockSpec(memory_space=pltpu.HBM)],
        out_specs=(
            vmem,
            vmem,
            pl.BlockSpec(memory_space=pltpu.HBM),
            pl.BlockSpec(memory_space=pltpu.SMEM),
        ),
        scratch_shapes=[
            pltpu.VMEM(place.shape, jnp.int32),
            pltpu.VMEM(place.shape, jnp.float32),
            pltpu.VMEM((1024, LANES), jnp.float32),
            pltpu.SemaphoreType.DMA,
            pltpu.SemaphoreType.DMA,
        ],
        compiler_params=pltpu.CompilerParams(vmem_limit_bytes=GRANT),
        name="finish",
    )(*shared, returned, place)


def exchange(x, axes):
    return lax.all_to_all(x, axes, split_axis=0, concat_axis=0, tiled=True)


def full_path(embeddings, a_row, owner):
    outgoing, slot = dispatch(embeddings, a_row, owner)
    centroid, representative, weight = process(exchange(outgoing, AXES))
    keep = collect(exchange(weight, AXES), slot)
    return (centroid, representative, keep.reshape(keep.shape[1]))


def on_device(embeddings, assignment, owner_map):
    rows = assignment.shape[0]
    a_row = assignment.reshape(1, rows)
    owner = owner_map.reshape(-1, LANES)
    outgoing, place = pooled_dispatch(embeddings, a_row, owner)
    arrived = exchange(outgoing, AXES)
    fixed = exchange(relay(arrived), "cent")
    *share, weight = combine(arrived, fixed, *direct(arrived))
    members = lax.axis_size("cent")
    shared = [share[0]]
    for i in range(1, members):
        shared.append(lax.ppermute(share[i], "cent", [(c, c ^ i) for c in range(members)]))
    returned = exchange(weight, AXES)
    centroid, representative, keep, flag = finish(shared, returned, place)
    centroid, representative, keep = lax.switch(
        flag[0, 0],
        (
            lambda: (centroid, representative, keep.reshape(rows)),
            lambda: full_path(embeddings, a_row, owner),
        ),
    )
    return (centroid, representative, keep)


def solution(mesh):
    in_specs = (P(AXES, None), P(AXES), P())
    out_specs = (P(AXES, None), P(AXES, None), P(AXES))
    return jax.shard_map(
        on_device, mesh=mesh, in_specs=in_specs, out_specs=out_specs, check_vma=False
    )
```

```python
import functools

import jax
import jax.numpy as jnp
from jax import lax
from jax.experimental import pallas as pl
from jax.experimental.pallas import tpu as pltpu
from jax.sharding import PartitionSpec as P

EPSILON = 1e-06
SHARPNESS = 8.0
LANES = 128
AXES = ("samp", "cent")


def iota(shape, dim):
    return lax.broadcasted_iota(jnp.int32, shape, dim)


def dot_nt(a, b):
    return lax.dot_general(a, b, (((1,), (1,)), ((), ())), preferred_element_type=jnp.float32)


def dot_tn(a, b):
    return lax.dot_general(a, b, (((0,), (0,)), ((), ())), preferred_element_type=jnp.float32)


def as_bf(mask):
    return jnp.where(mask, 1.0, 0.0).astype(jnp.bfloat16)


def dispatch_kernel(emb_ref, a_ref, owner_ref, out_ref, slot_ref, unit_ref, rank_ref):
    step = pl.program_id(0)
    rows = emb_ref.shape[0]
    blocks = owner_ref.shape[0]

    @pl.when(step == 0)
    def _():
        x = emb_ref[...]
        scale = lax.rsqrt(jnp.sum(x * x, axis=1, keepdims=True) + EPSILON)
        unit_ref[...] = (x * scale).astype(jnp.bfloat16)

        a = a_ref[...]
        hi = a >> 7
        lo = a & 127
        hi_onehot = as_bf(iota((blocks, rows), 0) == hi)
        owner = owner_ref[...]
        owners = dot_tn(owner.astype(jnp.float32).astype(jnp.bfloat16), hi_onehot)
        lane = iota((LANES, rows), 0)
        dest = jnp.sum(jnp.where(lane == lo, owners, 0.0), axis=0, keepdims=True)
        before = jnp.where(owners == dest, 1.0, 0.0)
        inside = jnp.sum(jnp.where(lane < lo, before, 0.0), axis=0, keepdims=True)

        counts = jnp.zeros((LANES, blocks), jnp.float32)
        device = iota((LANES, LANES), 0)
        column = iota((LANES, blocks), 1)
        for b in range(blocks):
            match = jnp.where(owner[b : b + 1, :] == device, 1.0, 0.0)
            total = jnp.sum(match, axis=1, keepdims=True)
            counts = counts + jnp.where(column == b, total, 0.0)
        earlier = as_bf(iota((blocks, rows), 0) < hi)
        prior = jnp.dot(
            counts.astype(jnp.bfloat16), earlier, preferred_element_type=jnp.float32
        )
        dest_int = dest.astype(jnp.int32)
        here = lane == dest_int
        rank = inside + jnp.sum(jnp.where(here, prior, 0.0), axis=0, keepdims=True)
        rank_ref[...] = rank.astype(jnp.int32)

        upper = as_bf(iota((rows, rows), 0) < iota((rows, rows), 1))
        running = jnp.dot(as_bf(here), upper, preferred_element_type=jnp.float32)
        within = jnp.sum(jnp.where(here, running, 0.0), axis=0, keepdims=True)
        slot_ref[...] = dest_int * 16 + within.astype(jnp.int32)

    i = iota((256, rows), 0)
    wanted = step * 256 + ((i & 127) >> 3) * 16 + (i & 7) + (i >> 7) * 8
    pick = as_bf(slot_ref[...] == wanted)
    moved = jnp.dot(pick, unit_ref[...], preferred_element_type=jnp.float32)
    for half in range(2):
        for j in range(8):
            piece = moved[half * 128 : half * 128 + 128, j * LANES : (j + 1) * LANES]
            out_ref[:, half * 8 + j, :, :] = piece.reshape(16, 8, LANES).astype(jnp.bfloat16)
    rank = rank_ref[...]
    tag = iota((LANES, rows), 0)
    tags = dot_nt(pick[:128], as_bf(tag == rank)) + dot_nt(pick[128:], as_bf(tag == rank + 64))
    out_ref[:, 16, :, :] = tags.reshape(16, 8, LANES).astype(jnp.bfloat16)


def dispatch(embeddings, a_row, owner):
    rows, width = embeddings.shape
    devices = 128
    return pl.pallas_call(
        dispatch_kernel,
        grid=(8,),
        out_shape=(
            jax.ShapeDtypeStruct((devices, 17, 8, LANES), jnp.bfloat16),
            jax.ShapeDtypeStruct((1, rows), jnp.int32),
        ),
        in_specs=[
            pl.BlockSpec((rows, width), lambda i: (0, 0)),
            pl.BlockSpec((1, rows), lambda i: (0, 0)),
            pl.BlockSpec(owner.shape, lambda i: (0, 0)),
        ],
        out_specs=(
            pl.BlockSpec((16, 17, 8, LANES), lambda i: (i, 0, 0, 0)),
            pl.BlockSpec((1, rows), lambda i: (0, 0)),
        ),
        scratch_shapes=[
            pltpu.VMEM((rows, width), jnp.bfloat16),
            pltpu.VMEM((1, rows), jnp.int32),
        ],
        compiler_params=pltpu.CompilerParams(vmem_limit_bytes=40 * 1024 * 1024),
        name="dispatch",
    )(embeddings, a_row, owner)


def process_kernel(in_ref, cent_ref, rep_ref, weight_ref, x_ref, row_ref, col_ref):
    half = 1024
    slots = 2 * half
    width = 1024
    block = 256
    labels = in_ref[:, 16, :, :].reshape(half, LANES)
    lane = iota((LANES, LANES), 1)
    source = iota((LANES, LANES), 0)
    for h in range(2):
        for j in range(8):
            x_ref[h * half : (h + 1) * half, j * LANES : (j + 1) * LANES] = in_ref[
                :, h * 8 + j, :, :
            ].reshape(half, LANES)
        take = as_bf((source == lane + h * 64) & (lane < 64))
        x_ref[h * half : (h + 1) * half, width:] = (
            4.0 * jnp.dot(labels, take, preferred_element_type=jnp.float32)
        ).astype(jnp.bfloat16)

    member4 = x_ref[:, width:]
    sums = dot_tn(member4, x_ref[:, :width]) * 0.25
    inverse = lax.rsqrt(jnp.sum(sums * sums, axis=1, keepdims=True) + EPSILON)
    centroid = sums * inverse
    cent_ref[...] = centroid[:64]
    coarse = centroid.astype(jnp.bfloat16)
    fine = (centroid - coarse.astype(jnp.float32)).astype(jnp.bfloat16)

    row_ref[...] = jnp.zeros_like(row_ref)
    col_ref[...] = jnp.zeros_like(col_ref)
    count = slots // block
    for i in range(count):
        left = x_ref[i * block : (i + 1) * block, :]
        for j in range(i, count):
            gram = dot_nt(left, x_ref[j * block : (j + 1) * block, :])
            kernel = jnp.exp(SHARPNESS * gram - 17.0 * SHARPNESS)
            row_ref[i * block : (i + 1) * block, :] += kernel[:, :LANES] + kernel[:, LANES:]
            if j > i:
                col_ref[:, j * block : (j + 1) * block] += jnp.sum(
                    kernel.reshape(block // 8, 8, block), axis=0
                )

    eye = iota((LANES, LANES), 0) == iota((LANES, LANES), 1)
    totals = jnp.zeros((LANES, LANES), jnp.float32)
    weighted = jnp.zeros((LANES, width), jnp.float32)
    device = iota((LANES, 8, LANES), 2)
    place = iota((LANES, 8, LANES), 1)
    for h in range(2):
        rows = slice(h * half, (h + 1) * half)
        x = x_ref[rows, :width]
        scores = dot_nt(x, jnp.concatenate([coarse, fine], axis=0))
        member = x_ref[rows, width:].astype(jnp.float32) * 0.25
        near = jnp.sum((scores[:, :LANES] + scores[:, LANES:]) * member, axis=1, keepdims=True)
        valid = jnp.sum(member, axis=1, keepdims=True) > 0.5
        density = jnp.sum(row_ref[rows, :], axis=1, keepdims=True)
        across = []
        for k in range(half // LANES):
            start = h * half + k * LANES
            line = jnp.sum(col_ref[:, start : start + LANES], axis=0, keepdims=True)
            across.append(jnp.sum(jnp.where(eye, line, 0.0), axis=1, keepdims=True))
        density = density + jnp.concatenate(across, axis=0)
        weight = jnp.where(valid, jnp.exp(1.0 - near) / jnp.where(valid, density, 1.0), 0.0)
        rounded = weight.astype(jnp.bfloat16).astype(jnp.float32)
        weighted = weighted + dot_tn((member * rounded).astype(jnp.bfloat16), x)
        wide = jnp.broadcast_to(weight, (half, LANES)).reshape(LANES, 8, LANES)
        totals = totals + jnp.sum(jnp.where(device == place + h * 8, wide, 0.0), axis=1)
    weight_ref[...] = totals
    rep = weighted * lax.rsqrt(jnp.sum(weighted * weighted, axis=1, keepdims=True) + EPSILON)
    rep_ref[...] = rep[:64]


def process(arrived):
    devices = arrived.shape[0]
    return pl.pallas_call(
        process_kernel,
        out_shape=(
            jax.ShapeDtypeStruct((64, 1024), jnp.float32),
            jax.ShapeDtypeStruct((64, 1024), jnp.float32),
            jax.ShapeDtypeStruct((devices, LANES), jnp.float32),
        ),
        in_specs=[pl.BlockSpec(memory_space=pltpu.VMEM)],
        out_specs=(pl.BlockSpec(memory_space=pltpu.VMEM),) * 3,
        scratch_shapes=[
            pltpu.VMEM((2048, 1152), jnp.bfloat16),
            pltpu.VMEM((2048, LANES), jnp.float32),
            pltpu.VMEM((8, 2048), jnp.float32),
        ],
        compiler_params=pltpu.CompilerParams(vmem_limit_bytes=48 * 1024 * 1024),
        name="process",
    )(arrived)


def collect_kernel(returned_ref, slot_ref, keep_hbm, keep_ref, sem):
    slot = slot_ref[...]
    rows = slot.shape[1]
    values = returned_ref[...]
    first = values.astype(jnp.bfloat16)
    rest = values - first.astype(jnp.float32)
    second = rest.astype(jnp.bfloat16)
    third = (rest - second.astype(jnp.float32)).astype(jnp.bfloat16)
    place = iota((LANES, rows), 0)
    here = as_bf(place == (slot >> 4))
    lines = dot_tn(first, here) + dot_tn(second, here) + dot_tn(third, here)
    keep_ref[...] = jnp.sum(jnp.where(place == (slot & 15), lines, 0.0), axis=0, keepdims=True)
    store = pltpu.make_async_copy(keep_ref, keep_hbm, sem)
    store.start()
    store.wait()


def collect(returned, slot):
    return pl.pallas_call(
        collect_kernel,
        out_shape=jax.ShapeDtypeStruct(slot.shape, jnp.float32),
        in_specs=[pl.BlockSpec(memory_space=pltpu.VMEM)] * 2,
        out_specs=pl.BlockSpec(memory_space=pltpu.HBM),
        scratch_shapes=[pltpu.VMEM(slot.shape, jnp.float32), pltpu.SemaphoreType.DMA],
        name="collect",
    )(returned, slot)

POOL = 8
GRANT = 24 * 1024 * 1024


def member_of(owner, rank):
    return (owner & ~7) | ((owner + rank) & 7)


def route(a, owner, rows):
    blocks = owner.shape[0]
    hi = a >> 7
    lo = a & 127
    hi_onehot = as_bf(iota((blocks, rows), 0) == hi)
    owners = dot_tn(owner.astype(jnp.float32).astype(jnp.bfloat16), hi_onehot)
    lane = iota((LANES, rows), 0)
    dest = jnp.sum(jnp.where(lane == lo, owners, 0.0), axis=0, keepdims=True)
    before = jnp.where(owners == dest, 1.0, 0.0)
    inside = jnp.sum(jnp.where(lane < lo, before, 0.0), axis=0, keepdims=True)
    turned = jnp.transpose(owner.astype(jnp.float32))
    twice = jnp.concatenate([turned, turned - 64.0], axis=1).astype(jnp.bfloat16)
    one = jnp.ones((), jnp.bfloat16)
    nil = jnp.zeros((), jnp.bfloat16)
    lines = []
    for d in range(64):
        match = jnp.where(twice == jnp.full((), d, jnp.bfloat16), one, nil)
        parts = [match[i * 16 : (i + 1) * 16] for i in range(8)]
        while len(parts) > 1:
            parts = [parts[i] + parts[i + 1] for i in range(0, len(parts), 2)]
        lines.append(jnp.sum(parts[0].astype(jnp.float32), axis=0, keepdims=True))
    pairs = jnp.concatenate(lines, axis=0)
    counts = jnp.concatenate([pairs[:, :64], pairs[:, 64:]], axis=0)
    earlier = as_bf(iota((blocks, rows), 0) < hi)
    prior = jnp.dot(counts.astype(jnp.bfloat16), earlier, preferred_element_type=jnp.float32)
    dest_int = dest.astype(jnp.int32)
    rank = inside + jnp.sum(jnp.where(lane == dest_int, prior, 0.0), axis=0, keepdims=True)
    return dest_int, rank.astype(jnp.int32)


def pooled_kernel(
    emb_hbm, a_hbm, owner_hbm, out_ref, place_hbm,
    emb_ref, a_ref, owner_ref, unit_ref, slot_ref, tag_ref, flag_ref, back_ref, sems,
):
    rows = emb_ref.shape[0]

    first = pltpu.make_async_copy(a_hbm, a_ref, sems.at[0])
    second = pltpu.make_async_copy(owner_hbm, owner_ref, sems.at[1])
    part = rows // 8
    thirds = [
        pltpu.make_async_copy(
            emb_hbm.at[pl.ds(i * part, part)], emb_ref.at[pl.ds(i * part, part)], sems.at[4 + i]
        )
        for i in range(8)
    ]
    first.start()
    second.start()
    for copy in thirds:
        copy.start()
    first.wait()
    second.wait()
    owner, rank = route(a_ref[...], owner_ref[...], rows)
    for copy in thirds:
        copy.wait()
    x = emb_ref[...]
    scale = lax.rsqrt(jnp.sum(x * x, axis=1, keepdims=True) + EPSILON)
    unit_ref[...] = (x * scale).astype(jnp.bfloat16)
    target = member_of(owner, rank)
    lane = iota((LANES, rows), 0)
    here = lane == target
    upper = as_bf(iota((rows, rows), 0) < iota((rows, rows), 1))
    running = jnp.dot(as_bf(here), upper, preferred_element_type=jnp.float32)
    within = jnp.sum(jnp.where(here, running, 0.0), axis=0, keepdims=True)
    count = jnp.sum(jnp.where(here, 1.0, 0.0), axis=1, keepdims=True)
    start = lax.axis_index("cent")
    a_dev = iota((LANES, LANES), 0)
    b_dev = iota((LANES, LANES), 1)
    together = (a_dev >> 3) == (b_dev >> 3)
    ahead = together & (((b_dev - start) & 7) < ((a_dev - start) & 7))
    open_slot = (count <= b_dev.astype(jnp.float32)) & (b_dev < POOL)
    level = jnp.dot(as_bf(together), as_bf(open_slot), preferred_element_type=jnp.float32)
    above = jnp.dot(
        level.astype(jnp.bfloat16), as_bf(a_dev > b_dev), preferred_element_type=jnp.float32
    )
    turn = above + jnp.dot(as_bf(ahead), as_bf(open_slot), preferred_element_type=jnp.float32)
    turn = jnp.where(open_slot, turn + (a_dev >> 3).astype(jnp.float32) * 1024.0, -1.0)
    past = within > POOL - 0.5
    group = as_bf((iota((16, rows), 0) == (target >> 3)) & past)
    order = jnp.dot(group, upper, preferred_element_type=jnp.float32)
    order = jnp.sum(order * group.astype(jnp.float32), axis=0, keepdims=True)
    wanted = jnp.where(past, order + (target >> 3).astype(jnp.float32) * 1024.0, -2.0)
    found = jnp.zeros((LANES, rows), jnp.float32)
    label = lane.astype(jnp.float32) * POOL + 1.0
    for i in range(POOL):
        found = found + jnp.where(turn[:, i : i + 1] == wanted, label + i, 0.0)
    relay_slot = jnp.sum(found, axis=0, keepdims=True)
    placed = relay_slot > 0.5
    within_int = within.astype(jnp.int32)
    lost = (past & jnp.logical_not(placed)) | (within_int >= 24)
    slot = jnp.where(past, relay_slot.astype(jnp.int32) - 1, target * POOL + within_int)
    slot_ref[...] = slot
    tag = (
        (lane == ((owner & 7) * 8 + (rank >> 3)))
        | (lane == 64 + (target & 7))
        | (past & (lane == 72 + within_int - POOL))
    )
    tag_ref[...] = as_bf(tag)
    flag_ref[...] = jnp.broadcast_to(
        jnp.max(jnp.where(lost, 1.0, 0.0), axis=1, keepdims=True), (1, LANES)
    )
    lane_back = jnp.minimum(jnp.where(past, within_int + 64, within_int), 126)
    back_ref[...] = target * LANES + lane_back
    fourth = pltpu.make_async_copy(back_ref, place_hbm, sems.at[3])
    fourth.start()
    chunk = 512
    for k in range(1024 // chunk):
        pick = as_bf(slot_ref[...] == iota((chunk, rows), 0) + k * chunk)
        outs = pl.ds(k * chunk // 8, chunk // 8)
        tags = dot_nt(pick, tag_ref[...])
        tags = jnp.where(iota((chunk, LANES), 1) == 127, flag_ref[...], tags)
        out_ref[outs, 8, :, :] = tags.reshape(chunk // 8, 8, LANES).astype(jnp.bfloat16)
        for j in range(4):
            moved = jnp.dot(
                pick, unit_ref[:, j * 256 : (j + 1) * 256], preferred_element_type=jnp.float32
            )
            for h in range(2):
                piece = moved[:, h * LANES : (h + 1) * LANES]
                out_ref[outs, 2 * j + h, :, :] = piece.reshape(chunk // 8, 8, LANES).astype(
                    jnp.bfloat16
                )
    fourth.wait()


def pooled_dispatch(embeddings, a_row, owner):
    rows, width = embeddings.shape
    return pl.pallas_call(
        pooled_kernel,
        out_shape=(
            jax.ShapeDtypeStruct((LANES, 9, 8, LANES), jnp.bfloat16),
            jax.ShapeDtypeStruct((1, rows), jnp.int32),
        ),
        in_specs=[pl.BlockSpec(memory_space=pltpu.HBM)] * 3,
        out_specs=(
            pl.BlockSpec(memory_space=pltpu.VMEM),
            pl.BlockSpec(memory_space=pltpu.HBM),
        ),
        scratch_shapes=[
            pltpu.VMEM((rows, width), jnp.float32),
            pltpu.VMEM((1, rows), jnp.int32),
            pltpu.VMEM(owner.shape, jnp.int32),
            pltpu.VMEM((rows, width), jnp.bfloat16),
            pltpu.VMEM((1, rows), jnp.int32),
            pltpu.VMEM((LANES, rows), jnp.bfloat16),
            pltpu.VMEM((1, LANES), jnp.float32),
            pltpu.VMEM((1, rows), jnp.int32),
            pltpu.SemaphoreType.DMA((12,)),
        ],
        compiler_params=pltpu.CompilerParams(vmem_limit_bytes=GRANT),
        name="pooled_dispatch",
    )(embeddings, a_row, owner)


def relay_kernel(in_ref, out_hbm, out_ref, sems):
    slots = 1024
    me = lax.axis_index("cent")
    tags = in_ref[:, 8, :, :].reshape(slots, LANES)
    turned = dot_nt(as_bf(iota((LANES, LANES), 0) == iota((LANES, LANES), 1)), tags)
    wrong = jnp.where(iota((8, slots), 0) == me, 0.0, turned[64:72])
    pieces = [wrong[:, k * LANES : (k + 1) * LANES] for k in range(8)]
    stacked = jnp.concatenate(pieces, axis=0)
    upper = as_bf(iota((LANES, LANES), 0) < iota((LANES, LANES), 1))
    inner = jnp.dot(stacked.astype(jnp.bfloat16), upper, preferred_element_type=jnp.float32)
    carry = jnp.zeros((8, 1), jnp.float32)
    member = iota((8, LANES), 0).astype(jnp.float32) * 8.0
    lines = []
    excess = jnp.zeros((8, LANES), jnp.float32)
    for k in range(8):
        order = inner[k * 8 : (k + 1) * 8] + carry
        excess = jnp.maximum(excess, jnp.where(order > 15.5, pieces[k], 0.0))
        goal = member + order + jnp.where(order > 7.5, 57.0, 1.0)
        goal = jnp.where((pieces[k] > 0.5) & (order < 15.5), goal, 0.0)
        lines.append(jnp.sum(goal, axis=0, keepdims=True))
        carry = carry + jnp.sum(pieces[k], axis=1, keepdims=True)
    goal = jnp.concatenate(lines, axis=1).astype(jnp.int32) - 1
    pick = as_bf(goal == iota((LANES, slots), 0))
    lane = iota((slots, LANES), 1)
    source = (iota((slots, LANES), 0) >> 3).astype(jnp.float32)
    named = jnp.where(lane == 96, source, tags.astype(jnp.float32)).astype(jnp.bfloat16)
    moved = jnp.dot(pick, named, preferred_element_type=jnp.float32)
    flag = jnp.maximum(jnp.max(turned[127:128], axis=1, keepdims=True), jnp.max(excess))
    moved = jnp.where(iota((LANES, LANES), 1) == 127, flag, moved)
    for half in range(2):
        out_ref[:, 16 + half, :, :] = (
            moved[half * 64 : half * 64 + 64].reshape(8, 8, LANES).astype(jnp.bfloat16)
        )
    copies = []

    def leave(tile):
        part = pl.ds(tile, 2)
        copies.append(
            pltpu.make_async_copy(out_ref.at[:, part], out_hbm.at[:, part], sems.at[len(copies)])
        )
        copies[-1].start()

    leave(16)
    for j in range(0, 8, 2):
        pair = [in_ref[:, j + k, :, :].reshape(slots, LANES) for k in range(2)]
        piece = jnp.dot(pick, jnp.concatenate(pair, axis=1), preferred_element_type=jnp.float32)
        for half in range(2):
            for k in range(2):
                part = piece[half * 64 : half * 64 + 64, k * LANES : (k + 1) * LANES]
                out_ref[:, half * 8 + j + k, :, :] = part.reshape(8, 8, LANES).astype(jnp.bfloat16)
            leave(half * 8 + j)
    for copy in copies:
        copy.wait()


def relay(arrived):
    return pl.pallas_call(
        relay_kernel,
        out_shape=jax.ShapeDtypeStruct((8, 18, 8, LANES), jnp.bfloat16),
        in_specs=[pl.BlockSpec(memory_space=pltpu.VMEM)],
        out_specs=pl.BlockSpec(memory_space=pltpu.HBM),
        scratch_shapes=[
            pltpu.VMEM((8, 18, 8, LANES), jnp.bfloat16),
            pltpu.SemaphoreType.DMA((9,)),
        ],
        compiler_params=pltpu.CompilerParams(vmem_limit_bytes=GRANT),
        name="relay",
    )(arrived)


SLOTS = 1024
EXTRA = 128
WIDTH = 1024


def gather_rows(in_ref, x_ref):
    for j in range(8):
        x_ref[:, j * LANES : (j + 1) * LANES] = in_ref[:, j, :, :].reshape(SLOTS, LANES)


def direct_kernel(in_ref, sums_ref, note_ref, x_ref, dense_ref, col_ref):
    me = lax.axis_index("cent")
    block = LANES
    gather_rows(in_ref, x_ref)
    tags = in_ref[:, 8, :, :].reshape(SLOTS, LANES).astype(jnp.float32)
    lane = iota((SLOTS, LANES), 1)
    mine = jnp.sum(jnp.where(lane == 64 + me, tags, 0.0), axis=1, keepdims=True)
    member4 = jnp.where(lane < 64, tags * mine * 4.0, 0.0)
    x_ref[:, WIDTH:] = member4.astype(jnp.bfloat16)
    sums_ref[...] = dot_tn(x_ref[:, WIDTH:], x_ref[:, :WIDTH])[:64] * 0.25

    col_ref[...] = jnp.zeros_like(col_ref)
    count = SLOTS // block
    for i in range(count):
        gram = dot_nt(x_ref[i * block : (i + 1) * block, :], x_ref[i * block :, :])
        kernel = jnp.exp(SHARPNESS * gram - 17.0 * SHARPNESS)
        across = kernel[:, :LANES]
        for j in range(1, count - i):
            piece = kernel[:, j * LANES : (j + 1) * LANES]
            across = across + piece
            col_ref[:, (i + j) * block : (i + j + 1) * block] += jnp.sum(
                piece.reshape(block // 8, 8, block), axis=0
            )
        dense_ref[i * block : (i + 1) * block, :] = across
    eye = iota((LANES, LANES), 0) == iota((LANES, LANES), 1)
    for k in range(count):
        line = jnp.sum(col_ref[:, k * LANES : (k + 1) * LANES], axis=0, keepdims=True)
        dense_ref[k * block : (k + 1) * block, :] += jnp.where(eye, line, 0.0)
    density = jnp.sum(dense_ref[...], axis=1, keepdims=True)
    note = jnp.where(lane == 127, tags, member4)
    for i in range(64, 67):
        part = density.astype(jnp.bfloat16).astype(jnp.float32)
        density = density - part
        note = jnp.where(lane == i, part, note)
    note_ref[...] = note.astype(jnp.bfloat16)


def direct(arrived):
    vmem = pl.BlockSpec(memory_space=pltpu.VMEM)
    return pl.pallas_call(
        direct_kernel,
        out_shape=(
            jax.ShapeDtypeStruct((64, WIDTH), jnp.float32),
            jax.ShapeDtypeStruct((SLOTS, LANES), jnp.bfloat16),
        ),
        in_specs=[vmem],
        out_specs=(vmem,) * 2,
        scratch_shapes=[
            pltpu.VMEM((SLOTS, WIDTH + LANES), jnp.bfloat16),
            pltpu.VMEM((SLOTS, LANES), jnp.float32),
            pltpu.VMEM((8, SLOTS), jnp.float32),
        ],
        compiler_params=pltpu.CompilerParams(vmem_limit_bytes=GRANT),
        cost_estimate=pl.CostEstimate(
            flops=2 * 640 * 1024 * 1152, bytes_accessed=6 * 1024 * 1024, transcendentals=640 * 1024
        ),
        name="direct",
    )(arrived)


def combine_kernel(in_ref, fix_ref, sums_ref, note_ref, *refs):
    share_refs = refs[:8]
    weight_hbm, x_ref, y_ref, share_ref, table_ref, sem = refs[8:]
    me = lax.axis_index("cent")
    gather_rows(in_ref, x_ref)
    note = note_ref[...].astype(jnp.float32)
    lane = iota((SLOTS, LANES), 1)
    x_ref[:, WIDTH:] = jnp.where(lane < 64, note, 0.0).astype(jnp.bfloat16)
    density = jnp.where((lane >= 64) & (lane < 67), note, 0.0)
    half_extra = EXTRA // 2
    for h in range(2):
        rows = slice(h * half_extra, (h + 1) * half_extra)
        for j in range(8):
            y_ref[rows, j * LANES : (j + 1) * LANES] = fix_ref[:, h * 8 + j, :, :].reshape(
                half_extra, LANES
            )
    fix_tags = jnp.concatenate(
        [fix_ref[:, 16 + h, :, :].reshape(half_extra, LANES) for h in range(2)], axis=0
    ).astype(jnp.float32)
    fix_lane = iota((EXTRA, LANES), 1)
    y_ref[:, WIDTH:] = jnp.where(fix_lane < 64, fix_tags * 4.0, 0.0).astype(jnp.bfloat16)

    sums = sums_ref[...] + dot_tn(y_ref[:, WIDTH:], y_ref[:, :WIDTH])[:64] * 0.25
    inverse = lax.rsqrt(jnp.sum(sums * sums, axis=1, keepdims=True) + EPSILON)
    centroid = sums * inverse
    coarse = jnp.concatenate([centroid, jnp.zeros_like(centroid)], axis=0).astype(jnp.bfloat16)

    def share(values, first):
        for j in range(8):
            piece = values[:, j * LANES : (j + 1) * LANES].reshape(8, 8, LANES)
            for c in range(8):
                share_ref[c ^ me, first + j, :, :] = piece[c].astype(jnp.bfloat16)

    share(centroid, 0)
    cross = jnp.exp(SHARPNESS * dot_nt(x_ref[...], y_ref[...]) - 17.0 * SHARPNESS)
    own = jnp.exp(SHARPNESS * dot_nt(y_ref[...], y_ref[...]) - 17.0 * SHARPNESS)
    eye = iota((LANES, LANES), 0) == iota((LANES, LANES), 1)
    line = jnp.sum(cross, axis=0, keepdims=True)

    def weigh(rows_ref, dense):
        rows = rows_ref[:, :WIDTH]
        member = rows_ref[:, WIDTH:].astype(jnp.float32) * 0.25
        near = jnp.sum(dot_nt(rows, coarse) * member, axis=1, keepdims=True)
        valid = jnp.sum(member, axis=1, keepdims=True) > 0.5
        density = jnp.sum(dense, axis=1, keepdims=True)
        weight = jnp.where(valid, jnp.exp(1.0 - near) / jnp.where(valid, density, 1.0), 0.0)
        rounded = weight.astype(jnp.bfloat16).astype(jnp.float32)
        return weight, valid, (member * rounded).astype(jnp.bfloat16)

    weight, _, scaled = weigh(x_ref, density + cross)
    fix_weight, present, fix_scaled = weigh(y_ref, own + jnp.where(eye, line, 0.0))

    wide = jnp.broadcast_to(weight, (SLOTS, LANES)).reshape(LANES, 8, LANES)
    place = iota((LANES, 8, LANES), 2) == iota((LANES, 8, LANES), 1)
    table = jnp.sum(jnp.where(place, wide, 0.0), axis=1)
    source = jnp.sum(jnp.where(fix_lane == 96, fix_tags, 0.0), axis=1, keepdims=True)
    origin = as_bf((fix_lane.astype(jnp.float32) == source) & present)
    values = jnp.where((fix_lane >= 72) & (fix_lane < 88), fix_tags * fix_weight, 0.0)
    for _ in range(3):
        part = values.astype(jnp.bfloat16)
        values = values - part.astype(jnp.float32)
        table = table + dot_tn(origin, part)
    flag = jnp.maximum(
        jnp.max(note, axis=0, keepdims=True),
        jnp.max(fix_tags, axis=0, keepdims=True),
    )
    table_ref[...] = jnp.where(iota((LANES, LANES), 1) == 127, flag, table)
    leave = pltpu.make_async_copy(table_ref, weight_hbm, sem)
    leave.start()

    weighted = dot_tn(scaled, x_ref[:, :WIDTH]) + dot_tn(fix_scaled, y_ref[:, :WIDTH])
    weighted = weighted[:64]
    rep = weighted * lax.rsqrt(jnp.sum(weighted * weighted, axis=1, keepdims=True) + EPSILON)
    share(rep, 8)
    for i in range(8):
        share_refs[i][...] = share_ref[i]
    leave.wait()


def combine(arrived, fixed, sums, note):
    vmem = pl.BlockSpec(memory_space=pltpu.VMEM)
    share = jax.ShapeDtypeStruct((16, 8, LANES), jnp.bfloat16)
    return pl.pallas_call(
        combine_kernel,
        out_shape=(share,) * 8 + (jax.ShapeDtypeStruct((LANES, LANES), jnp.float32),),
        in_specs=[vmem] * 4,
        out_specs=(vmem,) * 8 + (pl.BlockSpec(memory_space=pltpu.HBM),),
        scratch_shapes=[
            pltpu.VMEM((SLOTS, WIDTH + LANES), jnp.bfloat16),
            pltpu.VMEM((EXTRA, WIDTH + LANES), jnp.bfloat16),
            pltpu.VMEM((8, 16, 8, LANES), jnp.bfloat16),
            pltpu.VMEM((LANES, LANES), jnp.float32),
            pltpu.SemaphoreType.DMA,
        ],
        compiler_params=pltpu.CompilerParams(vmem_limit_bytes=GRANT),
        name="combine",
    )(arrived, fixed, sums, note)


def finish_kernel(*refs):
    share_refs = refs[:8]
    returned_ref, place_hbm, cent_ref, rep_ref, keep_hbm, flag_ref = refs[8:14]
    place_ref, keep_ref, mixed_ref, fetch_sem, keep_sem = refs[14:]
    fetch = pltpu.make_async_copy(place_hbm, place_ref, fetch_sem)
    fetch.start()
    me = lax.axis_index("cent")
    values = returned_ref[...]
    raised = jnp.max(jnp.where(iota((LANES, LANES), 1) == 127, values, 0.0))
    flag_ref[0, 0] = (raised > 0.5).astype(jnp.int32)
    fetch.wait()
    place = place_ref[...]
    rows = place.shape[1]
    row = iota((LANES, rows), 0)
    here = as_bf(row == (place >> 7))
    lines = jnp.zeros((LANES, rows), jnp.float32)
    for _ in range(3):
        part = values.astype(jnp.bfloat16)
        values = values - part.astype(jnp.float32)
        lines = lines + dot_tn(part, here)
    keep_ref[...] = jnp.sum(jnp.where(row == (place & 127), lines, 0.0), axis=0, keepdims=True)
    store = pltpu.make_async_copy(keep_ref, keep_hbm, keep_sem)
    store.start()
    for i in range(8):
        residue = ((me ^ i) - me) & 7
        for j in range(16):
            tile = share_refs[i][j, :, :].astype(jnp.float32)
            mixed_ref[pl.ds(j * 64 + residue, 8, stride=8), :] = tile
    for j in range(8):
        cols = slice(j * LANES, (j + 1) * LANES)
        cent_ref[:, cols] = mixed_ref[j * 64 : j * 64 + 64, :]
        rep_ref[:, cols] = mixed_ref[512 + j * 64 : 512 + j * 64 + 64, :]
    store.wait()


def finish(shared, returned, place):
    vmem = pl.BlockSpec(memory_space=pltpu.VMEM)
    return pl.pallas_call(
        finish_kernel,
        out_shape=(
            jax.ShapeDtypeStruct((64, 1024), jnp.float32),
            jax.ShapeDtypeStruct((64, 1024), jnp.float32),
            jax.ShapeDtypeStruct(place.shape, jnp.float32),
            jax.ShapeDtypeStruct((1, 1), jnp.int32),
        ),
        in_specs=[vmem] * 9 + [pl.BlockSpec(memory_space=pltpu.HBM)],
        out_specs=(
            vmem,
            vmem,
            pl.BlockSpec(memory_space=pltpu.HBM),
            pl.BlockSpec(memory_space=pltpu.SMEM),
        ),
        scratch_shapes=[
            pltpu.VMEM(place.shape, jnp.int32),
            pltpu.VMEM(place.shape, jnp.float32),
            pltpu.VMEM((1024, LANES), jnp.float32),
            pltpu.SemaphoreType.DMA,
            pltpu.SemaphoreType.DMA,
        ],
        compiler_params=pltpu.CompilerParams(vmem_limit_bytes=GRANT),
        name="finish",
    )(*shared, returned, place)


def exchange(x, axes):
    return lax.all_to_all(x, axes, split_axis=0, concat_axis=0, tiled=True)


def full_path(embeddings, a_row, owner):
    outgoing, slot = dispatch(embeddings, a_row, owner)
    centroid, representative, weight = process(exchange(outgoing, AXES))
    keep = collect(exchange(weight, AXES), slot)
    return (centroid, representative, keep.reshape(keep.shape[1]))


def on_device(embeddings, assignment, owner_map):
    rows = assignment.shape[0]
    a_row = assignment.reshape(1, rows)
    owner = owner_map.reshape(-1, LANES)
    outgoing, place = pooled_dispatch(embeddings, a_row, owner)
    arrived = exchange(outgoing, AXES)
    fixed = exchange(relay(arrived), "cent")
    *share, weight = combine(arrived, fixed, *direct(arrived))
    members = lax.axis_size("cent")
    shared = list(share)
    for i in (4, 5, 2, 3, 6, 7, 1):
        shared[i] = lax.ppermute(share[i], "cent", [(c, c ^ i) for c in range(members)])
    returned = exchange(weight, AXES)
    centroid, representative, keep, flag = finish(shared, returned, place)
    centroid, representative, keep = lax.switch(
        flag[0, 0],
        (
            lambda: (centroid, representative, keep.reshape(rows)),
            lambda: full_path(embeddings, a_row, owner),
        ),
    )
    return (centroid, representative, keep)


def solution(mesh):
    in_specs = (P(AXES, None), P(AXES), P())
    out_specs = (P(AXES, None), P(AXES, None), P(AXES))
    return jax.shard_map(
        on_device, mesh=mesh, in_specs=in_specs, out_specs=out_specs, check_vma=False
    )
```
